32 devices in a mesh: rows: 8 (over y, x, core), cols: 4 (over z).
Axes of the slice: x: 2, y: 2, z: 4, core: 2. Of those that a mesh axis runs over, the one named last changes fastest.
Arguments:
- unary: float32 [21, 128, 512], P(None, 'rows', 'cols'), may hold values from -8 to 300
- features: bfloat16 [64, 128, 512], P(None, 'rows', 'cols'), may hold values from -9 to 9
- compat: float32 [21, 21], replicated, may hold values from -6 to 6
- grad_output: float32 [21, 128, 512], P(None, 'rows', 'cols'), may hold values from -6 to 6
Outputs:
- unary_grad: float32 [21, 128, 512], P(None, 'rows', 'cols')
- feature_grad: float32 [64, 128, 512], P(None, 'rows', 'cols')
- compat_grad: float32 [21, 21], replicated
The draws below stay inside these ranges and needn't reach their ends.
All inputs are finite; a program needn't handle non-finite values.
Results may differ from the reference program's by a relative error of at most 0.0003.
Values may be sent and summed in bfloat16 or wider, within the bound.
No kernel may reach another device: no remote copies, remote signals or barrier semaphores. Data moves between devices by JAX's collectives and lax.ppermute only.
A program may use at most 128 MiB of HBM per device.

```python
import math
import jax
import jax.numpy as jnp
from jax import lax

CLASSES = 21
FEAT = 64
ITERS = 2
NH = 128
NW = 512


def draw_unary(key, part):
    base_key = jax.random.fold_in(key, 0)
    return jnp.clip(2.0 * jax.random.normal(base_key, (CLASSES, NH, NW), jnp.float32), -8.0, 8.0)


def block_levels(stream_key, shape, pieces, low, top_value):
    def one(axis_at, parts):
        heights = jax.random.uniform(jax.random.fold_in(jax.random.fold_in(stream_key, 6), axis_at), (parts,), jnp.float32, low / len(pieces), top_value / len(pieces))
        return jnp.repeat(jnp.exp(heights), shape[axis_at] // parts).reshape((-1,) + (1,) * (len(shape) - axis_at - 1))

    gain = one(*pieces[0])
    for cut in pieces[1:]:
        gain = gain * one(*cut)
    return gain


def gaussian(own_key, shape, deviation, most, pieces=(), held_as=jnp.bfloat16):
    array = deviation * jax.random.normal(own_key, shape, jnp.float32)
    if pieces:
        array = array * block_levels(own_key, shape, pieces, -0.22, 0.18)
    return jnp.clip(array, -most, most).astype(held_as)


def setup_inputs(seed: int = 0) -> dict:
    arg_keys = jax.random.split(jax.random.key(seed), 5)
    return {
        "unary": draw_unary(jax.random.fold_in(arg_keys[4], 71), 0),
        "features": gaussian(arg_keys[1], (FEAT, NH, NW), 1.5, 9.0, ((1, 8), (2, 4))),
        "compat": gaussian(arg_keys[2], (CLASSES, CLASSES), 1.0, 6.0, (), jnp.float32),
        "grad_output": gaussian(arg_keys[3], (CLASSES, NH, NW), 1.0, 6.0, ((1, 8), (2, 4)), jnp.float32),
    }


THETA_PIXELS = 3.0
WINDOW_OFFSETS = [(row_step, col_step) for row_step in range(-3, 4) for col_step in range(-3, 4) if row_step != 0 or col_step != 0]

def spatial_weight(row_step, col_step):
    return math.exp(-(row_step * row_step + col_step * col_step) / (2.0 * THETA_PIXELS * THETA_PIXELS))

def shifted_view(padded, row_step, col_step, height, width_cells):
    return padded[:, 3 + row_step:3 + row_step + height, 3 + col_step:3 + col_step + width_cells]

def affinity(padded_features):
    height = padded_features.shape[1] - 6
    width_cells = padded_features.shape[2] - 6
    center = shifted_view(padded_features, 0, 0, height, width_cells).astype(jnp.float32)
    factor = 1.0 / (2.0 * padded_features.shape[0])
    layers = []
    for row_step, col_step in WINDOW_OFFSETS:
        shifted = shifted_view(padded_features, row_step, col_step, height, width_cells).astype(jnp.float32)
        distance = lax.optimization_barrier(jnp.sum((shifted - center) * (shifted - center), axis=0))
        layers.append(spatial_weight(row_step, col_step) * jnp.exp(-distance * factor))
    return jnp.stack(layers)

def message(kernel, padded):
    height = kernel.shape[1]
    width_cells = kernel.shape[2]
    total = jnp.zeros((padded.shape[0], height, width_cells), jnp.float32)
    for number, (row_step, col_step) in enumerate(WINDOW_OFFSETS):
        total = total + kernel[number][None] * shifted_view(padded, row_step, col_step, height, width_cells)
    return total

def pair_terms(grad_padded, prob_padded):
    height = grad_padded.shape[1] - 6
    width_cells = grad_padded.shape[2] - 6
    grad_center = shifted_view(grad_padded, 0, 0, height, width_cells)
    prob_center = shifted_view(prob_padded, 0, 0, height, width_cells)
    layers = []
    for row_step, col_step in WINDOW_OFFSETS:
        prob_shift = shifted_view(prob_padded, row_step, col_step, height, width_cells)
        grad_shift = shifted_view(grad_padded, row_step, col_step, height, width_cells)
        layers.append(lax.optimization_barrier(jnp.sum(grad_center * prob_shift + grad_shift * prob_center, axis=0)))
    return jnp.stack(layers)

def feature_term(coefs, kernel, padded_features):
    height = kernel.shape[1]
    width_cells = kernel.shape[2]
    center = shifted_view(padded_features, 0, 0, height, width_cells).astype(jnp.float32)
    factor = 1.0 / padded_features.shape[0]
    total = jnp.zeros(center.shape, jnp.float32)
    for number, (row_step, col_step) in enumerate(WINDOW_OFFSETS):
        shifted = shifted_view(padded_features, row_step, col_step, height, width_cells).astype(jnp.float32)
        weight_map = coefs[number] * kernel[number] * factor
        total = total + weight_map[None] * (shifted - center)
    return total

def mix(compat, values):
    return jnp.einsum('cd,dhw->chw', compat, values, precision=lax.Precision.HIGHEST)

def mix_back(compat, values):
    return jnp.einsum('cd,chw->dhw', compat, values, precision=lax.Precision.HIGHEST)

def outer_sum(left, right):
    return jnp.einsum('chw,dhw->cd', left, right, precision=lax.Precision.HIGHEST)

def softmax_grad(prob, cotangent):
    return prob * (cotangent - lax.optimization_barrier(jnp.sum(cotangent * prob, axis=0, keepdims=True)))

def pad_three(values):
    return jnp.pad(values, ((0, 0), (3, 3), (3, 3)))

def reference(unary, features, compat, grad_output):
    feat_wide = pad_three(features)
    kernel = affinity(feat_wide)
    prob_list = [jax.nn.softmax(unary, axis=0)]
    message_list = []
    for step in range(ITERS):
        message_out = message(kernel, pad_three(prob_list[-1]))
        message_list.append(message_out)
        prob_list.append(jax.nn.softmax(unary - mix(compat, message_out), axis=0))
    cotangent = grad_output
    unary_sum = jnp.zeros(unary.shape, jnp.float32)
    compat_sum = jnp.zeros(compat.shape, jnp.float32)
    coefs = jnp.zeros((len(WINDOW_OFFSETS), unary.shape[1], unary.shape[2]), jnp.float32)
    for step in reversed(range(ITERS)):
        logit_grad = softmax_grad(prob_list[step + 1], cotangent)
        unary_sum = unary_sum + logit_grad
        compat_sum = compat_sum - outer_sum(logit_grad, message_list[step])
        msg_grad = -mix_back(compat, logit_grad)
        grad_wide = pad_three(msg_grad)
        cotangent = message(kernel, grad_wide)
        coefs = coefs + pair_terms(grad_wide, pad_three(prob_list[step]))
    unary_grad = unary_sum + softmax_grad(prob_list[0], cotangent)
    feature_grad = feature_term(coefs, kernel, feat_wide)
    compat_grad = compat_sum / math.sqrt(unary.shape[1] * unary.shape[2])
    return (unary_grad, feature_grad, compat_grad)
```

```python
import functools
import math

import jax
import jax.numpy as jnp
from jax import lax
from jax.experimental import pallas as pl
from jax.experimental.pallas import tpu as pltpu
from jax.sharding import PartitionSpec as P

ITERS = 2
REACH = 3
HALO = 2 * ITERS * REACH
STRIP = 16
PAD = 24
LOW = -1e30
VMEM = pl.BlockSpec(memory_space=pltpu.VMEM)
SMEM = pl.BlockSpec(memory_space=pltpu.SMEM)
HIGH = lax.Precision.HIGHEST


def params():
    return pltpu.CompilerParams(vmem_limit_bytes=56 * 1024 * 1024)


def sublane(width=128):
    return lax.broadcasted_iota(jnp.int32, (8, width), 0)


def lane(width=128):
    return lax.broadcasted_iota(jnp.int32, (1, width), 1)


def shifted(value, step):
    width = value.shape[-1]
    return pltpu.roll(value, (-step) % width, axis=value.ndim - 1)


def merge(parts):
    row = sublane(parts[0].shape[-1])
    bit = 1
    while len(parts) > 1:
        low = (row & bit) == 0
        parts = [
            jnp.where(low, first, second)
            + pltpu.roll(jnp.where(low, second, first), 8 - bit, axis=0)
            for first, second in zip(parts[::2], parts[1::2])
        ]
        bit *= 2
    return parts[0]


def fold(value):
    total = value[0:8]
    for start in range(8, value.shape[0], 8):
        total = total + value[start : start + 8]
    return total


def pack_kernel(feat, unary, grad, centre, left, right, wide):
    channels, height, _ = feat.shape
    classes = unary.shape[0] // height
    wide[...] = feat[...].astype(jnp.float32).reshape(channels * height, 128) * (
        1.0 / math.sqrt(channels)
    )
    empty = jnp.zeros((PAD - classes, 128), jnp.float32)
    side = lane()
    ends = [[], []]
    for y in range(height):
        rows = jnp.concatenate(
            [
                wide[pl.ds(y, channels, stride=height), :],
                unary[pl.ds(y, classes, stride=height), :],
                empty + LOW,
                grad[pl.ds(y, classes, stride=height), :],
                empty,
            ],
            axis=0,
        )
        centre[y] = rows
        at = (y % 8) * STRIP
        here = (side >= at) & (side < at + STRIP)
        for end, shift in ((0, at), (1, (at + STRIP) % 128)):
            moved = pltpu.roll(rows, shift, axis=1)
            if y % 8 == 0:
                ends[end].append(moved)
            else:
                ends[end][-1] = jnp.where(here, moved, ends[end][-1])
    for slot in range(height // 8):
        left[slot] = ends[0][slot]
        right[slot] = ends[1][slot]


def pack(feat, unary, grad):
    channels, height, _ = feat.shape
    depth = channels + 2 * PAD
    strips = jax.ShapeDtypeStruct((height // 8, depth, 128), jnp.float32)
    return pl.pallas_call(
        pack_kernel,
        out_shape=(jax.ShapeDtypeStruct((height, depth, 128), jnp.float32), strips, strips),
        in_specs=[VMEM] * 3,
        out_specs=(VMEM,) * 3,
        scratch_shapes=[pltpu.VMEM((channels * height, 128), jnp.float32)],
        compiler_params=params(),
        name="pack",
    )(feat, unary.reshape(-1, 128), grad.reshape(-1, 128))


def pass_row(y, kern, field, turned):
    def weight(row, at):
        return kern[row, pl.ds(at, 1), :]

    total = None

    def plus(total, term):
        return term if total is None else total + term

    for group in range(REACH):
        step = group + 1
        for a in range(-REACH, REACH + 1):
            total = plus(
                total, weight(y, 8 * group + a + REACH) * turned[group, y + a + REACH]
            )
        total = total + weight(y, 8 * group + 7) * field[y + step + REACH]
        total = total + weight(y - step, 8 * group + 7) * field[y - step + REACH]
    for group in range(REACH):
        back = None
        for a in range(-REACH, REACH + 1):
            back = plus(
                back, weight(y - a, 8 * group + a + REACH) * field[y - a + REACH]
            )
        total = total + shifted(back, -(group + 1))
    return total


def turn(field, turned, low, high):
    def body(row, carry):
        value = field[row]
        for group in range(REACH):
            turned[group, row] = shifted(value, group + 1)
        return carry

    lax.fori_loop(low, high, body, 0)


def softmax(value):
    top = jnp.max(value, axis=0, keepdims=True)
    power = jnp.exp(value - top)
    return power * (1.0 / jnp.sum(power, axis=0, keepdims=True))


def field_kernel(
    place, compat, compat_t, centre, first, second, from_left, from_right,
    feat_out, kern_out, prob0_out, prob1_out, grad1_out, grad0_out, unary_out, share,
    feat, feat_turned, norm, norm_turned, kern, unary, grad, prob0, prob1, grad1, grad0,
    turned, message0, message1, logit,
):
    height = centre.shape[0]
    rows = height + 2 * HALO
    channels = feat.shape[1]
    side = lane()

    feat[pl.ds(0, REACH)] = jnp.zeros((REACH,) + feat.shape[1:], jnp.float32)
    feat[pl.ds(rows + REACH, REACH)] = jnp.zeros((REACH,) + feat.shape[1:], jnp.float32)

    def put(row, main, left, right, slot):
        moved_right = pltpu.roll(right, (128 - slot * STRIP) % 128, axis=1)
        moved_left = pltpu.roll(left, (128 - STRIP - slot * STRIP) % 128, axis=1)
        edge = jnp.where(side < 64, moved_right, moved_left)
        feat[row + REACH, :, 0:128] = main[0:channels]
        feat[row + REACH, :, 128:256] = edge[0:channels]
        unary[row, :, 0:128] = main[channels : channels + PAD]
        unary[row, :, 128:256] = edge[channels : channels + PAD]
        grad[row, :, 0:128] = main[channels + PAD :]
        grad[row, :, 128:256] = edge[channels + PAD :]

    for y in range(height):
        put(HALO + y, centre[y], from_left[y // 8], from_right[y // 8], y % 8)
    strips = height // 8
    for source, above in ((first, place[0] == 0), (second, place[0] == 1)):
        base = jnp.where(above, 0, HALO + height)
        for y in range(HALO):
            gap = height - HALO

            @pl.when(above)
            def _(y=y, source=source):
                at = y + gap
                put(
                    y, source[y], source[HALO + at // 8], source[HALO + strips + at // 8], at % 8
                )

            @pl.when(jnp.logical_not(above))
            def _(y=y, source=source):
                put(
                    HALO + height + y, source[y], source[HALO + y // 8],
                    source[HALO + strips + y // 8], y % 8,
                )

    wide_lane = lane(256)
    inside_lane = (
        (wide_lane < 128)
        | ((wide_lane < 192) & (place[2] == 0))
        | ((wide_lane >= 192) & (place[1] == 0))
    )

    def inside(y):
        row = place[3] + y
        return inside_lane & (row >= 0) & (row < place[4])

    def turn_feat(row, carry):
        value = feat[row]
        size = fold(value * value) * 0.5
        norm[row] = size
        for group in range(REACH):
            feat_turned[group, row] = shifted(value, group + 1)
            norm_turned[group, row] = shifted(size, group + 1)
        return carry

    lax.fori_loop(0, rows + 2 * REACH, turn_feat, 0)

    sub = sublane()

    def affinity_row(y, carry):
        for tile in range(2):
            cols = pl.ds(128 * tile, 128)
            here = feat[y + REACH, :, cols]
            size = norm[y + REACH, :, cols]
            for group in range(REACH):
                parts = []
                for a in range(-REACH, REACH + 1):
                    there = feat_turned[group, y + a + REACH, :, cols]
                    parts.append(
                        fold(here * there) - (size + norm_turned[group, y + a + REACH, :, cols])
                    )
                below = y + group + 1 + REACH
                parts.append(fold(here * feat[below, :, cols]) - (size + norm[below, :, cols]))
                step_a = jnp.where(sub == 7, group + 1, sub - REACH)
                step_b = jnp.where(sub == 7, 0, group + 1)
                far = (step_a * step_a + step_b * step_b).astype(jnp.float32)
                kern[y, pl.ds(8 * group, 8), cols] = jnp.exp(
                    merge(parts) - far * (1.0 / (2.0 * REACH * REACH))
                )
        return carry

    lax.fori_loop(0, rows, affinity_row, 0)

    for ref in (prob0, prob1, grad1, grad0):
        ref[...] = jnp.zeros_like(ref)

    def start(y, carry):
        prob0[y + REACH] = jnp.where(inside(y), softmax(unary[y]), 0.0)
        return carry

    lax.fori_loop(0, rows, start, 0)

    def run_pass(field, out, low, high):
        turn(field, turned, low, high + 2 * REACH)

        def body(y, carry):
            out[y] = pass_row(y, kern, field, turned)
            return carry

        lax.fori_loop(low, high, body, 0)

    def dot(left, right):
        return jnp.dot(left, right, precision=HIGH, preferred_element_type=jnp.float32)

    def outer(left, right):
        return lax.dot_general(
            left, right, (((1,), (1,)), ((), ())), precision=HIGH,
            preferred_element_type=jnp.float32,
        )

    run_pass(prob0, message0, REACH, rows - REACH)

    def mix(y, carry):
        prob1[y + REACH] = jnp.where(
            inside(y), softmax(unary[y] - dot(compat[...], message0[y])), 0.0
        )
        return carry

    lax.fori_loop(REACH, rows - REACH, mix, 0)
    run_pass(prob1, message1, 2 * REACH, rows - 2 * REACH)

    def back1(y, carry):
        prob = softmax(unary[y] - dot(compat[...], message1[y]))
        cot = grad[y]
        change = prob * (cot - jnp.sum(cot * prob, axis=0, keepdims=True))
        logit[y] = change
        grad1[y + REACH] = jnp.where(inside(y), -dot(compat_t[...], change), 0.0)
        return carry

    lax.fori_loop(2 * REACH, rows - 2 * REACH, back1, 0)
    total = jnp.zeros((PAD, PAD), jnp.float32)

    def add_share(message):
        def body(y, carry):
            return carry - outer(logit[y, :, 0:128], message[y, :, 0:128])

        return body

    total = lax.fori_loop(HALO, HALO + height, add_share(message1), total)

    def keep(y, carry):
        unary_out[y - HALO] = logit[y, :, 0:128]
        return carry

    lax.fori_loop(HALO, HALO + height, keep, 0)
    run_pass(grad1, message1, 3 * REACH, rows - 3 * REACH)

    def back0(y, carry):
        prob = prob1[y + REACH]
        cot = message1[y]
        change = prob * (cot - jnp.sum(cot * prob, axis=0, keepdims=True))
        logit[y] = change
        grad0[y + REACH] = jnp.where(inside(y), -dot(compat_t[...], change), 0.0)
        return carry

    lax.fori_loop(3 * REACH, rows - 3 * REACH, back0, 0)
    total = lax.fori_loop(HALO, HALO + height, add_share(message0), total)

    def keep0(y, carry):
        unary_out[y - HALO] += logit[y, :, 0:128]
        return carry

    lax.fori_loop(HALO, HALO + height, keep0, 0)

    total = jnp.concatenate([total, jnp.zeros((PAD, 128 - PAD), jnp.float32)], axis=1)
    packed = (
        total[0:8]
        + pltpu.roll(total[8:16], 32, axis=1)
        + pltpu.roll(total[16:24], 64, axis=1)
    )
    for slot in range(share.shape[0]):
        share[slot] = packed

    near = height + 2 * REACH

    def copy(row, carry):
        at = row + HALO
        feat_out[row] = feat[at]
        prob0_out[row] = prob0[at]
        prob1_out[row] = prob1[at]
        grad1_out[row] = grad1[at]
        grad0_out[row] = grad0[at]
        kern_out[row] = kern[at - REACH]
        return carry

    lax.fori_loop(0, near, copy, 0)


def iterate(place, compat, centre, first, second, from_left, from_right, devices):
    height, depth, _ = centre.shape
    channels = depth - 2 * PAD
    rows = height + 2 * HALO
    tall = rows + 2 * REACH
    near = height + 2 * REACH

    def shape(*dims):
        return jax.ShapeDtypeStruct(dims, jnp.float32)

    def room(*dims):
        return pltpu.VMEM(dims, jnp.float32)

    return pl.pallas_call(
        field_kernel,
        out_shape=(
            shape(near, channels, 256),
            shape(near, PAD, 256),
            shape(near, PAD, 256),
            shape(near, PAD, 256),
            shape(near, PAD, 256),
            shape(near, PAD, 256),
            shape(height, PAD, 128),
            shape(devices, 8, 128),
        ),
        in_specs=[SMEM] + [VMEM] * 7,
        out_specs=(VMEM,) * 8,
        scratch_shapes=[
            room(tall, channels, 256),
            room(REACH, tall, channels, 256),
            room(tall, 8, 256),
            room(REACH, tall, 8, 256),
            room(rows, PAD, 256),
            room(rows, PAD, 256),
            room(rows, PAD, 256),
            room(tall, PAD, 256),
            room(tall, PAD, 256),
            room(tall, PAD, 256),
            room(tall, PAD, 256),
            room(REACH, tall, PAD, 256),
            room(rows, PAD, 256),
            room(rows, PAD, 256),
            room(rows, PAD, 256),
        ],
        compiler_params=params(),
        name="iterate",
    )(place, compat, compat.T, centre, first, second, from_left, from_right)


def finish_kernel(
    feat, kern, prob0, prob1, grad1, grad0, partial, unary_out, feat_out,
    feat_turned, all_turned, turned, kern_back, weights,
):
    height = partial.shape[0]
    near = height + 2 * REACH
    channels = feat.shape[1]
    classes = unary_out.shape[0] // height
    steps = range(-REACH, REACH + 1)

    def prepare(row, carry):
        value = feat[row]
        for b in steps:
            feat_turned[b + REACH, row] = shifted(value, b)[:, 0:128] if b else value[:, 0:128]
        for place, field in enumerate((prob0, prob1, grad1, grad0)):
            value = field[row]
            for b in steps:
                moved = shifted(value, b) if b else value
                all_turned[b + REACH, row, pl.ds(place * PAD, PAD), :] = moved[:, 0:128]
                if field is grad0 and b > 0:
                    turned[b - 1, row] = moved
        for group in range(REACH):
            value = kern[row, pl.ds(8 * group, 8), :]
            kern_back[row, pl.ds(8 * group, 8), :] = jnp.where(
                sublane() == 7, value[:, 0:128], shifted(value, -(group + 1))[:, 0:128]
            )
        return carry

    lax.fori_loop(0, near, prepare, 0)

    def unary_row(y, carry):
        cot = pass_row(y + REACH, kern, _Offset(grad0), _Offset(turned, 1))[:, 0:128]
        prob = prob0[y + REACH, :, 0:128]
        value = partial[y] + prob * (cot - jnp.sum(cot * prob, axis=0, keepdims=True))
        for start in range(0, classes, 8):
            size = min(8, classes - start)
            unary_out[pl.ds(start * height + y, size, stride=height), :] = value[
                start : start + size
            ]
        return carry

    lax.fori_loop(0, height, unary_row, 0)
    sub = sublane()

    def feature_row(y, carry):
        row = y + REACH
        own = all_turned[REACH, row]
        mate = jnp.concatenate(
            [own[3 * PAD :], own[2 * PAD : 3 * PAD], own[PAD : 2 * PAD], own[0:PAD]], axis=0
        )
        total = None
        whole = None
        for sign in (1, -1):
            for group in range(REACH):
                parts = []
                places = []
                for s in range(8):
                    a, b = (s - REACH, group + 1) if s < 7 else (group + 1, 0)
                    a, b = sign * a, sign * b
                    places.append((a, b))
                    parts.append(fold(mate * all_turned[b + REACH, row + a]))
                if sign > 0:
                    weight = kern[row, pl.ds(8 * group, 8), 0:128]
                else:
                    weight = kern_back[row - (group + 1), pl.ds(8 * group, 8), :]
                    for s in range(7):
                        weight = jnp.where(
                            sub == s, kern_back[row - (s - REACH), pl.ds(8 * group, 8), :], weight
                        )
                weight = weight * merge(parts)
                whole = weight if whole is None else whole + weight
                at = 8 * (group + (0 if sign > 0 else REACH))
                weights[y, pl.ds(at, 8), :] = weight
                for s, (a, b) in enumerate(places):
                    term = weights[y, pl.ds(at + s, 1), :] * feat_turned[b + REACH, row + a]
                    total = term if total is None else total + term
        whole = jnp.sum(whole, axis=0, keepdims=True)
        total = total - whole * feat_turned[REACH, row]
        feat_out[pl.ds(y, channels, stride=height), :] = total * (1.0 / math.sqrt(channels))
        return carry

    lax.fori_loop(0, height, feature_row, 0)


class _Offset:
    def __init__(self, ref, axis=0):
        self.ref, self.axis = ref, axis

    def __getitem__(self, index):
        if self.axis:
            return self.ref[index[0], index[1] - REACH]
        return self.ref[index - REACH]


def finish(feat, kern, prob0, prob1, grad1, grad0, partial, classes):
    near, channels, _ = feat.shape
    height = partial.shape[0]

    def room(*dims):
        return pltpu.VMEM(dims, jnp.float32)

    return pl.pallas_call(
        finish_kernel,
        out_shape=(
            jax.ShapeDtypeStruct((classes * height, 128), jnp.float32),
            jax.ShapeDtypeStruct((channels * height, 128), jnp.float32),
        ),
        in_specs=[VMEM] * 7,
        out_specs=(VMEM,) * 2,
        scratch_shapes=[
            room(2 * REACH + 1, near, channels, 128),
            room(2 * REACH + 1, near, 4 * PAD, 128),
            room(REACH, near, PAD, 256),
            room(near, PAD, 128),
            room(height, 6 * 8, 128),
        ],
        compiler_params=params(),
        cost_estimate=pl.CostEstimate(flops=200_000_000, bytes_accessed=8_000_000, transcendentals=0),
        name="finish",
    )(feat, kern, prob0, prob1, grad1, grad0, partial)


def on_device(unary, features, compat, grad_output):
    classes, height, width = unary.shape
    n_rows, n_cols = lax.axis_size("rows"), lax.axis_size("cols")
    row, col = lax.axis_index("rows"), lax.axis_index("cols")
    odd = row % 2

    centre, left, right = pack(features, unary, grad_output)
    forward = [(i, i + 1) for i in range(n_cols - 1)]
    backward = [(i + 1, i) for i in range(n_cols - 1)]
    from_left = lax.ppermute(right, "cols", forward)
    from_right = lax.ppermute(left, "cols", backward)
    strips = jnp.concatenate([from_left, from_right], axis=0)

    top = jnp.concatenate([centre[:HALO], strips], axis=0)
    bottom = jnp.concatenate([centre[height - HALO :], strips], axis=0)
    below = [pair for i in range(0, n_rows, 2) for pair in ((i, i + 1), (i + 1, i))]
    above = [
        pair
        for i in range(1, n_rows, 2)
        for pair in ((i, (i + 1) % n_rows), ((i + 1) % n_rows, i))
    ]
    first = lax.ppermute(jnp.where(odd == 0, bottom, top), "rows", below)
    second = lax.ppermute(jnp.where(odd == 0, top, bottom), "rows", above)

    place = jnp.stack(
        [1 - odd, col == 0, col == n_cols - 1, row * height - HALO, n_rows * height]
    ).astype(jnp.int32)
    square = jnp.pad(compat, ((0, PAD - classes), (0, PAD - classes)))
    devices = n_rows * n_cols
    *fields, partial, share = iterate(
        place, square, centre, first, second, from_left, from_right, devices
    )
    shares = lax.all_to_all(share, ("rows", "cols"), 0, 0)
    unary_grad, feature_grad = finish(*fields, partial, classes)
    summed = jnp.sum(shares, axis=0) / math.sqrt(n_rows * height * n_cols * width)
    compat_grad = jnp.concatenate(
        [summed[:, 0:PAD], summed[:, 32 : 32 + PAD], summed[:, 64 : 64 + PAD]], axis=0
    )[:classes, :classes]
    return (
        unary_grad.reshape(unary.shape),
        feature_grad.reshape(features.shape),
        compat_grad,
    )


def solution(mesh):
    placed = (P(None, "rows", "cols"), P(None, "rows", "cols"), P(), P(None, "rows", "cols"))
    return jax.shard_map(
        on_device,
        mesh=mesh,
        in_specs=placed,
        out_specs=(P(None, "rows", "cols"), P(None, "rows", "cols"), P()),
        check_vma=False,
    )
```

```python
import functools
import math

import jax
import jax.numpy as jnp
from jax import lax
from jax.experimental import pallas as pl
from jax.experimental.pallas import tpu as pltpu
from jax.sharding import PartitionSpec as P

ITERS = 2
REACH = 3
HALO = 2 * ITERS * REACH
STRIP = 16
PAD = 24
DEEP = 32
LOW = -1e30
VMEM = pl.BlockSpec(memory_space=pltpu.VMEM)
SMEM = pl.BlockSpec(memory_space=pltpu.SMEM)


def params():
    return pltpu.CompilerParams(vmem_limit_bytes=56 * 1024 * 1024)


def sublane(width=128):
    return lax.broadcasted_iota(jnp.int32, (8, width), 0)


def lane(width=128):
    return lax.broadcasted_iota(jnp.int32, (1, width), 1)


def shifted(value, step):
    low, high = value[:, 0:128], value[:, 128:256]
    column = lane() + step
    here = (column >= 0) & (column < 128)
    low = pltpu.roll(low, (-step) % 128, axis=1)
    high = pltpu.roll(high, (-step) % 128, axis=1)
    return jnp.concatenate([jnp.where(here, low, high), jnp.where(here, high, low)], axis=1)


def each_row(low, high, step, body):
    def some(turn, carry):
        for at in range(step):
            body(low + turn * step + at)
        return carry

    turns = (high - low) // step
    lax.fori_loop(0, turns, some, 0)
    for y in range(low + turns * step, high):
        body(y)


def split(value):
    parts = []
    for _ in range(2):
        part = value.astype(jnp.bfloat16)
        parts.append(part)
        value = value - part.astype(jnp.float32)
    return parts + [value.astype(jnp.bfloat16)]


def deep(value):
    return jnp.concatenate([value, jnp.zeros((DEEP - PAD, value.shape[1]), value.dtype)], axis=0)


def apply(square, value):
    high, middle, low = split(deep(value))
    stack = jnp.concatenate([high, middle, high, low, middle, high], axis=0)
    return jnp.dot(square, stack, preferred_element_type=jnp.float32)[0:PAD]


def spread(square):
    size = DEEP - square.shape[0]
    square = jnp.pad(square, ((0, size), (0, size)))
    high = lax.reduce_precision(square, 8, 7)
    middle = lax.reduce_precision(square - high, 8, 7)
    low = square - high - middle
    return jnp.concatenate([high, high, middle, high, middle, low], axis=1).astype(jnp.bfloat16)


def outer(left, right):
    left = jnp.concatenate(split(deep(left)), axis=0)
    right = jnp.concatenate(split(deep(right)), axis=0)
    full = lax.dot_general(
        left, right, (((1,), (1,)), ((), ())), preferred_element_type=jnp.float32
    )
    total = None
    for i in range(3):
        for j in range(3 - i):
            term = full[i * DEEP : i * DEEP + PAD, j * DEEP : j * DEEP + PAD]
            total = term if total is None else total + term
    return total


def merge(parts):
    row = sublane(parts[0].shape[-1])
    bit = 1
    while len(parts) > 1:
        low = (row & bit) == 0
        parts = [
            jnp.where(low, first, second)
            + pltpu.roll(jnp.where(low, second, first), 8 - bit, axis=0)
            for first, second in zip(parts[::2], parts[1::2])
        ]
        bit *= 2
    return parts[0]


def fold(value):
    total = value[0:8]
    for start in range(8, value.shape[0], 8):
        total = total + value[start : start + 8]
    return total


def pack_kernel(feat, unary, grad, centre, left, right, wide):
    channels, height, _ = feat.shape
    classes = unary.shape[0] // height
    wide[...] = feat[...].astype(jnp.float32).reshape(channels * height, 128) * (
        1.0 / math.sqrt(channels)
    )
    empty = jnp.zeros((PAD - classes, 128), jnp.float32)
    side = lane()
    ends = [[], []]
    for y in range(height):
        rows = jnp.concatenate(
            [
                wide[pl.ds(y, channels, stride=height), :],
                unary[pl.ds(y, classes, stride=height), :],
                empty + LOW,
                grad[pl.ds(y, classes, stride=height), :],
                empty,
            ],
            axis=0,
        )
        centre[y] = rows
        at = (y % 8) * STRIP
        here = (side >= at) & (side < at + STRIP)
        for end, shift in ((0, at), (1, (at + STRIP) % 128)):
            moved = pltpu.roll(rows, shift, axis=1)
            if y % 8 == 0:
                ends[end].append(moved)
            else:
                ends[end][-1] = jnp.where(here, moved, ends[end][-1])
    for slot in range(height // 8):
        left[slot] = ends[0][slot]
        right[slot] = ends[1][slot]


def pack(feat, unary, grad):
    channels, height, _ = feat.shape
    depth = channels + 2 * PAD
    strips = jax.ShapeDtypeStruct((height // 8, depth, 128), jnp.float32)
    return pl.pallas_call(
        pack_kernel,
        out_shape=(jax.ShapeDtypeStruct((height, depth, 128), jnp.float32), strips, strips),
        in_specs=[VMEM] * 3,
        out_specs=(VMEM,) * 3,
        scratch_shapes=[pltpu.VMEM((channels * height, 128), jnp.float32)],
        compiler_params=params(),
        name="pack",
    )(feat, unary.reshape(-1, 128), grad.reshape(-1, 128))


def pass_row(y, kern, field, turned):
    def weight(row, at):
        return kern[row, pl.ds(at, 1), :]

    total = None

    def plus(total, term):
        return term if total is None else total + term

    for group in range(REACH):
        step = group + 1
        back = None
        for a in range(-REACH, REACH + 1):
            at = 8 * group + a + REACH
            total = plus(total, weight(y, at) * turned[group, y + a])
            back = plus(back, weight(y - a, at) * field[y - a])
        total = total + weight(y, 8 * group + 7) * field[y + step]
        total = total + weight(y - step, 8 * group + 7) * field[y - step]
        total = total + shifted(back, -step)
    return total


def softmax(value):
    top = jnp.max(value, axis=0, keepdims=True)
    power = jnp.exp(value - top)
    return power * (1.0 / jnp.sum(power, axis=0, keepdims=True))


def field_kernel(
    place, compat, compat_t, centre, first, second, from_left, from_right,
    feat_out, kern_out, prob0_out, prob1_out, grad1_out, grad0_out, unary_out, share,
    feat, feat_turned, norm, norm_turned, kern, unary, grad, prob0, prob1, grad1, grad0,
    turned, message0, message1, logit1, logit0,
):
    height = centre.shape[0]
    rows = height + 2 * HALO
    channels = feat.shape[1]
    side = lane()

    feat[pl.ds(0, REACH)] = jnp.zeros((REACH,) + feat.shape[1:], jnp.float32)
    feat[pl.ds(rows + REACH, REACH)] = jnp.zeros((REACH,) + feat.shape[1:], jnp.float32)

    def put(row, main, left, right, slot):
        moved_right = pltpu.roll(right, (128 - slot * STRIP) % 128, axis=1)
        moved_left = pltpu.roll(left, (128 - STRIP - slot * STRIP) % 128, axis=1)
        edge = jnp.where(side < 64, moved_right, moved_left)
        feat[row + REACH, :, 0:128] = main[0:channels]
        feat[row + REACH, :, 128:256] = edge[0:channels]
        unary[row, :, 0:128] = main[channels : channels + PAD]
        unary[row, :, 128:256] = edge[channels : channels + PAD]
        grad[row, :, 0:128] = main[channels + PAD :]
        grad[row, :, 128:256] = edge[channels + PAD :]

    for y in range(height):
        put(HALO + y, centre[y], from_left[y // 8], from_right[y // 8], y % 8)
    strips = height // 8
    for source, above in ((first, place[0] == 0), (second, place[0] == 1)):
        base = jnp.where(above, 0, HALO + height)
        for y in range(HALO):
            gap = height - HALO

            @pl.when(above)
            def _(y=y, source=source):
                at = y + gap
                put(
                    y, source[y], source[HALO + at // 8], source[HALO + strips + at // 8], at % 8
                )

            @pl.when(jnp.logical_not(above))
            def _(y=y, source=source):
                put(
                    HALO + height + y, source[y], source[HALO + y // 8],
                    source[HALO + strips + y // 8], y % 8,
                )

    wide_lane = lane(256)
    inside_lane = (
        (wide_lane < 128)
        | ((wide_lane < 192) & (place[2] == 0))
        | ((wide_lane >= 192) & (place[1] == 0))
    )

    def inside(y):
        row = place[3] + y
        return inside_lane & (row >= 0) & (row < place[4])

    def turn_feat(row):
        value = feat[row]
        size = fold(value * value) * 0.5
        norm[row] = size
        for group in range(REACH):
            feat_turned[group, row] = shifted(value, group + 1)
            norm_turned[group, row] = shifted(size, group + 1)

    each_row(0, rows + 2 * REACH, 2, turn_feat)

    sub = sublane()

    def affinity_row(y):
        for tile in range(2):
            cols = pl.ds(128 * tile, 128)
            here = feat[y + REACH, :, cols]
            size = norm[y + REACH, :, cols]
            for group in range(REACH):
                parts = []
                for a in range(-REACH, REACH + 1):
                    there = feat_turned[group, y + a + REACH, :, cols]
                    parts.append(
                        fold(here * there) - (size + norm_turned[group, y + a + REACH, :, cols])
                    )
                below = y + group + 1 + REACH
                parts.append(fold(here * feat[below, :, cols]) - (size + norm[below, :, cols]))
                step_a = jnp.where(sub == 7, group + 1, sub - REACH)
                step_b = jnp.where(sub == 7, 0, group + 1)
                far = (step_a * step_a + step_b * step_b).astype(jnp.float32)
                kern[y, pl.ds(8 * group, 8), cols] = jnp.exp(
                    merge(parts) - far * (1.0 / (2.0 * REACH * REACH))
                )

    each_row(0, rows, 1, affinity_row)

    def put_field(field, y, value):
        field[y] = value
        for group in range(REACH):
            turned[group, y] = shifted(value, group + 1)

    def start(y):
        put_field(prob0, y, jnp.where(inside(y), softmax(unary[y]), 0.0))

    each_row(0, rows, 4, start)

    def run_pass(field, out, low, high):
        def body(y):
            out[y] = pass_row(y, kern, field, turned)

        each_row(low, high, 2, body)

    run_pass(prob0, message0, REACH, rows - REACH)

    def mix(y):
        value = softmax(unary[y] - apply(compat[...], message0[y]))
        put_field(prob1, y, jnp.where(inside(y), value, 0.0))

    each_row(REACH, rows - REACH, 4, mix)
    run_pass(prob1, message1, 2 * REACH, rows - 2 * REACH)

    def back1(y):
        prob = softmax(unary[y] - apply(compat[...], message1[y]))
        cot = grad[y]
        change = prob * (cot - jnp.sum(cot * prob, axis=0, keepdims=True))
        logit1[y] = change
        put_field(grad1, y, jnp.where(inside(y), -apply(compat_t[...], change), 0.0))

    each_row(2 * REACH, rows - 2 * REACH, 4, back1)
    total = jnp.zeros((PAD, PAD), jnp.float32)

    def add_share(change, message):
        def body(turn, carry):
            at = HALO + 4 * turn
            left = jnp.concatenate([change[at + i, :, 0:128] for i in range(4)], axis=1)
            right = jnp.concatenate([message[at + i, :, 0:128] for i in range(4)], axis=1)
            return carry - outer(left, right)

        return body

    total = lax.fori_loop(0, height // 4, add_share(logit1, message1), total)
    run_pass(grad1, message1, 3 * REACH, rows - 3 * REACH)

    def back0(y):
        prob = prob1[y]
        cot = message1[y]
        change = prob * (cot - jnp.sum(cot * prob, axis=0, keepdims=True))
        logit0[y] = change
        grad0[y] = jnp.where(inside(y), -apply(compat_t[...], change), 0.0)

    each_row(3 * REACH, rows - 3 * REACH, 4, back0)
    total = lax.fori_loop(0, height // 4, add_share(logit0, message0), total)

    total = jnp.concatenate([total, jnp.zeros((PAD, 128 - PAD), jnp.float32)], axis=1)
    packed = (
        total[0:8]
        + pltpu.roll(total[8:16], 32, axis=1)
        + pltpu.roll(total[16:24], 64, axis=1)
    )
    for slot in range(share.shape[0]):
        share[slot] = packed

    near = height + 2 * REACH

    def copy(row):
        at = row + HALO - REACH
        feat_out[row] = feat[at + REACH]
        prob0_out[row] = prob0[at]
        prob1_out[row] = prob1[at]
        grad1_out[row] = grad1[at]
        grad0_out[row] = grad0[at]
        kern_out[row] = kern[at]

    each_row(0, near, 2, copy)

    def add_logit(y):
        unary_out[y] = logit0[y + HALO, :, 0:128] + logit1[y + HALO, :, 0:128]

    each_row(0, height, 4, add_logit)


def iterate(place, compat, centre, first, second, from_left, from_right, devices):
    height, depth, _ = centre.shape
    channels = depth - 2 * PAD
    rows = height + 2 * HALO
    tall = rows + 2 * REACH
    near = height + 2 * REACH

    def shape(*dims):
        return jax.ShapeDtypeStruct(dims, jnp.float32)

    def room(*dims):
        return pltpu.VMEM(dims, jnp.float32)

    return pl.pallas_call(
        field_kernel,
        out_shape=(
            shape(near, channels, 256),
            shape(near, PAD, 256),
            shape(near, PAD, 256),
            shape(near, PAD, 256),
            shape(near, PAD, 256),
            shape(near, PAD, 256),
            shape(height, PAD, 128),
            shape(devices, 8, 128),
        ),
        in_specs=[SMEM] + [VMEM] * 7,
        out_specs=(VMEM,) * 8,
        scratch_shapes=[
            room(tall, channels, 256),
            room(REACH, tall, channels, 256),
            room(tall, 8, 256),
            room(REACH, tall, 8, 256),
            *[room(rows, PAD, 256)] * 7,
            room(REACH, rows, PAD, 256),
            *[room(rows, PAD, 256)] * 4,
        ],
        compiler_params=params(),
        name="iterate",
    )(place, spread(compat), spread(compat.T), centre, first, second, from_left, from_right)


def finish_kernel(
    feat, kern, prob0, prob1, grad1, grad0, partial, unary_out, feat_out,
    feat_turned, all_turned, turned, kern_back, weights,
):
    height = partial.shape[0]
    near = height + 2 * REACH
    channels = feat.shape[1]
    classes = unary_out.shape[0] // height
    steps = range(-REACH, REACH + 1)

    def prepare(row, carry):
        value = feat[row]
        for b in steps:
            feat_turned[b + REACH, row] = shifted(value, b)[:, 0:128] if b else value[:, 0:128]
        for place, field in enumerate((prob0, prob1, grad1, grad0)):
            value = field[row]
            for b in steps:
                moved = shifted(value, b) if b else value
                all_turned[b + REACH, row, pl.ds(place * PAD, PAD), :] = moved[:, 0:128]
                if field is grad0 and b > 0:
                    turned[b - 1, row] = moved
        for group in range(REACH):
            value = kern[row, pl.ds(8 * group, 8), :]
            kern_back[row, pl.ds(8 * group, 8), :] = jnp.where(
                sublane() == 7, value[:, 0:128], shifted(value, -(group + 1))[:, 0:128]
            )
        return carry

    lax.fori_loop(0, near, prepare, 0)

    def unary_row(y, carry):
        cot = pass_row(y + REACH, kern, grad0, turned)[:, 0:128]
        prob = prob0[y + REACH, :, 0:128]
        value = partial[y] + prob * (cot - jnp.sum(cot * prob, axis=0, keepdims=True))
        for start in range(0, classes, 8):
            size = min(8, classes - start)
            unary_out[pl.ds(start * height + y, size, stride=height), :] = value[
                start : start + size
            ]
        return carry

    lax.fori_loop(0, height, unary_row, 0)
    sub = sublane()

    def feature_row(y, carry):
        row = y + REACH
        own = all_turned[REACH, row]
        mate = jnp.concatenate(
            [own[3 * PAD :], own[2 * PAD : 3 * PAD], own[PAD : 2 * PAD], own[0:PAD]], axis=0
        )
        total = None
        whole = None
        for sign in (1, -1):
            for group in range(REACH):
                parts = []
                places = []
                for s in range(8):
                    a, b = (s - REACH, group + 1) if s < 7 else (group + 1, 0)
                    a, b = sign * a, sign * b
                    places.append((a, b))
                    parts.append(fold(mate * all_turned[b + REACH, row + a]))
                if sign > 0:
                    weight = kern[row, pl.ds(8 * group, 8), 0:128]
                else:
                    weight = kern_back[row - (group + 1), pl.ds(8 * group, 8), :]
                    for s in range(7):
                        weight = jnp.where(
                            sub == s, kern_back[row - (s - REACH), pl.ds(8 * group, 8), :], weight
                        )
                weight = weight * merge(parts)
                whole = weight if whole is None else whole + weight
                at = 8 * (group + (0 if sign > 0 else REACH))
                weights[y, pl.ds(at, 8), :] = weight
                for s, (a, b) in enumerate(places):
                    term = weights[y, pl.ds(at + s, 1), :] * feat_turned[b + REACH, row + a]
                    total = term if total is None else total + term
        whole = jnp.sum(whole, axis=0, keepdims=True)
        total = total - whole * feat_turned[REACH, row]
        feat_out[pl.ds(y, channels, stride=height), :] = total * (1.0 / math.sqrt(channels))
        return carry

    lax.fori_loop(0, height, feature_row, 0)


def finish(feat, kern, prob0, prob1, grad1, grad0, partial, classes):
    near, channels, _ = feat.shape
    height = partial.shape[0]

    def room(*dims):
        return pltpu.VMEM(dims, jnp.float32)

    return pl.pallas_call(
        finish_kernel,
        out_shape=(
            jax.ShapeDtypeStruct((classes * height, 128), jnp.float32),
            jax.ShapeDtypeStruct((channels * height, 128), jnp.float32),
        ),
        in_specs=[VMEM] * 7,
        out_specs=(VMEM,) * 2,
        scratch_shapes=[
            room(2 * REACH + 1, near, channels, 128),
            room(2 * REACH + 1, near, 4 * PAD, 128),
            room(REACH, near, PAD, 256),
            room(near, PAD, 128),
            room(height, 6 * 8, 128),
        ],
        compiler_params=params(),
        cost_estimate=pl.CostEstimate(flops=200_000_000, bytes_accessed=8_000_000, transcendentals=0),
        name="finish",
    )(feat, kern, prob0, prob1, grad1, grad0, partial)


def on_device(unary, features, compat, grad_output):
    classes, height, width = unary.shape
    n_rows, n_cols = lax.axis_size("rows"), lax.axis_size("cols")
    row, col = lax.axis_index("rows"), lax.axis_index("cols")
    odd = row % 2

    centre, left, right = pack(features, unary, grad_output)
    forward = [(i, i + 1) for i in range(n_cols - 1)]
    backward = [(i + 1, i) for i in range(n_cols - 1)]
    from_left = lax.ppermute(right, "cols", forward)
    from_right = lax.ppermute(left, "cols", backward)
    strips = jnp.concatenate([from_left, from_right], axis=0)

    top = jnp.concatenate([centre[:HALO], strips], axis=0)
    bottom = jnp.concatenate([centre[height - HALO :], strips], axis=0)
    below = [pair for i in range(0, n_rows, 2) for pair in ((i, i + 1), (i + 1, i))]
    above = [
        pair
        for i in range(1, n_rows, 2)
        for pair in ((i, (i + 1) % n_rows), ((i + 1) % n_rows, i))
    ]
    first = lax.ppermute(jnp.where(odd == 0, bottom, top), "rows", below)
    second = lax.ppermute(jnp.where(odd == 0, top, bottom), "rows", above)

    place = jnp.stack(
        [1 - odd, col == 0, col == n_cols - 1, row * height - HALO, n_rows * height]
    ).astype(jnp.int32)
    devices = n_rows * n_cols
    *fields, partial, share = iterate(
        place, compat, centre, first, second, from_left, from_right, devices
    )
    shares = lax.all_to_all(share, ("rows", "cols"), 0, 0)
    unary_grad, feature_grad = finish(*fields, partial, classes)
    summed = jnp.sum(shares, axis=0) / math.sqrt(n_rows * height * n_cols * width)
    compat_grad = jnp.concatenate(
        [summed[:, 0:PAD], summed[:, 32 : 32 + PAD], summed[:, 64 : 64 + PAD]], axis=0
    )[:classes, :classes]
    return (
        unary_grad.reshape(unary.shape),
        feature_grad.reshape(features.shape),
        compat_grad,
    )


def solution(mesh):
    placed = (P(None, "rows", "cols"), P(None, "rows", "cols"), P(), P(None, "rows", "cols"))
    return jax.shard_map(
        on_device,
        mesh=mesh,
        in_specs=placed,
        out_specs=(P(None, "rows", "cols"), P(None, "rows", "cols"), P()),
        check_vma=False,
    )
```

```python
import functools
import math

import jax
import jax.numpy as jnp
from jax import lax
from jax.experimental import pallas as pl
from jax.experimental.pallas import tpu as pltpu
from jax.sharding import PartitionSpec as P

ITERS = 2
REACH = 3
HALO = 2 * ITERS * REACH
STRIP = 16
PAD = 24
DEEP = 32
LOW = -1e30
VMEM = pl.BlockSpec(memory_space=pltpu.VMEM)
SMEM = pl.BlockSpec(memory_space=pltpu.SMEM)


def params():
    return pltpu.CompilerParams(vmem_limit_bytes=56 * 1024 * 1024)


def sublane(width=128):
    return lax.broadcasted_iota(jnp.int32, (8, width), 0)


def lane(width=128):
    return lax.broadcasted_iota(jnp.int32, (1, width), 1)


def shifted(value, step):
    low, high = value[:, 0:128], value[:, 128:256]
    column = lane() + step
    here = (column >= 0) & (column < 128)
    low = pltpu.roll(low, (-step) % 128, axis=1)
    high = pltpu.roll(high, (-step) % 128, axis=1)
    return jnp.concatenate([jnp.where(here, low, high), jnp.where(here, high, low)], axis=1)


def each_row(low, high, step, body):
    def some(turn, carry):
        for at in range(step):
            body(low + turn * step + at)
        return carry

    turns = (high - low) // step
    lax.fori_loop(0, turns, some, 0)
    for y in range(low + turns * step, high):
        body(y)


def split(value):
    parts = []
    for _ in range(2):
        part = value.astype(jnp.bfloat16)
        parts.append(part)
        value = value - part.astype(jnp.float32)
    return parts + [value.astype(jnp.bfloat16)]


def deep(value):
    return jnp.concatenate([value, jnp.zeros((DEEP - PAD, value.shape[1]), value.dtype)], axis=0)


def apply(square, value):
    high, middle, low = split(deep(value))
    stack = jnp.concatenate([high, middle, high, low, middle, high], axis=0)
    return jnp.dot(square, stack, preferred_element_type=jnp.float32)[0:PAD]


def spread(square):
    size = DEEP - square.shape[0]
    square = jnp.pad(square, ((0, size), (0, size)))
    high = lax.reduce_precision(square, 8, 7)
    middle = lax.reduce_precision(square - high, 8, 7)
    low = square - high - middle
    return jnp.concatenate([high, high, middle, high, middle, low], axis=1).astype(jnp.bfloat16)


def outer(left, right):
    left = jnp.concatenate(split(deep(left)), axis=0)
    right = jnp.concatenate(split(deep(right)), axis=0)
    full = lax.dot_general(
        left, right, (((1,), (1,)), ((), ())), preferred_element_type=jnp.float32
    )
    total = None
    for i in range(3):
        for j in range(3 - i):
            term = full[i * DEEP : i * DEEP + PAD, j * DEEP : j * DEEP + PAD]
            total = term if total is None else total + term
    return total


def merge(parts):
    row = sublane(parts[0].shape[-1])
    bit = 1
    while len(parts) > 1:
        low = (row & bit) == 0
        parts = [
            jnp.where(low, first, second)
            + pltpu.roll(jnp.where(low, second, first), 8 - bit, axis=0)
            for first, second in zip(parts[::2], parts[1::2])
        ]
        bit *= 2
    return parts[0]


def fold(value):
    total = value[0:8]
    for start in range(8, value.shape[0], 8):
        total = total + value[start : start + 8]
    return total


def pack_kernel(
    place, feat, unary, grad, centre, left, right, inner, outer_feat, outer_rest, wide
):
    channels, height, _ = feat.shape
    classes = unary.shape[0] // height
    wide[...] = feat[...].astype(jnp.float32).reshape(channels * height, 128) * (
        1.0 / math.sqrt(channels)
    )
    empty = jnp.zeros((PAD - classes, 128), jnp.float32)
    side = lane()
    ends = [[], []]
    for y in range(height):
        rows = jnp.concatenate(
            [
                wide[pl.ds(y, channels, stride=height), :],
                unary[pl.ds(y, classes, stride=height), :],
                empty + LOW,
                grad[pl.ds(y, classes, stride=height), :],
                empty,
            ],
            axis=0,
        )
        centre[y] = rows
        at = (y % 8) * STRIP
        here = (side >= at) & (side < at + STRIP)
        for end, shift in ((0, at), (1, (at + STRIP) % 128)):
            moved = pltpu.roll(rows, shift, axis=1)
            if y % 8 == 0:
                ends[end].append(moved)
            else:
                ends[end][-1] = jnp.where(here, moved, ends[end][-1])
    for slot in range(height // 8):
        left[slot] = ends[0][slot]
        right[slot] = ends[1][slot]
    even = place[0] == 1
    low = height - HALO
    inner_base = jnp.where(even, low, 0)
    outer_base = jnp.where(even, 0, low)
    grad_base = jnp.where(even, 0, height - HALO // 2)
    for i in range(HALO):
        inner[i] = centre[inner_base + i]
        outer_feat[i] = centre[outer_base + i, 0:channels].astype(jnp.bfloat16)
        outer_rest[i] = centre[outer_base + i, channels : channels + PAD]
    for i in range(HALO // 2):
        outer_rest[HALO + i] = centre[grad_base + i, channels + PAD :]


def pack(place, feat, unary, grad):
    channels, height, _ = feat.shape
    depth = channels + 2 * PAD

    def shape(*dims, dtype=jnp.float32):
        return jax.ShapeDtypeStruct(dims, dtype)

    return pl.pallas_call(
        pack_kernel,
        out_shape=(
            shape(height, depth, 128),
            shape(height // 8, depth, 128),
            shape(height // 8, depth, 128),
            shape(HALO, depth, 128),
            shape(HALO, channels, 128, dtype=jnp.bfloat16),
            shape(HALO + HALO // 2, PAD, 128),
        ),
        in_specs=[SMEM] + [VMEM] * 3,
        out_specs=(VMEM,) * 6,
        scratch_shapes=[pltpu.VMEM((channels * height, 128), jnp.float32)],
        compiler_params=params(),
        name="pack",
    )(place, feat, unary.reshape(-1, 128), grad.reshape(-1, 128))


def corner_kernel(place, left, right, inner, outer):
    depth = left.shape[1]
    short = depth - PAD
    even = place[0] == 1
    side = lane()
    for out, top in ((inner, jnp.logical_not(even)), (outer, even)):
        whole = jnp.where(top, 0, 1)
        out[pl.ds(0, depth)] = left[whole]
        out[pl.ds(depth, depth)] = right[whole]
        mine = (side < 64) == top
        out[pl.ds(2 * depth, short)] = jnp.where(
            mine,
            left[1 - whole, 0:short],
            pltpu.roll(right[1 - whole, 0:short], 64, axis=1),
        )


def corners(place, left, right):
    depth = left.shape[1]
    out = jax.ShapeDtypeStruct((3 * depth - PAD, 128), jnp.float32)
    return pl.pallas_call(
        corner_kernel,
        out_shape=(out, out),
        in_specs=[SMEM] + [VMEM] * 2,
        out_specs=(VMEM,) * 2,
        compiler_params=params(),
        name="corners",
    )(place, left, right)


def pass_row(y, kern, field, turned):
    def weight(row, at):
        return kern[row, pl.ds(at, 1), :]

    total = None

    def plus(total, term):
        return term if total is None else total + term

    for group in range(REACH):
        step = group + 1
        back = None
        for a in range(-REACH, REACH + 1):
            at = 8 * group + a + REACH
            total = plus(total, weight(y, at) * turned[group, y + a])
            back = plus(back, weight(y - a, at) * field[y - a])
        total = total + weight(y, 8 * group + 7) * field[y + step]
        total = total + weight(y - step, 8 * group + 7) * field[y - step]
        total = total + shifted(back, -step)
    return total


def softmax(value):
    top = jnp.max(value, axis=0, keepdims=True)
    power = jnp.exp(value - top)
    return power * (1.0 / jnp.sum(power, axis=0, keepdims=True))


def field_kernel(
    place, compat, compat_t, centre, inner, outer_feat, outer_rest, inner_corner, outer_corner,
    from_left, from_right, feat_out, kern_out, prob0_out, prob1_out, grad1_out, grad0_out, unary_out, share,
    feat, feat_turned, norm, norm_turned, kern, unary, grad, prob0, prob1, grad1, grad0,
    turned, message0, message1, logit1, logit0,
):
    height = centre.shape[0]
    rows = height + 2 * HALO
    channels = feat.shape[1]
    side = lane()

    feat[pl.ds(0, REACH)] = jnp.zeros((REACH,) + feat.shape[1:], jnp.float32)
    feat[pl.ds(rows + REACH, REACH)] = jnp.zeros((REACH,) + feat.shape[1:], jnp.float32)

    def put(row, main, left, left_at, right, right_at):
        moved_right = pltpu.roll(right, (128 - right_at) % 128, axis=1)
        moved_left = pltpu.roll(left, (128 - STRIP - left_at) % 128, axis=1)
        edge = jnp.where(side < 64, moved_right, moved_left)
        for value, cols in ((main, slice(0, 128)), (edge, slice(128, 256))):
            feat[row + REACH, :, cols] = value[0:channels]
            unary[row, :, cols] = value[channels : channels + PAD]
            if value.shape[0] > channels + PAD:
                grad[row, :, cols] = value[channels + PAD :]

    for y in range(height):
        at = (y % 8) * STRIP
        put(HALO + y, centre[y], from_left[y // 8], at, from_right[y // 8], at)

    depth = channels + 2 * PAD
    short = channels + PAD
    near = HALO // 2

    def put_inner(i, top):
        return inner[i]

    def put_outer(i, top):
        parts = [outer_feat[i].astype(jnp.float32), outer_rest[i]]
        row = i if top else i - near
        if 0 <= row < near:
            parts.append(outer_rest[HALO + row])
        return jnp.concatenate(parts, axis=0)

    def put_rows(main, corner, top):
        base = HALO + height if top else 0
        half = HALO - 8
        for i in range(HALO):
            at = (i if top else i - half) * STRIP
            if 0 <= at < 128:
                left, right = corner[pl.ds(0, depth)], corner[pl.ds(depth, depth)]
                left_at = right_at = at
            else:
                left = right = corner[pl.ds(2 * depth, short)]
                left_at = (i - 8) * STRIP if top else 64 + i * STRIP
                right_at = (left_at + 64) % 128
            rows_main = main(i, top)
            size = min(rows_main.shape[0], left.shape[0])
            put(base + i, rows_main[0:size], left[0:size], left_at, right[0:size], right_at)

    even = place[0] == 1
    for main, corner, below in (
        (put_inner, inner_corner, even),
        (put_outer, outer_corner, jnp.logical_not(even)),
    ):
        pl.when(below)(functools.partial(put_rows, main, corner, True))
        pl.when(jnp.logical_not(below))(functools.partial(put_rows, main, corner, False))

    wide_lane = lane(256)
    inside_lane = (
        (wide_lane < 128)
        | ((wide_lane < 192) & (place[2] == 0))
        | ((wide_lane >= 192) & (place[1] == 0))
    )

    def inside(y):
        row = place[3] + y
        return inside_lane & (row >= 0) & (row < place[4])

    def turn_feat(row):
        value = feat[row]
        size = fold(value * value) * 0.5
        norm[row] = size
        for group in range(REACH):
            feat_turned[group, row] = shifted(value, group + 1)
            norm_turned[group, row] = shifted(size, group + 1)

    each_row(0, rows + 2 * REACH, 2, turn_feat)

    sub = sublane()

    def affinity_row(y):
        for tile in range(2):
            cols = pl.ds(128 * tile, 128)
            here = feat[y + REACH, :, cols]
            size = norm[y + REACH, :, cols]
            for group in range(REACH):
                parts = []
                for a in range(-REACH, REACH + 1):
                    there = feat_turned[group, y + a + REACH, :, cols]
                    parts.append(
                        fold(here * there) - (size + norm_turned[group, y + a + REACH, :, cols])
                    )
                below = y + group + 1 + REACH
                parts.append(fold(here * feat[below, :, cols]) - (size + norm[below, :, cols]))
                step_a = jnp.where(sub == 7, group + 1, sub - REACH)
                step_b = jnp.where(sub == 7, 0, group + 1)
                far = (step_a * step_a + step_b * step_b).astype(jnp.float32)
                kern[y, pl.ds(8 * group, 8), cols] = jnp.exp(
                    merge(parts) - far * (1.0 / (2.0 * REACH * REACH))
                )

    each_row(0, rows, 1, affinity_row)

    def put_field(field, y, value):
        field[y] = value
        for group in range(REACH):
            turned[group, y] = shifted(value, group + 1)

    def start(y):
        put_field(prob0, y, jnp.where(inside(y), softmax(unary[y]), 0.0))

    each_row(0, rows, 4, start)

    def run_pass(field, out, low, high):
        def body(y):
            out[y] = pass_row(y, kern, field, turned)

        each_row(low, high, 2, body)

    run_pass(prob0, message0, REACH, rows - REACH)

    def mix(y):
        value = softmax(unary[y] - apply(compat[...], message0[y]))
        put_field(prob1, y, jnp.where(inside(y), value, 0.0))

    each_row(REACH, rows - REACH, 4, mix)
    run_pass(prob1, message1, 2 * REACH, rows - 2 * REACH)

    def back1(y):
        prob = softmax(unary[y] - apply(compat[...], message1[y]))
        cot = grad[y]
        change = prob * (cot - jnp.sum(cot * prob, axis=0, keepdims=True))
        logit1[y] = change
        put_field(grad1, y, jnp.where(inside(y), -apply(compat_t[...], change), 0.0))

    each_row(2 * REACH, rows - 2 * REACH, 4, back1)
    total = jnp.zeros((PAD, PAD), jnp.float32)

    def add_share(change, message):
        def body(turn, carry):
            at = HALO + 4 * turn
            left = jnp.concatenate([change[at + i, :, 0:128] for i in range(4)], axis=1)
            right = jnp.concatenate([message[at + i, :, 0:128] for i in range(4)], axis=1)
            return carry - outer(left, right)

        return body

    total = lax.fori_loop(0, height // 4, add_share(logit1, message1), total)
    run_pass(grad1, message1, 3 * REACH, rows - 3 * REACH)

    def back0(y):
        prob = prob1[y]
        cot = message1[y]
        change = prob * (cot - jnp.sum(cot * prob, axis=0, keepdims=True))
        logit0[y] = change
        grad0[y] = jnp.where(inside(y), -apply(compat_t[...], change), 0.0)

    each_row(3 * REACH, rows - 3 * REACH, 4, back0)
    total = lax.fori_loop(0, height // 4, add_share(logit0, message0), total)

    total = jnp.concatenate([total, jnp.zeros((PAD, 128 - PAD), jnp.float32)], axis=1)
    packed = (
        total[0:8]
        + pltpu.roll(total[8:16], 32, axis=1)
        + pltpu.roll(total[16:24], 64, axis=1)
    )
    for slot in range(share.shape[0]):
        share[slot] = packed

    def copy(row):
        at = row + HALO - REACH
        feat_out[row] = feat[at + REACH]
        prob0_out[row] = prob0[at]
        prob1_out[row] = prob1[at]
        grad1_out[row] = grad1[at]
        grad0_out[row] = grad0[at]
        kern_out[row] = kern[at]

    each_row(0, height + 2 * REACH, 2, copy)

    def add_logit(y):
        unary_out[y] = logit0[y + HALO, :, 0:128] + logit1[y + HALO, :, 0:128]

    each_row(0, height, 4, add_logit)


def iterate(place, compat, centre, received, devices):
    height, depth, _ = centre.shape
    channels = depth - 2 * PAD
    rows = height + 2 * HALO
    tall = rows + 2 * REACH
    near = height + 2 * REACH

    def shape(*dims):
        return jax.ShapeDtypeStruct(dims, jnp.float32)

    def room(*dims):
        return pltpu.VMEM(dims, jnp.float32)

    return pl.pallas_call(
        field_kernel,
        out_shape=(
            shape(near, channels, 256),
            shape(near, PAD, 256),
            shape(near, PAD, 256),
            shape(near, PAD, 256),
            shape(near, PAD, 256),
            shape(near, PAD, 256),
            shape(height, PAD, 128),
            shape(devices, 8, 128),
        ),
        in_specs=[SMEM] + [VMEM] * 10,
        out_specs=(VMEM,) * 8,
        scratch_shapes=[
            room(tall, channels, 256),
            room(REACH, tall, channels, 256),
            room(tall, 8, 256),
            room(REACH, tall, 8, 256),
            *[room(rows, PAD, 256)] * 7,
            room(REACH, rows, PAD, 256),
            *[room(rows, PAD, 256)] * 4,
        ],
        compiler_params=params(),
        name="iterate",
    )(place, spread(compat), spread(compat.T), centre, *received)


def finish_kernel(
    feat, kern, prob0, prob1, grad1, grad0, partial, unary_out, feat_out,
    feat_turned, all_turned, turned, kern_back, weights,
):
    height = partial.shape[0]
    near = height + 2 * REACH
    channels = feat.shape[1]
    classes = unary_out.shape[0] // height
    steps = range(-REACH, REACH + 1)

    def prepare(row, carry):
        value = feat[row]
        for b in steps:
            feat_turned[b + REACH, row] = shifted(value, b)[:, 0:128] if b else value[:, 0:128]
        for place, field in enumerate((prob0, prob1, grad1, grad0)):
            value = field[row]
            for b in steps:
                moved = shifted(value, b) if b else value
                all_turned[b + REACH, row, pl.ds(place * PAD, PAD), :] = moved[:, 0:128]
                if field is grad0 and b > 0:
                    turned[b - 1, row] = moved
        for group in range(REACH):
            value = kern[row, pl.ds(8 * group, 8), :]
            kern_back[row, pl.ds(8 * group, 8), :] = jnp.where(
                sublane() == 7, value[:, 0:128], shifted(value, -(group + 1))[:, 0:128]
            )
        return carry

    lax.fori_loop(0, near, prepare, 0)

    def unary_row(y, carry):
        cot = pass_row(y + REACH, kern, grad0, turned)[:, 0:128]
        prob = prob0[y + REACH, :, 0:128]
        value = partial[y] + prob * (cot - jnp.sum(cot * prob, axis=0, keepdims=True))
        for start in range(0, classes, 8):
            size = min(8, classes - start)
            unary_out[pl.ds(start * height + y, size, stride=height), :] = value[
                start : start + size
            ]
        return carry

    lax.fori_loop(0, height, unary_row, 0)
    sub = sublane()

    def feature_row(y, carry):
        row = y + REACH
        own = all_turned[REACH, row]
        mate = jnp.concatenate(
            [own[3 * PAD :], own[2 * PAD : 3 * PAD], own[PAD : 2 * PAD], own[0:PAD]], axis=0
        )
        total = None
        whole = None
        for sign in (1, -1):
            for group in range(REACH):
                parts = []
                places = []
                for s in range(8):
                    a, b = (s - REACH, group + 1) if s < 7 else (group + 1, 0)
                    a, b = sign * a, sign * b
                    places.append((a, b))
                    parts.append(fold(mate * all_turned[b + REACH, row + a]))
                if sign > 0:
                    weight = kern[row, pl.ds(8 * group, 8), 0:128]
                else:
                    weight = kern_back[row - (group + 1), pl.ds(8 * group, 8), :]
                    for s in range(7):
                        weight = jnp.where(
                            sub == s, kern_back[row - (s - REACH), pl.ds(8 * group, 8), :], weight
                        )
                weight = weight * merge(parts)
                whole = weight if whole is None else whole + weight
                at = 8 * (group + (0 if sign > 0 else REACH))
                weights[y, pl.ds(at, 8), :] = weight
                for s, (a, b) in enumerate(places):
                    term = weights[y, pl.ds(at + s, 1), :] * feat_turned[b + REACH, row + a]
                    total = term if total is None else total + term
        whole = jnp.sum(whole, axis=0, keepdims=True)
        total = total - whole * feat_turned[REACH, row]
        feat_out[pl.ds(y, channels, stride=height), :] = total * (1.0 / math.sqrt(channels))
        return carry

    lax.fori_loop(0, height, feature_row, 0)


def finish(feat, kern, prob0, prob1, grad1, grad0, partial, classes):
    near, channels, _ = feat.shape
    height = partial.shape[0]

    def room(*dims):
        return pltpu.VMEM(dims, jnp.float32)

    return pl.pallas_call(
        finish_kernel,
        out_shape=(
            jax.ShapeDtypeStruct((classes * height, 128), jnp.float32),
            jax.ShapeDtypeStruct((channels * height, 128), jnp.float32),
        ),
        in_specs=[VMEM] * 7,
        out_specs=(VMEM,) * 2,
        scratch_shapes=[
            room(2 * REACH + 1, near, channels, 128),
            room(2 * REACH + 1, near, 4 * PAD, 128),
            room(REACH, near, PAD, 256),
            room(near, PAD, 128),
            room(height, 6 * 8, 128),
        ],
        compiler_params=params(),
        cost_estimate=pl.CostEstimate(flops=200_000_000, bytes_accessed=8_000_000, transcendentals=0),
        name="finish",
    )(feat, kern, prob0, prob1, grad1, grad0, partial)


def on_device(unary, features, compat, grad_output):
    classes, height, width = unary.shape
    n_rows, n_cols = lax.axis_size("rows"), lax.axis_size("cols")
    row, col = lax.axis_index("rows"), lax.axis_index("cols")
    odd = row % 2

    place = jnp.stack(
        [1 - odd, col == 0, col == n_cols - 1, row * height - HALO, n_rows * height]
    ).astype(jnp.int32)

    below = [pair for i in range(0, n_rows, 2) for pair in ((i, i + 1), (i + 1, i))]
    above = [
        pair
        for i in range(1, n_rows, 2)
        for pair in ((i, (i + 1) % n_rows), ((i + 1) % n_rows, i))
    ]
    forward = [(i, i + 1) for i in range(n_cols - 1)]
    backward = [(i + 1, i) for i in range(n_cols - 1)]
    centre, left, right, inner, outer_feat, outer_rest = pack(
        place, features, unary, grad_output
    )
    from_left = lax.ppermute(right, "cols", forward)
    from_right = lax.ppermute(left, "cols", backward)
    outer_feat = lax.ppermute(outer_feat, "rows", above)
    outer_rest = lax.ppermute(outer_rest, "rows", above)
    inner = lax.ppermute(inner, "rows", below)
    inner_corner, outer_corner = corners(place, from_left, from_right)
    outer_corner = lax.ppermute(outer_corner, "rows", above)
    inner_corner = lax.ppermute(inner_corner, "rows", below)
    received = (
        inner, outer_feat, outer_rest, inner_corner, outer_corner, from_left, from_right
    )

    devices = n_rows * n_cols
    *fields, partial, share = iterate(
        place, compat, centre, received, devices
    )
    shares = lax.all_to_all(share, ("rows", "cols"), 0, 0)
    unary_grad, feature_grad = finish(*fields, partial, classes)
    summed = jnp.sum(shares, axis=0) / math.sqrt(n_rows * height * n_cols * width)
    compat_grad = jnp.concatenate(
        [summed[:, 0:PAD], summed[:, 32 : 32 + PAD], summed[:, 64 : 64 + PAD]], axis=0
    )[:classes, :classes]
    return (
        unary_grad.reshape(unary.shape),
        feature_grad.reshape(features.shape),
        compat_grad,
    )


def solution(mesh):
    placed = (P(None, "rows", "cols"), P(None, "rows", "cols"), P(), P(None, "rows", "cols"))
    return jax.shard_map(
        on_device,
        mesh=mesh,
        in_specs=placed,
        out_specs=(P(None, "rows", "cols"), P(None, "rows", "cols"), P()),
        check_vma=False,
    )
```

```python
import functools
import math

import jax
import jax.numpy as jnp
from jax import lax
from jax.experimental import pallas as pl
from jax.experimental.pallas import tpu as pltpu
from jax.sharding import PartitionSpec as P

ITERS = 2
REACH = 3
HALO = 2 * ITERS * REACH
STRIP = 16
PAD = 24
DEEP = 32
LOW = -1e30
VMEM = pl.BlockSpec(memory_space=pltpu.VMEM)


def params():
    return pltpu.CompilerParams(vmem_limit_bytes=56 * 1024 * 1024)


def position(height):
    row, col = lax.axis_index("rows"), lax.axis_index("cols")
    return (
        row % 2 == 0,
        col > 0,
        col < lax.axis_size("cols") - 1,
        row * height - HALO,
        lax.axis_size("rows") * height,
    )


def sublane(width=128):
    return lax.broadcasted_iota(jnp.int32, (8, width), 0)


def lane(width=128):
    return lax.broadcasted_iota(jnp.int32, (1, width), 1)


def shifted(value, step):
    low, high = value[:, 0:128], value[:, 128:256]
    column = lane() + step
    here = (column >= 0) & (column < 128)
    low = pltpu.roll(low, (-step) % 128, axis=1)
    high = pltpu.roll(high, (-step) % 128, axis=1)
    return jnp.concatenate([jnp.where(here, low, high), jnp.where(here, high, low)], axis=1)


def turns(steps, width):
    source = lax.broadcasted_iota(jnp.int32, (256, width), 0)
    target = lax.broadcasted_iota(jnp.int32, (256, width), 1)
    return jnp.concatenate(
        [(source == (target + step) % 256).astype(jnp.bfloat16) for step in steps], axis=1
    )


def each_row(low, high, step, body):
    def some(turn, carry):
        for at in range(step):
            body(low + turn * step + at)
        return carry

    turns = (high - low) // step
    lax.fori_loop(0, turns, some, 0)
    for y in range(low + turns * step, high):
        body(y)


def split(value):
    parts = []
    for _ in range(2):
        part = value.astype(jnp.bfloat16)
        parts.append(part)
        value = value - part.astype(jnp.float32)
    return parts + [value.astype(jnp.bfloat16)]


def deep(value):
    return jnp.concatenate([value, jnp.zeros((DEEP - PAD, value.shape[1]), value.dtype)], axis=0)


def apply(square, value):
    high, middle, low = split(deep(value))
    stack = jnp.concatenate([high, middle, high, low, middle, high], axis=0)
    return jnp.dot(square, stack, preferred_element_type=jnp.float32)[0:PAD]


def spread(square):
    size = DEEP - square.shape[0]
    square = jnp.pad(square, ((0, size), (0, size)))
    high = lax.reduce_precision(square, 8, 7)
    middle = lax.reduce_precision(square - high, 8, 7)
    low = square - high - middle
    return jnp.concatenate([high, high, middle, high, middle, low], axis=1).astype(jnp.bfloat16)


def outer(left, right):
    left = jnp.concatenate(split(deep(left)), axis=0)
    right = jnp.concatenate(split(deep(right)), axis=0)
    full = lax.dot_general(
        left, right, (((1,), (1,)), ((), ())), preferred_element_type=jnp.float32
    )
    total = None
    for i in range(3):
        for j in range(3 - i):
            term = full[i * DEEP : i * DEEP + PAD, j * DEEP : j * DEEP + PAD]
            total = term if total is None else total + term
    return total


def merge(parts):
    row = sublane(parts[0].shape[-1])
    bit = 1
    while len(parts) > 1:
        low = (row & bit) == 0
        parts = [
            jnp.where(low, first, second)
            + pltpu.roll(jnp.where(low, second, first), 8 - bit, axis=0)
            for first, second in zip(parts[::2], parts[1::2])
        ]
        bit *= 2
    return parts[0]


def fold(value):
    total = value[0:8]
    for start in range(8, value.shape[0], 8):
        total = total + value[start : start + 8]
    return total


def pack_kernel(
    feat, unary, grad, centre, left, right, inner, outer_feat, outer_rest, wide
):
    channels, height, _ = feat.shape
    classes = unary.shape[0] // height
    wide[...] = feat[...].astype(jnp.float32).reshape(channels * height, 128) * (
        1.0 / math.sqrt(channels)
    )
    empty = jnp.zeros((PAD - classes, 128), jnp.float32)
    side = lane()
    for slot in range(height // 8):
        ends = [None, None]
        for i in range(8):
            y = 8 * slot + i
            rows = jnp.concatenate(
                [
                    wide[pl.ds(y, channels, stride=height), :],
                    unary[pl.ds(y, classes, stride=height), :],
                    empty + LOW,
                    grad[pl.ds(y, classes, stride=height), :],
                    empty,
                ],
                axis=0,
            )
            centre[y] = rows
            at = i * STRIP
            here = (side >= at) & (side < at + STRIP)
            for end, shift in ((0, at), (1, (at + STRIP) % 128)):
                moved = pltpu.roll(rows, shift, axis=1)
                ends[end] = moved if i == 0 else jnp.where(here, moved, ends[end])
        left[slot], right[slot] = ends
    even = position(height)[0]
    low = height - HALO
    inner_base = jnp.where(even, low, 0)
    outer_base = jnp.where(even, 0, low)
    grad_base = jnp.where(even, 0, height - HALO // 2)
    for i in range(HALO):
        inner[i] = centre[inner_base + i]
        outer_feat[i] = centre[outer_base + i, 0:channels].astype(jnp.bfloat16)
        outer_rest[i] = centre[outer_base + i, channels : channels + PAD]
    for i in range(HALO // 2):
        outer_rest[HALO + i] = centre[grad_base + i, channels + PAD :]


def pack(feat, unary, grad):
    channels, height, _ = feat.shape
    depth = channels + 2 * PAD

    def shape(*dims, dtype=jnp.float32):
        return jax.ShapeDtypeStruct(dims, dtype)

    return pl.pallas_call(
        pack_kernel,
        out_shape=(
            shape(height, depth, 128),
            shape(height // 8, depth, 128),
            shape(height // 8, depth, 128),
            shape(HALO, depth, 128),
            shape(HALO, channels, 128, dtype=jnp.bfloat16),
            shape(HALO + HALO // 2, PAD, 128),
        ),
        in_specs=[VMEM] * 3,
        out_specs=(VMEM,) * 6,
        scratch_shapes=[pltpu.VMEM((channels * height, 128), jnp.float32)],
        compiler_params=params(),
        name="pack",
    )(feat, unary.reshape(-1, 128), grad.reshape(-1, 128))


def corner_kernel(left, right, _, inner, outer):
    depth = left.shape[1]
    short = depth - PAD
    even = position(8 * left.shape[0])[0]
    side = lane()
    for out, top in ((inner, jnp.logical_not(even)), (outer, even)):
        whole = jnp.where(top, 0, 1)
        out[pl.ds(0, depth)] = left[whole]
        out[pl.ds(depth, depth)] = right[whole]
        mine = (side < 64) == top
        out[pl.ds(2 * depth, short)] = jnp.where(
            mine,
            left[1 - whole, 0:short],
            pltpu.roll(right[1 - whole, 0:short], 64, axis=1),
        )


def corners(left, right, earlier):
    depth = left.shape[1]
    out = jax.ShapeDtypeStruct((3 * depth - PAD, 128), jnp.float32)
    return pl.pallas_call(
        corner_kernel,
        out_shape=(out, out),
        in_specs=[VMEM, VMEM, pl.BlockSpec(memory_space=pl.ANY)],
        out_specs=(VMEM,) * 2,
        compiler_params=params(),
        name="corners",
    )(left, right, earlier)


def pass_row(y, kern, field, turned):
    def weight(row, at):
        return kern[row, pl.ds(at, 1), :]

    total = None

    def plus(total, term):
        return term if total is None else total + term

    for group in range(REACH):
        step = group + 1
        back = None
        for a in range(-REACH, REACH + 1):
            at = 8 * group + a + REACH
            total = plus(total, weight(y, at) * turned[group, y + a])
            back = plus(back, weight(y - a, at) * field[y - a])
        total = total + weight(y, 8 * group + 7) * field[y + step]
        total = total + weight(y - step, 8 * group + 7) * field[y - step]
        total = total + shifted(back, -step)
    return total


def softmax(value):
    top = jnp.max(value, axis=0, keepdims=True)
    power = jnp.exp(value - top)
    return power * (1.0 / jnp.sum(power, axis=0, keepdims=True))


def field_kernel(
    compat, compat_t, centre, inner, outer_feat, outer_rest, inner_corner, outer_corner,
    from_left, from_right, feat_out, kern_out, prob0_out, prob1_out, grad1_out, grad0_out, unary_out, share,
    feat, feat_turned, norm, norm_turned, kern, unary, grad, prob0, prob1, grad1, grad0,
    turned, message0, message1, logit1, logit0, turner,
):
    height = centre.shape[0]
    rows = height + 2 * HALO
    channels = feat.shape[1]
    side = lane()

    feat[pl.ds(0, REACH)] = jnp.zeros((REACH,) + feat.shape[1:], jnp.float32)
    feat[pl.ds(rows + REACH, REACH)] = jnp.zeros((REACH,) + feat.shape[1:], jnp.float32)

    def put(row, main, left, left_at, right, right_at):
        moved_right = pltpu.roll(right, (128 - right_at) % 128, axis=1)
        moved_left = pltpu.roll(left, (128 - STRIP - left_at) % 128, axis=1)
        edge = jnp.where(side < 64, moved_right, moved_left)
        for value, cols in ((main, slice(0, 128)), (edge, slice(128, 256))):
            feat[row + REACH, :, cols] = value[0:channels]
            unary[row, :, cols] = value[channels : channels + PAD]
            if value.shape[0] > channels + PAD:
                grad[row, :, cols] = value[channels + PAD :]

    for y in range(height):
        at = (y % 8) * STRIP
        put(HALO + y, centre[y], from_left[y // 8], at, from_right[y // 8], at)

    depth = channels + 2 * PAD
    short = channels + PAD
    near = HALO // 2

    def put_inner(i, top):
        return inner[i]

    def put_outer(i, top):
        parts = [outer_feat[i].astype(jnp.float32), outer_rest[i]]
        row = i if top else i - near
        if 0 <= row < near:
            parts.append(outer_rest[HALO + row])
        return jnp.concatenate(parts, axis=0)

    def put_rows(main, corner, top):
        base = HALO + height if top else 0
        half = HALO - 8
        for i in range(HALO):
            at = (i if top else i - half) * STRIP
            if 0 <= at < 128:
                left, right = corner[pl.ds(0, depth)], corner[pl.ds(depth, depth)]
                left_at = right_at = at
            else:
                left = right = corner[pl.ds(2 * depth, short)]
                left_at = (i - 8) * STRIP if top else 64 + i * STRIP
                right_at = (left_at + 64) % 128
            rows_main = main(i, top)
            size = min(rows_main.shape[0], left.shape[0])
            put(base + i, rows_main[0:size], left[0:size], left_at, right[0:size], right_at)

    even, has_left, has_right, first_row, all_rows = position(height)
    for main, corner, below in (
        (put_inner, inner_corner, even),
        (put_outer, outer_corner, jnp.logical_not(even)),
    ):
        pl.when(below)(functools.partial(put_rows, main, corner, True))
        pl.when(jnp.logical_not(below))(functools.partial(put_rows, main, corner, False))

    wide_lane = lane(256)
    inside_lane = (
        (wide_lane < 128)
        | ((wide_lane < 192) & has_right)
        | ((wide_lane >= 192) & has_left)
    )

    def inside(y):
        row = first_row + y
        return inside_lane & (row >= 0) & (row < all_rows)

    turner[...] = turns(range(1, REACH + 1), 256)
    block = (rows + 2 * REACH) // 2

    def turn_feat(at):
        value = feat[pl.ds(at * block, block)].reshape(block * channels, 256)
        moved = jnp.dot(
            value.astype(jnp.bfloat16), turner[...], preferred_element_type=jnp.float32
        )
        for group in range(REACH):
            feat_turned[group, pl.ds(at * block, block)] = moved[
                :, 256 * group : 256 * group + 256
            ].reshape(block, channels, 256)

    each_row(0, (rows + 2 * REACH) // block, 1, turn_feat)

    def turn_norm(row):
        value = feat[row]
        size = fold(value * value) * 0.5
        norm[row] = size
        for group in range(REACH):
            norm_turned[group, row] = shifted(size, group + 1)

    each_row(0, rows + 2 * REACH, 6, turn_norm)

    sub = sublane()

    def affinity_row(y):
        for tile in range(2):
            cols = pl.ds(128 * tile, 128)
            here = feat[y + REACH, :, cols]
            size = norm[y + REACH, :, cols]
            for group in range(REACH):
                parts = []
                for a in range(-REACH, REACH + 1):
                    there = feat_turned[group, y + a + REACH, :, cols]
                    parts.append(
                        fold(here * there) - (size + norm_turned[group, y + a + REACH, :, cols])
                    )
                below = y + group + 1 + REACH
                parts.append(fold(here * feat[below, :, cols]) - (size + norm[below, :, cols]))
                step_a = jnp.where(sub == 7, group + 1, sub - REACH)
                step_b = jnp.where(sub == 7, 0, group + 1)
                far = (step_a * step_a + step_b * step_b).astype(jnp.float32)
                kern[y, pl.ds(8 * group, 8), cols] = jnp.exp(
                    merge(parts) - far * (1.0 / (2.0 * REACH * REACH))
                )

    each_row(0, rows, 1, affinity_row)

    def put_field(field, y, value):
        field[y] = value
        for group in range(REACH):
            turned[group, y] = shifted(value, group + 1)

    def start(y):
        put_field(prob0, y, jnp.where(inside(y), softmax(unary[y]), 0.0))

    each_row(0, rows, 4, start)

    def run_pass(field, out, low, high):
        def body(y):
            out[y] = pass_row(y, kern, field, turned)

        each_row(low, high, 2, body)

    run_pass(prob0, message0, REACH, rows - REACH)

    def mix(y):
        value = softmax(unary[y] - apply(compat[...], message0[y]))
        put_field(prob1, y, jnp.where(inside(y), value, 0.0))

    each_row(REACH, rows - REACH, 4, mix)
    run_pass(prob1, message1, 2 * REACH, rows - 2 * REACH)

    def back1(y):
        prob = softmax(unary[y] - apply(compat[...], message1[y]))
        cot = grad[y]
        change = prob * (cot - jnp.sum(cot * prob, axis=0, keepdims=True))
        logit1[y] = change
        put_field(grad1, y, jnp.where(inside(y), -apply(compat_t[...], change), 0.0))

    each_row(2 * REACH, rows - 2 * REACH, 4, back1)
    total = jnp.zeros((PAD, PAD), jnp.float32)

    def add_share(change, message):
        def body(turn, carry):
            at = HALO + 4 * turn
            left = jnp.concatenate([change[at + i, :, 0:128] for i in range(4)], axis=1)
            right = jnp.concatenate([message[at + i, :, 0:128] for i in range(4)], axis=1)
            return carry - outer(left, right)

        return body

    total = lax.fori_loop(0, height // 4, add_share(logit1, message1), total)
    run_pass(grad1, message1, 3 * REACH, rows - 3 * REACH)

    def back0(y):
        prob = prob1[y]
        cot = message1[y]
        change = prob * (cot - jnp.sum(cot * prob, axis=0, keepdims=True))
        logit0[y] = change
        grad0[y] = jnp.where(inside(y), -apply(compat_t[...], change), 0.0)

    each_row(3 * REACH, rows - 3 * REACH, 4, back0)
    total = lax.fori_loop(0, height // 4, add_share(logit0, message0), total)

    total = jnp.concatenate([total, jnp.zeros((PAD, 128 - PAD), jnp.float32)], axis=1)
    packed = (
        total[0:8]
        + pltpu.roll(total[8:16], 32, axis=1)
        + pltpu.roll(total[16:24], 64, axis=1)
    )
    for slot in range(share.shape[0]):
        share[slot] = packed

    def copy(row):
        at = row + HALO - REACH
        feat_out[row] = feat[at + REACH].astype(jnp.bfloat16)
        prob0_out[row] = prob0[at]
        prob1_out[row] = prob1[at]
        grad1_out[row] = grad1[at]
        grad0_out[row] = grad0[at]
        kern_out[row] = kern[at]

    each_row(0, height + 2 * REACH, 2, copy)

    def add_logit(y):
        unary_out[y] = logit0[y + HALO, :, 0:128] + logit1[y + HALO, :, 0:128]

    each_row(0, height, 4, add_logit)


def iterate(compat, centre, received, devices):
    height, depth, _ = centre.shape
    channels = depth - 2 * PAD
    rows = height + 2 * HALO
    tall = rows + 2 * REACH
    near = height + 2 * REACH

    def shape(*dims):
        return jax.ShapeDtypeStruct(dims, jnp.float32)

    def room(*dims):
        return pltpu.VMEM(dims, jnp.float32)

    return pl.pallas_call(
        field_kernel,
        out_shape=(
            jax.ShapeDtypeStruct((near, channels, 256), jnp.bfloat16),
            shape(near, PAD, 256),
            shape(near, PAD, 256),
            shape(near, PAD, 256),
            shape(near, PAD, 256),
            shape(near, PAD, 256),
            shape(height, PAD, 128),
            shape(devices, 8, 128),
        ),
        in_specs=[VMEM] * 10,
        out_specs=(VMEM,) * 8,
        scratch_shapes=[
            room(tall, channels, 256),
            room(REACH, tall, channels, 256),
            room(tall, 8, 256),
            room(REACH, tall, 8, 256),
            *[room(rows, PAD, 256)] * 7,
            room(REACH, rows, PAD, 256),
            *[room(rows, PAD, 256)] * 4,
            pltpu.VMEM((256, REACH * 256), jnp.bfloat16),
        ],
        compiler_params=params(),
        name="iterate",
    )(spread(compat), spread(compat.T), centre, *received)


def finish_kernel(
    feat, kern, prob0, prob1, grad1, grad0, partial, unary_out, feat_out,
    feat_turned, all_turned, kern_back, weights, turner,
):
    height = partial.shape[0]
    near = height + 2 * REACH
    channels = feat.shape[1]
    classes = unary_out.shape[0] // height
    steps = range(-REACH, REACH + 1)

    turner[...] = turns(steps, 128)
    block = near // 2
    column = lane()

    def moved(main, edge, b):
        if b == 0:
            return main
        mixed = jnp.where((column < b) if b > 0 else (column >= 128 + b), edge, main)
        return pltpu.roll(mixed, (-b) % 128, axis=1)

    def prepare_feat(at):
        value = feat[pl.ds(at * block, block)].reshape(block * channels, 256)
        full = jnp.dot(value, turner[...], preferred_element_type=jnp.float32)
        for place in range(len(steps)):
            feat_turned[place, pl.ds(at * block, block)] = full[
                :, 128 * place : 128 * place + 128
            ].reshape(block, channels, 128)

    each_row(0, near // block, 1, prepare_feat)

    def prepare(row):
        for place, field in enumerate((prob0, prob1, grad1, grad0)):
            main, edge = field[row, :, 0:128], field[row, :, 128:256]
            for b in steps:
                all_turned[b + REACH, row, pl.ds(place * PAD, PAD), :] = moved(main, edge, b)
        for group in range(REACH):
            rows = pl.ds(8 * group, 8)
            main, edge = kern[row, rows, 0:128], kern[row, rows, 128:256]
            kern_back[row, rows, :] = jnp.where(
                sublane() == 7, main, moved(main, edge, -(group + 1))
            )

    each_row(0, near, 2, prepare)

    def pass_centre(y):
        total = jnp.zeros((PAD, 128), jnp.float32)
        last = pl.ds(3 * PAD, PAD)
        for group in range(REACH):
            step = group + 1
            back = [jnp.zeros((PAD, 128), jnp.float32)] * 2
            for a in range(-REACH, REACH + 1):
                one = pl.ds(8 * group + a + REACH, 1)
                total = total + kern[y, one, 0:128] * all_turned[step + REACH, y + a, last, :]
                for tile in range(2):
                    cols = slice(128 * tile, 128 * tile + 128)
                    back[tile] = back[tile] + kern[y - a, one, cols] * grad0[y - a, :, cols]
            one = pl.ds(8 * group + 7, 1)
            total = total + kern[y, one, 0:128] * grad0[y + step, :, 0:128]
            total = total + kern[y - step, one, 0:128] * grad0[y - step, :, 0:128]
            total = total + moved(back[0], back[1], -step)
        return total

    def unary_row(y):
        cot = pass_centre(y + REACH)
        prob = prob0[y + REACH, :, 0:128]
        value = partial[y] + prob * (cot - jnp.sum(cot * prob, axis=0, keepdims=True))
        for start in range(0, classes, 8):
            size = min(8, classes - start)
            unary_out[pl.ds(start * height + y, size, stride=height), :] = value[
                start : start + size
            ]

    each_row(0, height, 2, unary_row)
    sub = sublane()

    def feature_row(y):
        row = y + REACH
        own = all_turned[REACH, row]
        mate = jnp.concatenate(
            [own[3 * PAD :], own[2 * PAD : 3 * PAD], own[PAD : 2 * PAD], own[0:PAD]], axis=0
        )
        total = None
        whole = None
        for sign in (1, -1):
            for group in range(REACH):
                parts = []
                places = []
                for s in range(8):
                    a, b = (s - REACH, group + 1) if s < 7 else (group + 1, 0)
                    a, b = sign * a, sign * b
                    places.append((a, b))
                    parts.append(fold(mate * all_turned[b + REACH, row + a]))
                if sign > 0:
                    weight = kern[row, pl.ds(8 * group, 8), 0:128]
                else:
                    weight = kern_back[row - (group + 1), pl.ds(8 * group, 8), :]
                    for s in range(7):
                        weight = jnp.where(
                            sub == s, kern_back[row - (s - REACH), pl.ds(8 * group, 8), :], weight
                        )
                weight = weight * merge(parts)
                whole = weight if whole is None else whole + weight
                at = 8 * (group + (0 if sign > 0 else REACH))
                weights[y, pl.ds(at, 8), :] = weight
                for s, (a, b) in enumerate(places):
                    term = weights[y, pl.ds(at + s, 1), :] * feat_turned[b + REACH, row + a]
                    total = term if total is None else total + term
        whole = jnp.sum(whole, axis=0, keepdims=True)
        total = total - whole * feat_turned[REACH, row]
        feat_out[pl.ds(y, channels, stride=height), :] = total * (1.0 / math.sqrt(channels))

    each_row(0, height, 1, feature_row)


def finish(feat, kern, prob0, prob1, grad1, grad0, partial, classes):
    near, channels, _ = feat.shape
    height = partial.shape[0]

    def room(*dims):
        return pltpu.VMEM(dims, jnp.float32)

    return pl.pallas_call(
        finish_kernel,
        out_shape=(
            jax.ShapeDtypeStruct((classes * height, 128), jnp.float32),
            jax.ShapeDtypeStruct((channels * height, 128), jnp.float32),
        ),
        in_specs=[VMEM] * 7,
        out_specs=(VMEM,) * 2,
        scratch_shapes=[
            room(2 * REACH + 1, near, channels, 128),
            room(2 * REACH + 1, near, 4 * PAD, 128),
            room(near, PAD, 128),
            room(height, 6 * 8, 128),
            pltpu.VMEM((256, (2 * REACH + 1) * 128), jnp.bfloat16),
        ],
        compiler_params=params(),
        cost_estimate=pl.CostEstimate(flops=200_000_000, bytes_accessed=8_000_000, transcendentals=0),
        name="finish",
    )(feat, kern, prob0, prob1, grad1, grad0, partial)


def on_device(unary, features, compat, grad_output):
    classes, height, width = unary.shape
    n_rows, n_cols = lax.axis_size("rows"), lax.axis_size("cols")

    below = [pair for i in range(0, n_rows, 2) for pair in ((i, i + 1), (i + 1, i))]
    above = [
        pair
        for i in range(1, n_rows, 2)
        for pair in ((i, (i + 1) % n_rows), ((i + 1) % n_rows, i))
    ]
    forward = [(i, i + 1) for i in range(n_cols - 1)]
    backward = [(i + 1, i) for i in range(n_cols - 1)]
    centre, left, right, inner, outer_feat, outer_rest = pack(features, unary, grad_output)
    inner = lax.ppermute(inner, "rows", below)
    outer_feat = lax.ppermute(outer_feat, "rows", above)
    outer_rest = lax.ppermute(outer_rest, "rows", above)
    from_left = lax.ppermute(right, "cols", forward)
    from_right = lax.ppermute(left, "cols", backward)
    inner_corner, outer_corner = corners(from_left, from_right, outer_feat)
    outer_corner = lax.ppermute(outer_corner, "rows", above)
    inner_corner = lax.ppermute(inner_corner, "rows", below)
    received = (
        inner, outer_feat, outer_rest, inner_corner, outer_corner, from_left, from_right
    )

    devices = n_rows * n_cols
    *fields, partial, share = iterate(
        compat, centre, received, devices
    )
    shares = lax.all_to_all(share, ("rows", "cols"), 0, 0)
    unary_grad, feature_grad = finish(*fields, partial, classes)
    summed = jnp.sum(shares, axis=0) / math.sqrt(n_rows * height * n_cols * width)
    compat_grad = jnp.concatenate(
        [summed[:, 0:PAD], summed[:, 32 : 32 + PAD], summed[:, 64 : 64 + PAD]], axis=0
    )[:classes, :classes]
    return (
        unary_grad.reshape(unary.shape),
        feature_grad.reshape(features.shape),
        compat_grad,
    )


def solution(mesh):
    placed = (P(None, "rows", "cols"), P(None, "rows", "cols"), P(), P(None, "rows", "cols"))
    return jax.shard_map(
        on_device,
        mesh=mesh,
        in_specs=placed,
        out_specs=(P(None, "rows", "cols"), P(None, "rows", "cols"), P()),
        check_vma=False,
    )
```

```python
import functools
import math

import jax
import jax.numpy as jnp
from jax import lax
from jax.experimental import pallas as pl
from jax.experimental.pallas import tpu as pltpu
from jax.sharding import PartitionSpec as P

ITERS = 2
REACH = 3
HALO = 2 * ITERS * REACH
STRIP = 16
PAD = 24
DEEP = 32
LOW = -1e30
VMEM = pl.BlockSpec(memory_space=pltpu.VMEM)


def params():
    return pltpu.CompilerParams(vmem_limit_bytes=56 * 1024 * 1024)


def position(height):
    row, col = lax.axis_index("rows"), lax.axis_index("cols")
    return (
        row % 2 == 0,
        col > 0,
        col < lax.axis_size("cols") - 1,
        row * height - HALO,
        lax.axis_size("rows") * height,
    )


def sublane(width=128):
    return lax.broadcasted_iota(jnp.int32, (8, width), 0)


def lane(width=128):
    return lax.broadcasted_iota(jnp.int32, (1, width), 1)


def shifted(value, step):
    low, high = value[:, 0:128], value[:, 128:256]
    column = lane() + step
    here = (column >= 0) & (column < 128)
    low = pltpu.roll(low, (-step) % 128, axis=1)
    high = pltpu.roll(high, (-step) % 128, axis=1)
    return jnp.concatenate([jnp.where(here, low, high), jnp.where(here, high, low)], axis=1)


def turns(steps, width):
    source = lax.broadcasted_iota(jnp.int32, (256, width), 0)
    target = lax.broadcasted_iota(jnp.int32, (256, width), 1)
    return jnp.concatenate(
        [(source == (target + step) % 256).astype(jnp.bfloat16) for step in steps], axis=1
    )


def each_row(low, high, step, body):
    def some(turn, carry):
        for at in range(step):
            body(low + turn * step + at)
        return carry

    turns = (high - low) // step
    if turns > 1:
        lax.fori_loop(0, turns, some, 0)
    else:
        turns = 0
    for y in range(low + turns * step, high):
        body(y)


def split(value):
    parts = []
    for _ in range(2):
        part = value.astype(jnp.bfloat16)
        parts.append(part)
        value = value - part.astype(jnp.float32)
    return parts + [value.astype(jnp.bfloat16)]


def deep(value):
    return jnp.concatenate([value, jnp.zeros((DEEP - PAD, value.shape[1]), value.dtype)], axis=0)


def apply(square, value):
    high, middle, low = [part.astype(jnp.float32) for part in split(value)]
    stack = jnp.concatenate([high, middle, high, low, middle, high], axis=0)
    return jnp.dot(square, stack.astype(jnp.bfloat16), preferred_element_type=jnp.float32)[0:PAD]


def spread(square):
    size = square.shape[0]
    square = jnp.pad(square, ((0, DEEP - size), (0, PAD - size)))
    high = lax.reduce_precision(square, 8, 7)
    middle = lax.reduce_precision(square - high, 8, 7)
    low = square - high - middle
    return jnp.concatenate([high, high, middle, high, middle, low], axis=1).astype(jnp.bfloat16)


def outer(left, right):
    left = jnp.concatenate(split(deep(left)), axis=0)
    right = jnp.concatenate(split(deep(right)), axis=0)
    full = lax.dot_general(
        left, right, (((1,), (1,)), ((), ())), preferred_element_type=jnp.float32
    )
    total = None
    for i in range(3):
        for j in range(3 - i):
            term = full[i * DEEP : i * DEEP + PAD, j * DEEP : j * DEEP + PAD]
            total = term if total is None else total + term
    return total


def merge(parts):
    row = sublane(parts[0].shape[-1])
    bit = 1
    while len(parts) > 1:
        low = (row & bit) == 0
        parts = [
            jnp.where(low, first, second)
            + pltpu.roll(jnp.where(low, second, first), 8 - bit, axis=0)
            for first, second in zip(parts[::2], parts[1::2])
        ]
        bit *= 2
    return parts[0]


def fold(value):
    total = value[0:8]
    for start in range(8, value.shape[0], 8):
        total = total + value[start : start + 8]
    return total


def pack_kernel(
    feat, unary, grad, centre, left, right, inner, outer_feat, outer_rest, wide
):
    channels, height, _ = feat.shape
    classes = unary.shape[0] // height
    wide[...] = feat[...].astype(jnp.float32).reshape(channels * height, 128) * (
        1.0 / math.sqrt(channels)
    )
    empty = jnp.zeros((PAD - classes, 128), jnp.float32)
    side = lane()
    for slot in range(height // 8):
        ends = [None, None]
        for i in range(8):
            y = 8 * slot + i
            rows = jnp.concatenate(
                [
                    wide[pl.ds(y, channels, stride=height), :],
                    unary[pl.ds(y, classes, stride=height), :],
                    empty + LOW,
                    grad[pl.ds(y, classes, stride=height), :],
                    empty,
                ],
                axis=0,
            )
            centre[y] = rows
            at = i * STRIP
            here = (side >= at) & (side < at + STRIP)
            for end, shift in ((0, at), (1, (at + STRIP) % 128)):
                moved = pltpu.roll(rows, shift, axis=1)
                ends[end] = moved if i == 0 else jnp.where(here, moved, ends[end])
        left[slot], right[slot] = ends
    even = position(height)[0]
    low = height - HALO
    inner_base = jnp.where(even, low, 0)
    outer_base = jnp.where(even, 0, low)
    grad_base = jnp.where(even, 0, height - HALO // 2)
    for i in range(HALO):
        inner[i] = centre[inner_base + i]
        outer_feat[i] = centre[outer_base + i, 0:channels].astype(jnp.bfloat16)
        outer_rest[i] = centre[outer_base + i, channels : channels + PAD]
    for i in range(HALO // 2):
        outer_rest[HALO + i] = centre[grad_base + i, channels + PAD :]


def pack(feat, unary, grad):
    channels, height, _ = feat.shape
    depth = channels + 2 * PAD

    def shape(*dims, dtype=jnp.float32):
        return jax.ShapeDtypeStruct(dims, dtype)

    return pl.pallas_call(
        pack_kernel,
        out_shape=(
            shape(height, depth, 128),
            shape(height // 8, depth, 128),
            shape(height // 8, depth, 128),
            shape(HALO, depth, 128),
            shape(HALO, channels, 128, dtype=jnp.bfloat16),
            shape(HALO + HALO // 2, PAD, 128),
        ),
        in_specs=[VMEM] * 3,
        out_specs=(VMEM,) * 6,
        scratch_shapes=[pltpu.VMEM((channels * height, 128), jnp.float32)],
        compiler_params=params(),
        name="pack",
    )(feat, unary.reshape(-1, 128), grad.reshape(-1, 128))


def corner_kernel(left, right, _, inner, outer):
    depth = left.shape[1]
    short = depth - PAD
    even = position(8 * left.shape[0])[0]
    side = lane()
    for out, top in ((inner, jnp.logical_not(even)), (outer, even)):
        whole = jnp.where(top, 0, 1)
        out[pl.ds(0, depth)] = left[whole]
        out[pl.ds(depth, depth)] = right[whole]
        mine = (side < 64) == top
        out[pl.ds(2 * depth, short)] = jnp.where(
            mine,
            left[1 - whole, 0:short],
            pltpu.roll(right[1 - whole, 0:short], 64, axis=1),
        )


def corners(left, right, earlier):
    depth = left.shape[1]
    out = jax.ShapeDtypeStruct((3 * depth - PAD, 128), jnp.float32)
    return pl.pallas_call(
        corner_kernel,
        out_shape=(out, out),
        in_specs=[VMEM, VMEM, pl.BlockSpec(memory_space=pl.ANY)],
        out_specs=(VMEM,) * 2,
        compiler_params=params(),
        name="corners",
    )(left, right, earlier)


def pass_row(y, kern, field, turned):
    def weight(row, at):
        return kern[row, pl.ds(at, 1), :]

    total = None

    def plus(total, term):
        return term if total is None else total + term

    for group in range(REACH):
        step = group + 1
        back = None
        for a in range(-REACH, REACH + 1):
            at = 8 * group + a + REACH
            total = plus(total, weight(y, at) * turned[group, y + a])
            back = plus(back, weight(y - a, at) * field[y - a])
        total = total + weight(y, 8 * group + 7) * field[y + step]
        total = total + weight(y - step, 8 * group + 7) * field[y - step]
        total = total + shifted(back, -step)
    return total


def softmax(value):
    top = jnp.max(value, axis=0, keepdims=True)
    power = jnp.exp(value - top)
    return power * (1.0 / jnp.sum(power, axis=0, keepdims=True))


def field_kernel(
    compat, compat_t, centre, inner, outer_feat, outer_rest, inner_corner, outer_corner,
    from_left, from_right, feat_out, kern_out, prob0_out, prob1_out, grad1_out, grad0_out, unary_out, share,
    feat, feat_turned, norm, norm_turned, kern, unary, grad, prob0, prob1, grad1, grad0,
    turned, message0, message1, logit1, logit0, turner,
):
    height = centre.shape[0]
    rows = height + 2 * HALO
    channels = feat.shape[1]
    side = lane()

    feat[pl.ds(0, REACH)] = jnp.zeros((REACH,) + feat.shape[1:], jnp.float32)
    feat[pl.ds(rows + REACH, REACH)] = jnp.zeros((REACH,) + feat.shape[1:], jnp.float32)

    def put(row, main, left, left_at, right, right_at):
        moved_right = pltpu.roll(right, (128 - right_at) % 128, axis=1)
        moved_left = pltpu.roll(left, (128 - STRIP - left_at) % 128, axis=1)
        edge = jnp.where(side < 64, moved_right, moved_left)
        for value, cols in ((main, slice(0, 128)), (edge, slice(128, 256))):
            feat[row + REACH, :, cols] = value[0:channels]
            unary[row, :, cols] = value[channels : channels + PAD]
            if value.shape[0] > channels + PAD:
                grad[row, :, cols] = value[channels + PAD :]

    for y in range(height):
        at = (y % 8) * STRIP
        put(HALO + y, centre[y], from_left[y // 8], at, from_right[y // 8], at)

    depth = channels + 2 * PAD
    short = channels + PAD
    near = HALO // 2

    def put_inner(i, top):
        return inner[i]

    def put_outer(i, top):
        parts = [outer_feat[i].astype(jnp.float32), outer_rest[i]]
        row = i if top else i - near
        if 0 <= row < near:
            parts.append(outer_rest[HALO + row])
        return jnp.concatenate(parts, axis=0)

    def put_rows(main, corner, top):
        base = HALO + height if top else 0
        half = HALO - 8
        for i in range(HALO):
            at = (i if top else i - half) * STRIP
            if 0 <= at < 128:
                left, right = corner[pl.ds(0, depth)], corner[pl.ds(depth, depth)]
                left_at = right_at = at
            else:
                left = right = corner[pl.ds(2 * depth, short)]
                left_at = (i - 8) * STRIP if top else 64 + i * STRIP
                right_at = (left_at + 64) % 128
            rows_main = main(i, top)
            size = min(rows_main.shape[0], left.shape[0])
            put(base + i, rows_main[0:size], left[0:size], left_at, right[0:size], right_at)

    even, has_left, has_right, first_row, all_rows = position(height)
    for main, corner, below in (
        (put_inner, inner_corner, even),
        (put_outer, outer_corner, jnp.logical_not(even)),
    ):
        pl.when(below)(functools.partial(put_rows, main, corner, True))
        pl.when(jnp.logical_not(below))(functools.partial(put_rows, main, corner, False))

    wide_lane = lane(256)
    inside_lane = (
        (wide_lane < 128)
        | ((wide_lane < 192) & has_right)
        | ((wide_lane >= 192) & has_left)
    )

    def inside(y):
        row = first_row + y
        return inside_lane & (row >= 0) & (row < all_rows)

    turner[...] = turns(range(1, REACH + 1), 256)
    tall = rows + 2 * REACH
    moved = jnp.dot(
        feat[...].reshape(tall * channels, 256).astype(jnp.bfloat16),
        turner[...],
        preferred_element_type=jnp.float32,
    )
    for group in range(REACH):
        feat_turned[group] = moved[:, 256 * group : 256 * group + 256].reshape(
            tall, channels, 256
        )

    def turn_norm(row):
        value = feat[row]
        size = fold(value * value) * 0.5
        norm[row] = size
        for group in range(REACH):
            norm_turned[group, row] = shifted(size, group + 1)

    each_row(0, rows + 2 * REACH, (rows + 2 * REACH) // 2, turn_norm)

    sub = sublane()

    def affinity_rows(y):
        for tile in range(2):
            cols = pl.ds(128 * tile, 128)
            here = [feat[y + i + REACH, :, cols] for i in range(2)]
            size = [norm[y + i + REACH, :, cols] for i in range(2)]
            for group in range(REACH):
                parts = [[], []]
                for row in range(-REACH, REACH + 2):
                    there = feat_turned[group, y + row + REACH, :, cols]
                    other = norm_turned[group, y + row + REACH, :, cols]
                    for i in range(2):
                        if -REACH <= row - i <= REACH:
                            parts[i].append(fold(here[i] * there) - (size[i] + other))
                step_a = jnp.where(sub == 7, group + 1, sub - REACH)
                step_b = jnp.where(sub == 7, 0, group + 1)
                far = (step_a * step_a + step_b * step_b).astype(jnp.float32)
                for i in range(2):
                    below = y + i + group + 1 + REACH
                    parts[i].append(
                        fold(here[i] * feat[below, :, cols]) - (size[i] + norm[below, :, cols])
                    )
                    kern[y + i, pl.ds(8 * group, 8), cols] = jnp.exp(
                        merge(parts[i]) - far * (1.0 / (2.0 * REACH * REACH))
                    )

    def affinity_turn(turn):
        affinity_rows(2 * turn)

    each_row(0, rows // 2, 1, affinity_turn)

    def put_field(field, y, value):
        field[y] = value
        for group in range(REACH):
            turned[group, y] = shifted(value, group + 1)

    def start(y):
        put_field(prob0, y, jnp.where(inside(y), softmax(unary[y]), 0.0))

    each_row(0, rows, rows // 2, start)

    def run_pass(field, out, low, high):
        def body(y):
            out[y] = pass_row(y, kern, field, turned)

        each_row(low, high, 2, body)

    run_pass(prob0, message0, REACH, rows - REACH)

    def mix(y):
        value = softmax(unary[y] - apply(compat[...], message0[y]))
        put_field(prob1, y, jnp.where(inside(y), value, 0.0))

    each_row(REACH, rows - REACH, rows, mix)
    run_pass(prob1, message1, 2 * REACH, rows - 2 * REACH)

    def back1(y):
        prob = softmax(unary[y] - apply(compat[...], message1[y]))
        cot = grad[y]
        change = prob * (cot - jnp.sum(cot * prob, axis=0, keepdims=True))
        logit1[y] = change
        put_field(grad1, y, jnp.where(inside(y), -apply(compat_t[...], change), 0.0))

    each_row(2 * REACH, rows - 2 * REACH, rows, back1)
    def share_of(change, message):
        block = range(HALO, HALO + height)
        left = jnp.concatenate([change[y, :, 0:128] for y in block], axis=1)
        right = jnp.concatenate([message[y, :, 0:128] for y in block], axis=1)
        return outer(left, right)

    total = -share_of(logit1, message1)
    run_pass(grad1, message1, 3 * REACH, rows - 3 * REACH)

    def back0(y):
        prob = prob1[y]
        cot = message1[y]
        change = prob * (cot - jnp.sum(cot * prob, axis=0, keepdims=True))
        logit0[y] = change
        grad0[y] = jnp.where(inside(y), -apply(compat_t[...], change), 0.0)

    each_row(3 * REACH, rows - 3 * REACH, rows, back0)
    total = total - share_of(logit0, message0)

    total = jnp.concatenate([total, jnp.zeros((PAD, 128 - PAD), jnp.float32)], axis=1)
    packed = (
        total[0:8]
        + pltpu.roll(total[8:16], 32, axis=1)
        + pltpu.roll(total[16:24], 64, axis=1)
    )
    for slot in range(share.shape[0]):
        share[slot] = packed

    def copy(row):
        at = row + HALO - REACH
        feat_out[row] = feat[at + REACH].astype(jnp.bfloat16)
        prob0_out[row] = prob0[at]
        prob1_out[row] = prob1[at]
        grad1_out[row] = grad1[at]
        grad0_out[row] = grad0[at]
        kern_out[row] = kern[at]

    each_row(0, height + 2 * REACH, 2, copy)

    def add_logit(y):
        unary_out[y] = logit0[y + HALO, :, 0:128] + logit1[y + HALO, :, 0:128]

    each_row(0, height, 4, add_logit)


def iterate(compat, centre, received, devices):
    height, depth, _ = centre.shape
    channels = depth - 2 * PAD
    rows = height + 2 * HALO
    tall = rows + 2 * REACH
    near = height + 2 * REACH

    def shape(*dims):
        return jax.ShapeDtypeStruct(dims, jnp.float32)

    def room(*dims):
        return pltpu.VMEM(dims, jnp.float32)

    return pl.pallas_call(
        field_kernel,
        out_shape=(
            jax.ShapeDtypeStruct((near, channels, 256), jnp.bfloat16),
            shape(near, PAD, 256),
            shape(near, PAD, 256),
            shape(near, PAD, 256),
            shape(near, PAD, 256),
            shape(near, PAD, 256),
            shape(height, PAD, 128),
            shape(devices, 8, 128),
        ),
        in_specs=[VMEM] * 10,
        out_specs=(VMEM,) * 8,
        scratch_shapes=[
            room(tall, channels, 256),
            room(REACH, tall, channels, 256),
            room(tall, 8, 256),
            room(REACH, tall, 8, 256),
            *[room(rows, PAD, 256)] * 7,
            room(REACH, rows, PAD, 256),
            *[room(rows, PAD, 256)] * 4,
            pltpu.VMEM((256, REACH * 256), jnp.bfloat16),
        ],
        compiler_params=params(),
        name="iterate",
    )(spread(compat), spread(compat.T), centre, *received)


def finish_kernel(
    feat, kern, prob0, prob1, grad1, grad0, partial, unary_out, feat_out,
    feat_turned, all_turned, kern_back, weights, turner,
):
    height = partial.shape[0]
    near = height + 2 * REACH
    channels = feat.shape[1]
    classes = unary_out.shape[0] // height
    steps = range(-REACH, REACH + 1)

    turner[...] = turns(steps, 128)
    column = lane()

    def moved(main, edge, b):
        if b == 0:
            return main
        mixed = jnp.where((column < b) if b > 0 else (column >= 128 + b), edge, main)
        return pltpu.roll(mixed, (-b) % 128, axis=1)

    full = jnp.dot(
        feat[...].reshape(near * channels, 256), turner[...], preferred_element_type=jnp.float32
    )
    for place in range(len(steps)):
        feat_turned[place] = full[:, 128 * place : 128 * place + 128].reshape(near, channels, 128)

    def prepare(row):
        for place, field in enumerate((prob0, prob1, grad1, grad0)):
            main, edge = field[row, :, 0:128], field[row, :, 128:256]
            for b in steps:
                all_turned[b + REACH, row, pl.ds(place * PAD, PAD), :] = moved(main, edge, b)
        for group in range(REACH):
            rows = pl.ds(8 * group, 8)
            main, edge = kern[row, rows, 0:128], kern[row, rows, 128:256]
            kern_back[row, rows, :] = jnp.where(
                sublane() == 7, main, moved(main, edge, -(group + 1))
            )

    each_row(0, near, near, prepare)

    def pass_centre(y):
        total = jnp.zeros((PAD, 128), jnp.float32)
        last = pl.ds(3 * PAD, PAD)
        for group in range(REACH):
            step = group + 1
            back = [jnp.zeros((PAD, 128), jnp.float32)] * 2
            for a in range(-REACH, REACH + 1):
                one = pl.ds(8 * group + a + REACH, 1)
                total = total + kern[y, one, 0:128] * all_turned[step + REACH, y + a, last, :]
                for tile in range(2):
                    cols = slice(128 * tile, 128 * tile + 128)
                    back[tile] = back[tile] + kern[y - a, one, cols] * grad0[y - a, :, cols]
            one = pl.ds(8 * group + 7, 1)
            total = total + kern[y, one, 0:128] * grad0[y + step, :, 0:128]
            total = total + kern[y - step, one, 0:128] * grad0[y - step, :, 0:128]
            total = total + moved(back[0], back[1], -step)
        return total

    def unary_row(y):
        cot = pass_centre(y + REACH)
        prob = prob0[y + REACH, :, 0:128]
        value = partial[y] + prob * (cot - jnp.sum(cot * prob, axis=0, keepdims=True))
        for start in range(0, classes, 8):
            size = min(8, classes - start)
            unary_out[pl.ds(start * height + y, size, stride=height), :] = value[
                start : start + size
            ]

    each_row(0, height, 4, unary_row)
    sub = sublane()

    def feature_row(y):
        row = y + REACH
        own = all_turned[REACH, row]
        mate = jnp.concatenate(
            [own[3 * PAD :], own[2 * PAD : 3 * PAD], own[PAD : 2 * PAD], own[0:PAD]], axis=0
        )
        total = None
        whole = None
        for sign in (1, -1):
            for group in range(REACH):
                parts = []
                places = []
                for s in range(8):
                    a, b = (s - REACH, group + 1) if s < 7 else (group + 1, 0)
                    a, b = sign * a, sign * b
                    places.append((a, b))
                    parts.append(fold(mate * all_turned[b + REACH, row + a]))
                if sign > 0:
                    weight = kern[row, pl.ds(8 * group, 8), 0:128]
                else:
                    weight = kern_back[row - (group + 1), pl.ds(8 * group, 8), :]
                    for s in range(7):
                        weight = jnp.where(
                            sub == s, kern_back[row - (s - REACH), pl.ds(8 * group, 8), :], weight
                        )
                weight = weight * merge(parts)
                whole = weight if whole is None else whole + weight
                at = 8 * (group + (0 if sign > 0 else REACH))
                weights[y, pl.ds(at, 8), :] = weight
                for s, (a, b) in enumerate(places):
                    term = weights[y, pl.ds(at + s, 1), :] * feat_turned[b + REACH, row + a]
                    total = term if total is None else total + term
        whole = jnp.sum(whole, axis=0, keepdims=True)
        total = total - whole * feat_turned[REACH, row]
        feat_out[pl.ds(y, channels, stride=height), :] = total * (1.0 / math.sqrt(channels))

    each_row(0, height, 1, feature_row)


def finish(feat, kern, prob0, prob1, grad1, grad0, partial, classes):
    near, channels, _ = feat.shape
    height = partial.shape[0]

    def room(*dims):
        return pltpu.VMEM(dims, jnp.float32)

    return pl.pallas_call(
        finish_kernel,
        out_shape=(
            jax.ShapeDtypeStruct((classes * height, 128), jnp.float32),
            jax.ShapeDtypeStruct((channels * height, 128), jnp.float32),
        ),
        in_specs=[VMEM] * 7,
        out_specs=(VMEM,) * 2,
        scratch_shapes=[
            room(2 * REACH + 1, near, channels, 128),
            room(2 * REACH + 1, near, 4 * PAD, 128),
            room(near, PAD, 128),
            room(height, 6 * 8, 128),
            pltpu.VMEM((256, (2 * REACH + 1) * 128), jnp.bfloat16),
        ],
        compiler_params=params(),
        cost_estimate=pl.CostEstimate(flops=200_000_000, bytes_accessed=8_000_000, transcendentals=0),
        name="finish",
    )(feat, kern, prob0, prob1, grad1, grad0, partial)


def on_device(unary, features, compat, grad_output):
    classes, height, width = unary.shape
    n_rows, n_cols = lax.axis_size("rows"), lax.axis_size("cols")

    below = [pair for i in range(0, n_rows, 2) for pair in ((i, i + 1), (i + 1, i))]
    above = [
        pair
        for i in range(1, n_rows, 2)
        for pair in ((i, (i + 1) % n_rows), ((i + 1) % n_rows, i))
    ]
    forward = [(i, i + 1) for i in range(n_cols - 1)]
    backward = [(i + 1, i) for i in range(n_cols - 1)]
    centre, left, right, inner, outer_feat, outer_rest = pack(features, unary, grad_output)
    inner = lax.ppermute(inner, "rows", below)
    outer_feat = lax.ppermute(outer_feat, "rows", above)
    outer_rest = lax.ppermute(outer_rest, "rows", above)
    from_left = lax.ppermute(right, "cols", forward)
    from_right = lax.ppermute(left, "cols", backward)
    inner_corner, outer_corner = corners(from_left, from_right, outer_feat)
    outer_corner = lax.ppermute(outer_corner, "rows", above)
    inner_corner = lax.ppermute(inner_corner, "rows", below)
    received = (
        inner, outer_feat, outer_rest, inner_corner, outer_corner, from_left, from_right
    )

    devices = n_rows * n_cols
    *fields, partial, share = iterate(
        compat, centre, received, devices
    )
    shares = lax.all_to_all(share, ("rows", "cols"), 0, 0)
    unary_grad, feature_grad = finish(*fields, partial, classes)
    summed = jnp.sum(shares, axis=0) / math.sqrt(n_rows * height * n_cols * width)
    compat_grad = jnp.concatenate(
        [summed[:, 0:PAD], summed[:, 32 : 32 + PAD], summed[:, 64 : 64 + PAD]], axis=0
    )[:classes, :classes]
    return (
        unary_grad.reshape(unary.shape),
        feature_grad.reshape(features.shape),
        compat_grad,
    )


def solution(mesh):
    placed = (P(None, "rows", "cols"), P(None, "rows", "cols"), P(), P(None, "rows", "cols"))
    return jax.shard_map(
        on_device,
        mesh=mesh,
        in_specs=placed,
        out_specs=(P(None, "rows", "cols"), P(None, "rows", "cols"), P()),
        check_vma=False,
    )
```

```python
import functools
import math

import jax
import jax.numpy as jnp
from jax import lax
from jax.experimental import pallas as pl
from jax.experimental.pallas import tpu as pltpu
from jax.sharding import PartitionSpec as P

ITERS = 2
REACH = 3
HALO = 2 * ITERS * REACH
STRIP = 16
PAD = 24
DEEP = 32
LOW = -1e30
VMEM = pl.BlockSpec(memory_space=pltpu.VMEM)
ANY = pl.BlockSpec(memory_space=pl.ANY)


def params(mebibytes):
    return pltpu.CompilerParams(vmem_limit_bytes=mebibytes * 1024 * 1024)


def fetch(pairs, sems):
    copies = [
        pltpu.make_async_copy(source, target, sems.at[i])
        for i, (source, target) in enumerate(pairs)
    ]
    for copy in copies:
        copy.start()
    for copy in copies:
        copy.wait()


def like(array):
    return pltpu.VMEM(array.shape, array.dtype)


def position(height):
    row, col = lax.axis_index("rows"), lax.axis_index("cols")
    return (
        row % 2 == 0,
        col > 0,
        col < lax.axis_size("cols") - 1,
        row * height - HALO,
        lax.axis_size("rows") * height,
    )


def sublane(width=128):
    return lax.broadcasted_iota(jnp.int32, (8, width), 0)


def lane(width=128):
    return lax.broadcasted_iota(jnp.int32, (1, width), 1)


def shifted(value, step):
    low, high = value[:, 0:128], value[:, 128:256]
    column = lane() + step
    here = (column >= 0) & (column < 128)
    low = pltpu.roll(low, (-step) % 128, axis=1)
    high = pltpu.roll(high, (-step) % 128, axis=1)
    return jnp.concatenate([jnp.where(here, low, high), jnp.where(here, high, low)], axis=1)


def turns(steps, width):
    source = lax.broadcasted_iota(jnp.int32, (256, width), 0)
    target = lax.broadcasted_iota(jnp.int32, (256, width), 1)
    return jnp.concatenate(
        [(source == (target + step) % 256).astype(jnp.bfloat16) for step in steps], axis=1
    )


def each_row(low, high, step, body):
    def some(turn, carry):
        for at in range(step):
            body(low + turn * step + at)
        return carry

    turns = (high - low) // step
    if turns > 1:
        lax.fori_loop(0, turns, some, 0)
    else:
        turns = 0
    for y in range(low + turns * step, high):
        body(y)


def split(value):
    parts = []
    for _ in range(2):
        part = value.astype(jnp.bfloat16)
        parts.append(part)
        value = value - part.astype(jnp.float32)
    return parts + [value.astype(jnp.bfloat16)]


def deep(value):
    return jnp.concatenate([value, jnp.zeros((DEEP - PAD, value.shape[1]), value.dtype)], axis=0)


def apply(square, value):
    high, middle, low = [part.astype(jnp.float32) for part in split(value)]
    stack = jnp.concatenate([high, middle, high, low, middle, high], axis=0)
    return jnp.dot(square, stack.astype(jnp.bfloat16), preferred_element_type=jnp.float32)[0:PAD]


def spread(square):
    size = square.shape[0]
    square = jnp.pad(square, ((0, DEEP - size), (0, PAD - size)))
    high = lax.reduce_precision(square, 8, 7)
    middle = lax.reduce_precision(square - high, 8, 7)
    low = square - high - middle
    return jnp.concatenate([high, high, middle, high, middle, low], axis=1).astype(jnp.bfloat16)


def outer(left, right):
    left = jnp.concatenate(split(deep(left)), axis=0)
    right = jnp.concatenate(split(deep(right)), axis=0)
    full = lax.dot_general(
        left, right, (((1,), (1,)), ((), ())), preferred_element_type=jnp.float32
    )
    total = None
    for i in range(3):
        for j in range(3 - i):
            term = full[i * DEEP : i * DEEP + PAD, j * DEEP : j * DEEP + PAD]
            total = term if total is None else total + term
    return total


def merge(parts):
    row = sublane(parts[0].shape[-1])
    bit = 1
    while len(parts) > 1:
        low = (row & bit) == 0
        parts = [
            jnp.where(low, first, second)
            + pltpu.roll(jnp.where(low, second, first), 8 - bit, axis=0)
            for first, second in zip(parts[::2], parts[1::2])
        ]
        bit *= 2
    return parts[0]


def fold(value):
    total = value[0:8]
    for start in range(8, value.shape[0], 8):
        total = total + value[start : start + 8]
    return total


def pack_kernel(
    feat, unary, grad, centre, left, right, inner_feat, inner_rest, outer_feat, outer_rest, wide
):
    channels, height, _ = feat.shape
    classes = unary.shape[0] // height
    wide[...] = feat[...].astype(jnp.float32).reshape(channels * height, 128) * (
        1.0 / math.sqrt(channels)
    )
    empty = jnp.zeros((PAD - classes, 128), jnp.float32)
    side = lane()
    for slot in range(height // 8):
        ends = [None, None]
        for i in range(8):
            y = 8 * slot + i
            rows = jnp.concatenate(
                [
                    wide[pl.ds(y, channels, stride=height), :],
                    unary[pl.ds(y, classes, stride=height), :],
                    empty + LOW,
                    grad[pl.ds(y, classes, stride=height), :],
                    empty,
                ],
                axis=0,
            )
            centre[y] = rows
            at = i * STRIP
            here = (side >= at) & (side < at + STRIP)
            for end, shift in ((0, at), (1, (at + STRIP) % 128)):
                moved = pltpu.roll(rows, shift, axis=1)
                ends[end] = moved if i == 0 else jnp.where(here, moved, ends[end])
        left[slot], right[slot] = ends
    even = position(height)[0]
    low = height - HALO
    for feat_out, rest_out, top in (
        (inner_feat, inner_rest, jnp.logical_not(even)),
        (outer_feat, outer_rest, even),
    ):
        base = jnp.where(top, 0, low)
        grad_base = jnp.where(top, 0, height - HALO // 2)
        for i in range(HALO):
            feat_out[i] = centre[base + i, 0:channels].astype(jnp.bfloat16)
            rest_out[i] = centre[base + i, channels : channels + PAD]
        for i in range(HALO // 2):
            rest_out[HALO + i] = centre[grad_base + i, channels + PAD :]


def pack(feat, unary, grad):
    channels, height, _ = feat.shape
    depth = channels + 2 * PAD

    def shape(*dims, dtype=jnp.float32):
        return jax.ShapeDtypeStruct(dims, dtype)

    return pl.pallas_call(
        pack_kernel,
        out_shape=(
            shape(height, depth, 128),
            shape(height // 8, depth, 128),
            shape(height // 8, depth, 128),
            shape(HALO, channels, 128, dtype=jnp.bfloat16),
            shape(HALO + HALO // 2, PAD, 128),
            shape(HALO, channels, 128, dtype=jnp.bfloat16),
            shape(HALO + HALO // 2, PAD, 128),
        ),
        in_specs=[VMEM] * 3,
        out_specs=(VMEM,) * 7,
        scratch_shapes=[pltpu.VMEM((channels * height, 128), jnp.float32)],
        compiler_params=params(56),
        name="pack",
    )(feat, unary.reshape(-1, 128), grad.reshape(-1, 128))


def corner_kernel(left_in, right_in, _, inner, outer, left, right, sems):
    fetch([(left_in, left), (right_in, right)], sems)
    depth = left.shape[1]
    short = depth - PAD
    even = position(8 * left.shape[0])[0]
    side = lane()
    for out, top in ((inner, jnp.logical_not(even)), (outer, even)):
        whole = jnp.where(top, 0, 1)
        out[pl.ds(0, depth)] = left[whole]
        out[pl.ds(depth, depth)] = right[whole]
        mine = (side < 64) == top
        out[pl.ds(2 * depth, short)] = jnp.where(
            mine,
            left[1 - whole, 0:short],
            pltpu.roll(right[1 - whole, 0:short], 64, axis=1),
        )


def corners(left, right, earlier):
    depth = left.shape[1]
    out = jax.ShapeDtypeStruct((3 * depth - PAD, 128), jnp.float32)
    return pl.pallas_call(
        corner_kernel,
        out_shape=(out, out),
        in_specs=[ANY] * 3,
        out_specs=(VMEM,) * 2,
        scratch_shapes=[like(left), like(right), pltpu.SemaphoreType.DMA((2,))],
        compiler_params=params(4),
        name="corners",
    )(left, right, earlier)


def pass_row(y, kern, field, turned):
    def weight(row, at):
        return kern[row, pl.ds(at, 1), :]

    total = None

    def plus(total, term):
        return term if total is None else total + term

    for group in range(REACH):
        step = group + 1
        back = None
        for a in range(-REACH, REACH + 1):
            at = 8 * group + a + REACH
            total = plus(total, weight(y, at) * turned[group, y + a])
            back = plus(back, weight(y - a, at) * field[y - a])
        total = total + weight(y, 8 * group + 7) * field[y + step]
        total = total + weight(y - step, 8 * group + 7) * field[y - step]
        total = total + shifted(back, -step)
    return total


def softmax(value):
    top = jnp.max(value, axis=0, keepdims=True)
    power = jnp.exp(value - top)
    return power * (1.0 / jnp.sum(power, axis=0, keepdims=True))


def field_kernel(
    compat, compat_t, centre, inner_feat, inner_rest, outer_feat, outer_rest, inner_corner,
    outer_corner, from_left, from_right, feat_out, kern_out, prob0_out, prob1_out, grad1_out,
    grad0_out, unary_out, share,
    feat, feat_turned, norm, norm_turned, kern, unary, grad, prob0, prob1, grad1, grad0,
    turned, message0, message1, logit1, logit0, turner,
):
    height = centre.shape[0]
    rows = height + 2 * HALO
    channels = feat.shape[1]
    side = lane()

    feat[pl.ds(0, REACH)] = jnp.zeros((REACH,) + feat.shape[1:], jnp.float32)
    feat[pl.ds(rows + REACH, REACH)] = jnp.zeros((REACH,) + feat.shape[1:], jnp.float32)

    def put(row, main, left, left_at, right, right_at):
        moved_right = pltpu.roll(right, (128 - right_at) % 128, axis=1)
        moved_left = pltpu.roll(left, (128 - STRIP - left_at) % 128, axis=1)
        edge = jnp.where(side < 64, moved_right, moved_left)
        for value, cols in ((main, slice(0, 128)), (edge, slice(128, 256))):
            feat[row + REACH, :, cols] = value[0:channels]
            unary[row, :, cols] = value[channels : channels + PAD]
            if value.shape[0] > channels + PAD:
                grad[row, :, cols] = value[channels + PAD :]

    for y in range(height):
        at = (y % 8) * STRIP
        put(HALO + y, centre[y], from_left[y // 8], at, from_right[y // 8], at)

    depth = channels + 2 * PAD
    short = channels + PAD
    near = HALO // 2

    def edge_row(feat_in, rest_in, i, top):
        parts = [feat_in[i].astype(jnp.float32), rest_in[i]]
        row = i if top else i - near
        if 0 <= row < near:
            parts.append(rest_in[HALO + row])
        return jnp.concatenate(parts, axis=0)

    def put_rows(main, corner, top):
        base = HALO + height if top else 0
        half = HALO - 8
        for i in range(HALO):
            at = (i if top else i - half) * STRIP
            if 0 <= at < 128:
                left, right = corner[pl.ds(0, depth)], corner[pl.ds(depth, depth)]
                left_at = right_at = at
            else:
                left = right = corner[pl.ds(2 * depth, short)]
                left_at = (i - 8) * STRIP if top else 64 + i * STRIP
                right_at = (left_at + 64) % 128
            rows_main = main(i, top)
            size = min(rows_main.shape[0], left.shape[0])
            put(base + i, rows_main[0:size], left[0:size], left_at, right[0:size], right_at)

    even, has_left, has_right, first_row, all_rows = position(height)
    for main, corner, below in (
        (functools.partial(edge_row, inner_feat, inner_rest), inner_corner, even),
        (functools.partial(edge_row, outer_feat, outer_rest), outer_corner, jnp.logical_not(even)),
    ):
        pl.when(below)(functools.partial(put_rows, main, corner, True))
        pl.when(jnp.logical_not(below))(functools.partial(put_rows, main, corner, False))

    wide_lane = lane(256)
    inside_lane = (
        (wide_lane < 128)
        | ((wide_lane < 192) & has_right)
        | ((wide_lane >= 192) & has_left)
    )

    def inside(y):
        row = first_row + y
        return inside_lane & (row >= 0) & (row < all_rows)

    turner[...] = turns(range(1, REACH + 1), 256)
    tall = rows + 2 * REACH
    moved = jnp.dot(
        feat[...].reshape(tall * channels, 256).astype(jnp.bfloat16),
        turner[...],
        preferred_element_type=jnp.float32,
    )
    for group in range(REACH):
        feat_turned[group] = moved[:, 256 * group : 256 * group + 256].reshape(
            tall, channels, 256
        )

    def turn_norm(row):
        value = feat[row]
        size = fold(value * value) * 0.5
        norm[row] = size
        for group in range(REACH):
            norm_turned[group, row] = shifted(size, group + 1)

    each_row(0, rows + 2 * REACH, (rows + 2 * REACH) // 2, turn_norm)

    sub = sublane()

    def affinity_rows(y):
        for tile in range(2):
            cols = pl.ds(128 * tile, 128)
            here = [feat[y + i + REACH, :, cols] for i in range(2)]
            size = [norm[y + i + REACH, :, cols] for i in range(2)]
            for group in range(REACH):
                parts = [[], []]
                for row in range(-REACH, REACH + 2):
                    there = feat_turned[group, y + row + REACH, :, cols]
                    other = norm_turned[group, y + row + REACH, :, cols]
                    for i in range(2):
                        if -REACH <= row - i <= REACH:
                            parts[i].append(fold(here[i] * there) - (size[i] + other))
                step_a = jnp.where(sub == 7, group + 1, sub - REACH)
                step_b = jnp.where(sub == 7, 0, group + 1)
                far = (step_a * step_a + step_b * step_b).astype(jnp.float32)
                for i in range(2):
                    below = y + i + group + 1 + REACH
                    parts[i].append(
                        fold(here[i] * feat[below, :, cols]) - (size[i] + norm[below, :, cols])
                    )
                    kern[y + i, pl.ds(8 * group, 8), cols] = jnp.exp(
                        merge(parts[i]) - far * (1.0 / (2.0 * REACH * REACH))
                    )

    def affinity_turn(turn):
        affinity_rows(2 * turn)

    each_row(0, rows // 2, 1, affinity_turn)

    def put_field(field, y, value):
        field[y] = value
        for group in range(REACH):
            turned[group, y] = shifted(value, group + 1)

    def start(y):
        put_field(prob0, y, jnp.where(inside(y), softmax(unary[y]), 0.0))

    each_row(0, rows, rows // 2, start)

    def run_pass(field, out, low, high):
        def body(y):
            out[y] = pass_row(y, kern, field, turned)

        each_row(low, high, 2, body)

    run_pass(prob0, message0, REACH, rows - REACH)

    def mix(y):
        value = softmax(unary[y] - apply(compat[...], message0[y]))
        put_field(prob1, y, jnp.where(inside(y), value, 0.0))

    each_row(REACH, rows - REACH, rows, mix)
    run_pass(prob1, message1, 2 * REACH, rows - 2 * REACH)

    def back1(y):
        prob = softmax(unary[y] - apply(compat[...], message1[y]))
        cot = grad[y]
        change = prob * (cot - jnp.sum(cot * prob, axis=0, keepdims=True))
        logit1[y] = change
        put_field(grad1, y, jnp.where(inside(y), -apply(compat_t[...], change), 0.0))

    each_row(2 * REACH, rows - 2 * REACH, rows, back1)
    def share_of(change, message):
        block = range(HALO, HALO + height)
        left = jnp.concatenate([change[y, :, 0:128] for y in block], axis=1)
        right = jnp.concatenate([message[y, :, 0:128] for y in block], axis=1)
        return outer(left, right)

    total = -share_of(logit1, message1)
    run_pass(grad1, message1, 3 * REACH, rows - 3 * REACH)

    def back0(y):
        prob = prob1[y]
        cot = message1[y]
        change = prob * (cot - jnp.sum(cot * prob, axis=0, keepdims=True))
        logit0[y] = change
        grad0[y] = jnp.where(inside(y), -apply(compat_t[...], change), 0.0)

    each_row(3 * REACH, rows - 3 * REACH, rows, back0)
    total = total - share_of(logit0, message0)

    total = jnp.concatenate([total, jnp.zeros((PAD, 128 - PAD), jnp.float32)], axis=1)
    packed = (
        total[0:8]
        + pltpu.roll(total[8:16], 32, axis=1)
        + pltpu.roll(total[16:24], 64, axis=1)
    )
    for slot in range(share.shape[0]):
        share[slot] = packed

    def copy(row):
        at = row + HALO - REACH
        feat_out[row] = feat[at + REACH].astype(jnp.bfloat16)
        prob0_out[row] = prob0[at]
        prob1_out[row] = prob1[at]
        grad1_out[row] = grad1[at]
        grad0_out[row] = grad0[at]
        kern_out[row] = kern[at]

    each_row(0, height + 2 * REACH, 2, copy)

    def add_logit(y):
        unary_out[y] = logit0[y + HALO, :, 0:128] + logit1[y + HALO, :, 0:128]

    each_row(0, height, 4, add_logit)


def iterate(compat, centre, received, devices):
    height, depth, _ = centre.shape
    channels = depth - 2 * PAD
    rows = height + 2 * HALO
    tall = rows + 2 * REACH
    near = height + 2 * REACH

    def shape(*dims):
        return jax.ShapeDtypeStruct(dims, jnp.float32)

    def room(*dims):
        return pltpu.VMEM(dims, jnp.float32)

    return pl.pallas_call(
        field_kernel,
        out_shape=(
            jax.ShapeDtypeStruct((near, channels, 256), jnp.bfloat16),
            shape(near, PAD, 256),
            shape(near, PAD, 256),
            shape(near, PAD, 256),
            shape(near, PAD, 256),
            shape(near, PAD, 256),
            shape(height, PAD, 128),
            shape(devices, 8, 128),
        ),
        in_specs=[VMEM] * (3 + len(received)),
        out_specs=(VMEM,) * 8,
        scratch_shapes=[
            room(tall, channels, 256),
            room(REACH, tall, channels, 256),
            room(tall, 8, 256),
            room(REACH, tall, 8, 256),
            *[room(rows, PAD, 256)] * 7,
            room(REACH, rows, PAD, 256),
            *[room(rows, PAD, 256)] * 4,
            pltpu.VMEM((256, REACH * 256), jnp.bfloat16),
        ],
        compiler_params=params(56),
        name="iterate",
    )(spread(compat), spread(compat.T), centre, *received)


def finish_kernel(
    feat, kern, prob0, prob1, grad1, grad0, partial, unary_out, feat_out,
    feat_turned, all_turned, kern_back, weights, turner,
):
    height = partial.shape[0]
    near = height + 2 * REACH
    channels = feat.shape[1]
    classes = unary_out.shape[0] // height
    steps = range(-REACH, REACH + 1)

    turner[...] = turns(steps, 128)
    column = lane()

    def moved(main, edge, b):
        if b == 0:
            return main
        mixed = jnp.where((column < b) if b > 0 else (column >= 128 + b), edge, main)
        return pltpu.roll(mixed, (-b) % 128, axis=1)

    full = jnp.dot(
        feat[...].reshape(near * channels, 256), turner[...], preferred_element_type=jnp.float32
    )
    for place in range(len(steps)):
        feat_turned[place] = full[:, 128 * place : 128 * place + 128].reshape(near, channels, 128)

    def prepare(row):
        for place, field in enumerate((prob0, prob1, grad1, grad0)):
            main, edge = field[row, :, 0:128], field[row, :, 128:256]
            for b in steps:
                all_turned[b + REACH, row, pl.ds(place * PAD, PAD), :] = moved(main, edge, b)
        for group in range(REACH):
            rows = pl.ds(8 * group, 8)
            main, edge = kern[row, rows, 0:128], kern[row, rows, 128:256]
            kern_back[row, rows, :] = jnp.where(
                sublane() == 7, main, moved(main, edge, -(group + 1))
            )

    each_row(0, near, near, prepare)

    def pass_centre(y):
        total = jnp.zeros((PAD, 128), jnp.float32)
        last = pl.ds(3 * PAD, PAD)
        for group in range(REACH):
            step = group + 1
            back = [jnp.zeros((PAD, 128), jnp.float32)] * 2
            for a in range(-REACH, REACH + 1):
                one = pl.ds(8 * group + a + REACH, 1)
                total = total + kern[y, one, 0:128] * all_turned[step + REACH, y + a, last, :]
                for tile in range(2):
                    cols = slice(128 * tile, 128 * tile + 128)
                    back[tile] = back[tile] + kern[y - a, one, cols] * grad0[y - a, :, cols]
            one = pl.ds(8 * group + 7, 1)
            total = total + kern[y, one, 0:128] * grad0[y + step, :, 0:128]
            total = total + kern[y - step, one, 0:128] * grad0[y - step, :, 0:128]
            total = total + moved(back[0], back[1], -step)
        return total

    def unary_row(y):
        cot = pass_centre(y + REACH)
        prob = prob0[y + REACH, :, 0:128]
        value = partial[y] + prob * (cot - jnp.sum(cot * prob, axis=0, keepdims=True))
        for start in range(0, classes, 8):
            size = min(8, classes - start)
            unary_out[pl.ds(start * height + y, size, stride=height), :] = value[
                start : start + size
            ]

    each_row(0, height, 4, unary_row)
    sub = sublane()

    def feature_row(y):
        row = y + REACH
        own = all_turned[REACH, row]
        mate = jnp.concatenate(
            [own[3 * PAD :], own[2 * PAD : 3 * PAD], own[PAD : 2 * PAD], own[0:PAD]], axis=0
        )
        total = None
        whole = None
        for sign in (1, -1):
            for group in range(REACH):
                parts = []
                places = []
                for s in range(8):
                    a, b = (s - REACH, group + 1) if s < 7 else (group + 1, 0)
                    a, b = sign * a, sign * b
                    places.append((a, b))
                    parts.append(fold(mate * all_turned[b + REACH, row + a]))
                if sign > 0:
                    weight = kern[row, pl.ds(8 * group, 8), 0:128]
                else:
                    weight = kern_back[row - (group + 1), pl.ds(8 * group, 8), :]
                    for s in range(7):
                        weight = jnp.where(
                            sub == s, kern_back[row - (s - REACH), pl.ds(8 * group, 8), :], weight
                        )
                weight = weight * merge(parts)
                whole = weight if whole is None else whole + weight
                at = 8 * (group + (0 if sign > 0 else REACH))
                weights[y, pl.ds(at, 8), :] = weight
                for s, (a, b) in enumerate(places):
                    term = weights[y, pl.ds(at + s, 1), :] * feat_turned[b + REACH, row + a]
                    total = term if total is None else total + term
        whole = jnp.sum(whole, axis=0, keepdims=True)
        total = total - whole * feat_turned[REACH, row]
        feat_out[pl.ds(y, channels, stride=height), :] = total * (1.0 / math.sqrt(channels))

    each_row(0, height, 1, feature_row)


def finish(feat, kern, prob0, prob1, grad1, grad0, partial, classes):
    near, channels, _ = feat.shape
    height = partial.shape[0]

    def room(*dims):
        return pltpu.VMEM(dims, jnp.float32)

    return pl.pallas_call(
        finish_kernel,
        out_shape=(
            jax.ShapeDtypeStruct((classes * height, 128), jnp.float32),
            jax.ShapeDtypeStruct((channels * height, 128), jnp.float32),
        ),
        in_specs=[VMEM] * 7,
        out_specs=(VMEM,) * 2,
        scratch_shapes=[
            room(2 * REACH + 1, near, channels, 128),
            room(2 * REACH + 1, near, 4 * PAD, 128),
            room(near, PAD, 128),
            room(height, 6 * 8, 128),
            pltpu.VMEM((256, (2 * REACH + 1) * 128), jnp.bfloat16),
        ],
        compiler_params=params(56),
        cost_estimate=pl.CostEstimate(flops=200_000_000, bytes_accessed=8_000_000, transcendentals=0),
        name="finish",
    )(feat, kern, prob0, prob1, grad1, grad0, partial)


def on_device(unary, features, compat, grad_output):
    classes, height, width = unary.shape
    n_rows, n_cols = lax.axis_size("rows"), lax.axis_size("cols")

    below = [pair for i in range(0, n_rows, 2) for pair in ((i, i + 1), (i + 1, i))]
    above = [
        pair
        for i in range(1, n_rows, 2)
        for pair in ((i, (i + 1) % n_rows), ((i + 1) % n_rows, i))
    ]
    forward = [(i, i + 1) for i in range(n_cols - 1)]
    backward = [(i + 1, i) for i in range(n_cols - 1)]
    centre, left, right, inner_feat, inner_rest, outer_feat, outer_rest = pack(
        features, unary, grad_output
    )
    inner_feat = lax.ppermute(inner_feat, "rows", below)
    inner_rest = lax.ppermute(inner_rest, "rows", below)
    outer_feat = lax.ppermute(outer_feat, "rows", above)
    outer_rest = lax.ppermute(outer_rest, "rows", above)
    from_left = lax.ppermute(right, "cols", forward)
    from_right = lax.ppermute(left, "cols", backward)
    inner_corner, outer_corner = corners(from_left, from_right, outer_rest)
    outer_corner = lax.ppermute(outer_corner, "rows", above)
    inner_corner = lax.ppermute(inner_corner, "rows", below)
    received = (
        inner_feat, inner_rest, outer_feat, outer_rest, inner_corner, outer_corner,
        from_left, from_right,
    )

    devices = n_rows * n_cols
    *fields, partial, share = iterate(
        compat, centre, received, devices
    )
    shares = lax.all_to_all(share, ("rows", "cols"), 0, 0)
    unary_grad, feature_grad = finish(*fields, partial, classes)
    summed = jnp.sum(shares, axis=0) / math.sqrt(n_rows * height * n_cols * width)
    compat_grad = jnp.concatenate(
        [summed[:, 0:PAD], summed[:, 32 : 32 + PAD], summed[:, 64 : 64 + PAD]], axis=0
    )[:classes, :classes]
    return (
        unary_grad.reshape(unary.shape),
        feature_grad.reshape(features.shape),
        compat_grad,
    )


def solution(mesh):
    placed = (P(None, "rows", "cols"), P(None, "rows", "cols"), P(), P(None, "rows", "cols"))
    return jax.shard_map(
        on_device,
        mesh=mesh,
        in_specs=placed,
        out_specs=(P(None, "rows", "cols"), P(None, "rows", "cols"), P()),
        check_vma=False,
    )
```

```python
import functools
import math

import jax
import jax.numpy as jnp
from jax import lax
from jax.experimental import pallas as pl
from jax.experimental.pallas import tpu as pltpu
from jax.sharding import PartitionSpec as P

ITERS = 2
REACH = 3
HALO = 2 * ITERS * REACH
GROUPS = 4
STRIP = 16
PAD = 24
DEEP = 32
LOW = -1e30
VMEM = pl.BlockSpec(memory_space=pltpu.VMEM)
ANY = pl.BlockSpec(memory_space=pl.ANY)


def params(mebibytes):
    return pltpu.CompilerParams(vmem_limit_bytes=mebibytes * 1024 * 1024)


def fetch(pairs, sems):
    copies = [
        pltpu.make_async_copy(source, target, sems.at[i])
        for i, (source, target) in enumerate(pairs)
    ]
    for copy in copies:
        copy.start()
    return copies


def wait(copies):
    for copy in copies:
        copy.wait()


def like(array):
    return pltpu.VMEM(array.shape, array.dtype)


def position(height):
    row, col = lax.axis_index("rows"), lax.axis_index("cols")
    return (
        row % 2 == 0,
        col > 0,
        col < lax.axis_size("cols") - 1,
        row * height - HALO,
        lax.axis_size("rows") * height,
    )


def sublane(width=128):
    return lax.broadcasted_iota(jnp.int32, (8, width), 0)


def lane(width=128):
    return lax.broadcasted_iota(jnp.int32, (1, width), 1)


def shifted(value, step):
    low, high = value[:, 0:128], value[:, 128:256]
    column = lane() + step
    here = (column >= 0) & (column < 128)
    low = pltpu.roll(low, (-step) % 128, axis=1)
    high = pltpu.roll(high, (-step) % 128, axis=1)
    return jnp.concatenate([jnp.where(here, low, high), jnp.where(here, high, low)], axis=1)


def turns(steps, width):
    source = lax.broadcasted_iota(jnp.int32, (256, width), 0)
    target = lax.broadcasted_iota(jnp.int32, (256, width), 1)
    return jnp.concatenate(
        [(source == (target + step) % 256).astype(jnp.bfloat16) for step in steps], axis=1
    )


def each_row(low, high, step, body):
    def some(turn, carry):
        for at in range(step):
            body(low + turn * step + at)
        return carry

    turns = (high - low) // step
    if turns > 1:
        lax.fori_loop(0, turns, some, 0)
    else:
        turns = 0
    for y in range(low + turns * step, high):
        body(y)


def split(value):
    parts = []
    for _ in range(2):
        part = value.astype(jnp.bfloat16)
        parts.append(part)
        value = value - part.astype(jnp.float32)
    return parts + [value.astype(jnp.bfloat16)]


def deep(value):
    return jnp.concatenate([value, jnp.zeros((DEEP - PAD, value.shape[1]), value.dtype)], axis=0)


def apply(square, value):
    high, middle, low = [part.astype(jnp.float32) for part in split(value)]
    stack = jnp.concatenate([high, middle, high, low, middle, high], axis=0)
    return jnp.dot(square, stack.astype(jnp.bfloat16), preferred_element_type=jnp.float32)[0:PAD]


def spread(square):
    high, middle, low = [part.astype(jnp.float32) for part in split(square[0:DEEP])]
    wide = [jnp.zeros((DEEP, 128), jnp.float32)] * 2
    for i, part in enumerate((high, high, middle, high, middle, low)):
        start = PAD * i
        moved = pltpu.roll(part, start % 128, axis=1)
        for tile in range(2):
            low_lane = start - 128 * tile
            if low_lane < 128 and low_lane + PAD > 0:
                here = (lane() >= low_lane) & (lane() < low_lane + PAD)
                wide[tile] = jnp.where(here, moved, wide[tile])
    return jnp.concatenate(wide, axis=1)[:, 0 : 6 * PAD].astype(jnp.bfloat16)


def outer(left, right):
    left = jnp.concatenate(split(deep(left)), axis=0)
    right = jnp.concatenate(split(deep(right)), axis=0)
    full = lax.dot_general(
        left, right, (((1,), (1,)), ((), ())), preferred_element_type=jnp.float32
    )
    total = None
    for i in range(3):
        for j in range(3 - i):
            term = full[i * DEEP : i * DEEP + PAD, j * DEEP : j * DEEP + PAD]
            total = term if total is None else total + term
    return total


def merge(parts):
    row = sublane(parts[0].shape[-1])
    bit = 1
    while len(parts) > 1:
        low = (row & bit) == 0
        parts = [
            jnp.where(low, first, second)
            + pltpu.roll(jnp.where(low, second, first), 8 - bit, axis=0)
            for first, second in zip(parts[::2], parts[1::2])
        ]
        bit *= 2
    return parts[0]


def fold(value):
    total = value[0:8]
    for start in range(8, value.shape[0], 8):
        total = total + value[start : start + 8]
    return total


def pack_kernel(
    feat, unary, grad, centre, left, right, inner_feat, inner_rest, outer_feat, outer_rest, wide
):
    channels, height, _ = feat.shape
    classes = unary.shape[0] // height
    wide[...] = feat[...].astype(jnp.float32).reshape(channels * height, 128) * (
        1.0 / math.sqrt(channels)
    )
    empty = jnp.zeros((PAD - classes, 128), jnp.float32)
    side = lane()
    for slot in range(height // 8):
        ends = [None, None]
        for i in range(8):
            y = 8 * slot + i
            rows = jnp.concatenate(
                [
                    wide[pl.ds(y, channels, stride=height), :],
                    unary[pl.ds(y, classes, stride=height), :],
                    empty + LOW,
                    grad[pl.ds(y, classes, stride=height), :],
                    empty,
                ],
                axis=0,
            )
            centre[y] = rows
            at = i * STRIP
            here = (side >= at) & (side < at + STRIP)
            for end, shift in ((0, at), (1, (at + STRIP) % 128)):
                moved = pltpu.roll(rows, shift, axis=1)
                ends[end] = moved if i == 0 else jnp.where(here, moved, ends[end])
        left[slot], right[slot] = ends
    even = position(height)[0]
    low = height - HALO
    for feat_out, rest_out, top in (
        (inner_feat, inner_rest, jnp.logical_not(even)),
        (outer_feat, outer_rest, even),
    ):
        base = jnp.where(top, 0, low)
        grad_base = jnp.where(top, 0, height - HALO // 2)
        for i in range(HALO):
            feat_out[i] = centre[base + i, 0:channels].astype(jnp.bfloat16)
            rest_out[i] = centre[base + i, channels : channels + PAD]
        for i in range(HALO // 2):
            rest_out[HALO + i] = centre[grad_base + i, channels + PAD :]


def pack(feat, unary, grad):
    channels, height, _ = feat.shape
    depth = channels + 2 * PAD

    def shape(*dims, dtype=jnp.float32):
        return jax.ShapeDtypeStruct(dims, dtype)

    return pl.pallas_call(
        pack_kernel,
        out_shape=(
            shape(height, depth, 128),
            shape(height // 8, depth, 128),
            shape(height // 8, depth, 128),
            shape(HALO, channels, 128, dtype=jnp.bfloat16),
            shape(HALO + HALO // 2, PAD, 128),
            shape(HALO, channels, 128, dtype=jnp.bfloat16),
            shape(HALO + HALO // 2, PAD, 128),
        ),
        in_specs=[VMEM] * 3,
        out_specs=(VMEM,) * 7,
        scratch_shapes=[pltpu.VMEM((channels * height, 128), jnp.float32)],
        compiler_params=params(56),
        name="pack",
    )(feat, unary.reshape(-1, 128), grad.reshape(-1, 128))


def corner_kernel(left_in, right_in, _, inner, outer, left, right, sems):
    wait(fetch([(left_in, left), (right_in, right)], sems))
    depth = left.shape[1]
    short = depth - PAD
    even = position(8 * left.shape[0])[0]
    side = lane()
    for out, top in ((inner, jnp.logical_not(even)), (outer, even)):
        whole = jnp.where(top, 0, 1)
        out[pl.ds(0, depth)] = left[whole]
        out[pl.ds(depth, depth)] = right[whole]
        mine = (side < 64) == top
        out[pl.ds(2 * depth, short)] = jnp.where(
            mine,
            left[1 - whole, 0:short],
            pltpu.roll(right[1 - whole, 0:short], 64, axis=1),
        )


def corners(left, right, earlier):
    depth = left.shape[1]
    out = jax.ShapeDtypeStruct((3 * depth - PAD, 128), jnp.float32)
    return pl.pallas_call(
        corner_kernel,
        out_shape=(out, out),
        in_specs=[ANY] * 3,
        out_specs=(VMEM,) * 2,
        scratch_shapes=[like(left), like(right), pltpu.SemaphoreType.DMA((2,))],
        compiler_params=params(4),
        name="corners",
    )(left, right, earlier)


def sizes(here, there, size, size_there):
    rows = here.shape[0]

    def body(row):
        value = here[row]
        size[row] = fold(value * value) * 0.5
        for group in range(REACH):
            value = there[group, row]
            size_there[group, row] = fold(value * value) * 0.5

    each_row(0, rows, rows // 2, body)


def affinities(here, there, size, size_there, out):
    sub = sublane()

    def two(turn):
        y = 2 * turn
        mine = [here[y + i + REACH] for i in range(2)]
        mine_size = [size[y + i + REACH] for i in range(2)]
        for group in range(REACH):
            parts = [[], []]
            for row in range(-REACH, REACH + 2):
                other = there[group, y + row + REACH]
                other_size = size_there[group, y + row + REACH]
                for i in range(2):
                    if -REACH <= row - i <= REACH:
                        parts[i].append(fold(mine[i] * other) - (mine_size[i] + other_size))
            step_a = jnp.where(sub == 7, group + 1, sub - REACH)
            step_b = jnp.where(sub == 7, 0, group + 1)
            far = (step_a * step_a + step_b * step_b).astype(jnp.float32)
            for i in range(2):
                below = y + i + group + 1 + REACH
                parts[i].append(fold(mine[i] * here[below]) - (mine_size[i] + size[below]))
                out[y + i, pl.ds(8 * group, 8), :] = jnp.exp(
                    merge(parts[i]) - far * (1.0 / (2.0 * REACH * REACH))
                )

    each_row(0, out.shape[0] // 2, 1, two)


def strip_edge(left, left_at, right, right_at):
    right = pltpu.roll(right, (128 - right_at) % 128, axis=1)
    left = pltpu.roll(left, (128 - STRIP - left_at) % 128, axis=1)
    return jnp.where(lane() < 64, right, left)


def main_kernel(
    centre_in, from_left_in, from_right_in, inner_in, outer_in, kern_out,
    centre, from_left, from_right, inner, outer, feat, short, turned, size, size_turned, turner,
    sems,
):
    coming = fetch(
        [
            (inner_in, inner), (outer_in, outer), (centre_in, centre),
            (from_left_in, from_left), (from_right_in, from_right),
        ],
        sems,
    )
    height, channels = centre.shape[0], feat.shape[1]
    tall = feat.shape[0]
    turner[...] = turns(range(1, REACH + 1), 128)
    blank = jnp.zeros((REACH, channels, 128), jnp.float32)
    for at in (0, tall - REACH):
        feat[pl.ds(at, REACH)] = blank
        short[pl.ds(at, REACH)] = jnp.zeros((REACH, channels, 256), jnp.bfloat16)
    even = position(height)[0]
    wait(coming)
    above = jnp.where(even, REACH + HALO + height, REACH)
    for source, base in ((inner, above), (outer, tall - HALO - above)):
        for i in range(HALO):
            feat[base + i] = source[i].astype(jnp.float32)
            short[base + i, :, 0:128] = source[i]
            short[base + i, :, 128:256] = jnp.zeros((channels, 128), jnp.bfloat16)
    for y in range(height):
        at = (y % 8) * STRIP
        row = y + HALO + REACH
        feat[row] = centre[y, 0:channels]
        short[row, :, 0:128] = centre[y, 0:channels].astype(jnp.bfloat16)
        edge = strip_edge(
            from_left[y // 8, 0:channels], at, from_right[y // 8, 0:channels], at
        )
        short[row, :, 128:256] = edge.astype(jnp.bfloat16)
    moved = jnp.dot(
        short[...].reshape(tall * channels, 256), turner[...], preferred_element_type=jnp.float32
    )
    for group in range(REACH):
        turned[group] = moved[:, 128 * group : 128 * group + 128].reshape(tall, channels, 128)
    sizes(feat, turned, size, size_turned)
    affinities(feat, turned, size, size_turned, kern_out)


def main_affinities(centre, from_left, from_right, inner, outer):
    height, depth, _ = centre.shape
    channels = depth - 2 * PAD
    rows = height + 2 * HALO
    tall = rows + 2 * REACH
    inputs = (centre, from_left, from_right, inner, outer)

    def room(*dims, dtype=jnp.float32):
        return pltpu.VMEM(dims, dtype)

    return pl.pallas_call(
        main_kernel,
        out_shape=jax.ShapeDtypeStruct((rows, PAD, 128), jnp.float32),
        in_specs=[ANY] * 5,
        out_specs=VMEM,
        scratch_shapes=[
            *map(like, inputs),
            room(tall, channels, 128),
            room(tall, channels, 256, dtype=jnp.bfloat16),
            room(REACH, tall, channels, 128),
            room(tall, 8, 128),
            room(REACH, tall, 8, 128),
            room(256, REACH * 128, dtype=jnp.bfloat16),
            pltpu.SemaphoreType.DMA((5,)),
        ],
        compiler_params=params(56),
        cost_estimate=pl.CostEstimate(
            flops=200_000_000, bytes_accessed=8_000_000, transcendentals=0
        ),
        name="main_affinities",
    )(*inputs)


def side_turns():
    target = lax.broadcasted_iota(jnp.int32, (256, 128), 1)
    source = lax.broadcasted_iota(jnp.int32, (256, 128), 0)
    place = target % 32
    column = jnp.where(place < 12, place - 12, jnp.where(place < 24, 116 + place, 101 + place))
    blocks = []
    for b in range(REACH + 1):
        hit = source == (column + b + 256) % 256
        blocks.append(
            jnp.concatenate(
                [(hit & (target // 32 == j)).astype(jnp.bfloat16) for j in range(GROUPS)], axis=0
            )
        )
    return jnp.concatenate(blocks, axis=1)


def pass_row(y, kern, field, turned):
    def weight(row, at):
        return kern[row, pl.ds(at, 1), :]

    total = None

    def plus(total, term):
        return term if total is None else total + term

    for group in range(REACH):
        step = group + 1
        back = None
        for a in range(-REACH, REACH + 1):
            at = 8 * group + a + REACH
            total = plus(total, weight(y, at) * turned[group, y + a])
            back = plus(back, weight(y - a, at) * field[y - a])
        total = total + weight(y, 8 * group + 7) * field[y + step]
        total = total + weight(y - step, 8 * group + 7) * field[y - step]
        total = total + shifted(back, -step)
    return total


def softmax(value):
    top = jnp.max(value, axis=0, keepdims=True)
    power = jnp.exp(value - top)
    return power * (1.0 / jnp.sum(power, axis=0, keepdims=True))


def field_kernel(
    square_in, centre_in, from_left_in, from_right_in, inner_feat_in, inner_rest_in,
    outer_feat_in, outer_rest_in, inner_corner_in, outer_corner_in, main_in,
    feat_out, kern_out, prob0_out, prob1_out, grad1_out, grad0_out, unary_out, share,
    centre, from_left, from_right, inner_feat, inner_rest, outer_feat, outer_rest, inner_corner,
    outer_corner, main, short, side_feat, side_turned, side_size, side_size_turned, side_kern,
    kern, unary, grad, prob0,
    prob1, grad1, grad0, turned, message0, message1, logit1, logit0, side_turner, square, compat, compat_t,
    in_sems, out_sems,
):
    coming = fetch(
        [
            (centre_in, centre), (from_left_in, from_left), (from_right_in, from_right),
            (inner_feat_in, inner_feat), (inner_rest_in, inner_rest),
            (outer_feat_in, outer_feat), (outer_rest_in, outer_rest),
            (inner_corner_in, inner_corner), (outer_corner_in, outer_corner), (main_in, main),
        ],
        in_sems,
    )
    going = []

    def send(source, target, low):
        copy = pltpu.make_async_copy(
            source.at[pl.ds(low, target.shape[0])], target, out_sems.at[len(going)]
        )
        copy.start()
        going.append(copy)

    height = centre.shape[0]
    rows = height + 2 * HALO
    channels = short.shape[1]
    side = lane()
    side_turner[...] = side_turns()
    square[...] = jnp.zeros_like(square)
    square[0 : square_in.shape[0], 0 : square_in.shape[1]] = square_in[...]
    compat[...] = spread(square[...])
    compat_t[...] = spread(square[...].T)

    for at in (0, rows + REACH):
        short[pl.ds(at, REACH)] = jnp.zeros((REACH, channels, 256), jnp.bfloat16)

    def put(row, own, left, left_at, right, right_at):
        edge = strip_edge(left, left_at, right, right_at)
        for value, cols in ((own, slice(0, 128)), (edge, slice(128, 256))):
            short[row + REACH, :, cols] = value[0:channels].astype(jnp.bfloat16)
            unary[row, :, cols] = value[channels : channels + PAD]
            if value.shape[0] > channels + PAD:
                grad[row, :, cols] = value[channels + PAD :]

    wait(coming[:3])
    for y in range(height):
        at = (y % 8) * STRIP
        put(HALO + y, centre[y], from_left[y // 8], at, from_right[y // 8], at)

    wait(coming[3:])
    depth = channels + 2 * PAD
    slim = channels + PAD
    near = HALO // 2

    def edge_row(feat_in, rest_in, i, top):
        parts = [feat_in[i].astype(jnp.float32), rest_in[i]]
        row = i if top else i - near
        if 0 <= row < near:
            parts.append(rest_in[HALO + row])
        return jnp.concatenate(parts, axis=0)

    def put_rows(edge_rows, corner, top):
        base = HALO + height if top else 0
        half = HALO - 8
        for i in range(HALO):
            at = (i if top else i - half) * STRIP
            if 0 <= at < 128:
                left, right = corner[pl.ds(0, depth)], corner[pl.ds(depth, depth)]
                left_at = right_at = at
            else:
                left = right = corner[pl.ds(2 * depth, slim)]
                left_at = (i - 8) * STRIP if top else 64 + i * STRIP
                right_at = (left_at + 64) % 128
            own = edge_rows(i, top)
            size = min(own.shape[0], left.shape[0])
            put(base + i, own[0:size], left[0:size], left_at, right[0:size], right_at)

    even, has_left, has_right, first_row, all_rows = position(height)
    for edge_rows, corner, below in (
        (functools.partial(edge_row, inner_feat, inner_rest), inner_corner, even),
        (functools.partial(edge_row, outer_feat, outer_rest), outer_corner, jnp.logical_not(even)),
    ):
        pl.when(below)(functools.partial(put_rows, edge_rows, corner, True))
        pl.when(jnp.logical_not(below))(functools.partial(put_rows, edge_rows, corner, False))

    wide_lane = lane(256)
    inside_lane = (
        (wide_lane < 128)
        | ((wide_lane < 192) & has_right)
        | ((wide_lane >= 192) & has_left)
    )

    def inside(y):
        row = first_row + y
        return inside_lane & (row >= 0) & (row < all_rows)

    send(short, feat_out, HALO)
    slots = rows // GROUPS
    tall = slots + 2 * REACH
    stacked = jnp.concatenate(
        [
            jnp.concatenate([short[slots * j + k] for j in range(GROUPS)], axis=1)
            for k in range(tall)
        ],
        axis=0,
    )
    moved = jnp.dot(stacked, side_turner[...], preferred_element_type=jnp.float32)
    side_feat[...] = moved[:, 0:128].reshape(tall, channels, 128)
    for group in range(REACH):
        start = 128 * group + 128
        side_turned[group] = moved[:, start : start + 128].reshape(tall, channels, 128)
    sizes(side_feat, side_turned, side_size, side_size_turned)
    affinities(side_feat, side_turned, side_size, side_size_turned, side_kern)
    for j in range(GROUPS):
        for k in range(slots):
            y, value = slots * j + k, side_kern[k]
            kern[y, :, 128:256] = pltpu.roll(value, (116 - 32 * j) % 128, axis=1)
            last = pltpu.roll(value, (101 - 32 * j) % 128, axis=1)
            kern[y, :, 0:128] = jnp.where(side < 128 - REACH, main[y], last)
    send(kern, kern_out, HALO - REACH)

    def put_field(field, y, value):
        field[y] = value
        for group in range(REACH):
            turned[group, y] = shifted(value, group + 1)

    def start(y):
        put_field(prob0, y, jnp.where(inside(y), softmax(unary[y]), 0.0))

    each_row(0, rows, rows // 2, start)
    send(prob0, prob0_out, HALO - REACH)

    def run_pass(field, out, low, high):
        def body(y):
            out[y] = pass_row(y, kern, field, turned)

        each_row(low, high, 2, body)

    run_pass(prob0, message0, REACH, rows - REACH)

    def mix(y):
        value = softmax(unary[y] - apply(compat[...], message0[y]))
        put_field(prob1, y, jnp.where(inside(y), value, 0.0))

    each_row(REACH, rows - REACH, rows, mix)
    send(prob1, prob1_out, HALO - REACH)
    run_pass(prob1, message1, 2 * REACH, rows - 2 * REACH)

    def back1(y):
        prob = softmax(unary[y] - apply(compat[...], message1[y]))
        cot = grad[y]
        change = prob * (cot - jnp.sum(cot * prob, axis=0, keepdims=True))
        logit1[y] = change
        put_field(grad1, y, jnp.where(inside(y), -apply(compat_t[...], change), 0.0))

    each_row(2 * REACH, rows - 2 * REACH, rows, back1)
    send(grad1, grad1_out, HALO - REACH)
    def share_of(change, message):
        block = range(HALO, HALO + height)
        left = jnp.concatenate([change[y, :, 0:128] for y in block], axis=1)
        right = jnp.concatenate([message[y, :, 0:128] for y in block], axis=1)
        return outer(left, right)

    total = -share_of(logit1, message1)
    run_pass(grad1, message1, 3 * REACH, rows - 3 * REACH)

    def back0(y):
        prob = prob1[y]
        cot = message1[y]
        change = prob * (cot - jnp.sum(cot * prob, axis=0, keepdims=True))
        logit0[y] = change
        grad0[y] = jnp.where(inside(y), -apply(compat_t[...], change), 0.0)

    each_row(3 * REACH, rows - 3 * REACH, rows, back0)
    send(grad0, grad0_out, HALO - REACH)
    total = total - share_of(logit0, message0)

    total = jnp.concatenate([total, jnp.zeros((PAD, 128 - PAD), jnp.float32)], axis=1)
    packed = (
        total[0:8]
        + pltpu.roll(total[8:16], 32, axis=1)
        + pltpu.roll(total[16:24], 64, axis=1)
    )
    for slot in range(share.shape[0]):
        share[slot] = packed

    def add_logit(y):
        unary_out[y] = logit0[y + HALO, :, 0:128] + logit1[y + HALO, :, 0:128]

    each_row(0, height, height, add_logit)
    wait(going)


def iterate(compat, centre, received, main, devices):
    height, depth, _ = centre.shape
    channels = depth - 2 * PAD
    rows = height + 2 * HALO
    tall = rows + 2 * REACH
    near = height + 2 * REACH
    slots = rows // GROUPS

    def shape(*dims):
        return jax.ShapeDtypeStruct(dims, jnp.float32)

    def room(*dims):
        return pltpu.VMEM(dims, jnp.float32)

    return pl.pallas_call(
        field_kernel,
        out_shape=(
            jax.ShapeDtypeStruct((near, channels, 256), jnp.bfloat16),
            shape(near, PAD, 256),
            shape(near, PAD, 256),
            shape(near, PAD, 256),
            shape(near, PAD, 256),
            shape(near, PAD, 256),
            shape(height, PAD, 128),
            shape(devices, 8, 128),
        ),
        in_specs=[VMEM] + [ANY] * (2 + len(received)),
        out_specs=(ANY,) * 6 + (VMEM,) * 2,
        scratch_shapes=[
            like(centre),
            *map(like, received),
            like(main),
            pltpu.VMEM((tall, channels, 256), jnp.bfloat16),
            room(slots + 2 * REACH, channels, 128),
            room(REACH, slots + 2 * REACH, channels, 128),
            room(slots + 2 * REACH, 8, 128),
            room(REACH, slots + 2 * REACH, 8, 128),
            room(slots, PAD, 128),
            *[room(rows, PAD, 256)] * 7,
            room(REACH, rows, PAD, 256),
            *[room(rows, PAD, 256)] * 4,
            pltpu.VMEM((GROUPS * 256, (REACH + 1) * 128), jnp.bfloat16),
            room(128, 128),
            pltpu.VMEM((DEEP, 6 * PAD), jnp.bfloat16),
            pltpu.VMEM((DEEP, 6 * PAD), jnp.bfloat16),
            pltpu.SemaphoreType.DMA((2 + len(received),)),
            pltpu.SemaphoreType.DMA((6,)),
        ],
        compiler_params=params(56),
        name="iterate",
    )(compat, centre, *received, main)


def finish_kernel(
    feat_in, kern_in, prob0_in, prob1_in, grad1_in, grad0_in, partial_in, unary_out, feat_out,
    feat, kern, prob0, prob1, grad1, grad0, partial, feat_turned, all_turned, kern_back, weights,
    turner, unary_rows, in_sems, out_sem,
):
    coming = fetch(
        [
            (feat_in, feat), (kern_in, kern), (prob0_in, prob0), (prob1_in, prob1),
            (grad1_in, grad1), (grad0_in, grad0), (partial_in, partial),
        ],
        in_sems,
    )
    height = partial.shape[0]
    near = height + 2 * REACH
    channels = feat.shape[1]
    classes = unary_out.shape[0] // height
    steps = range(-REACH, REACH + 1)

    turner[...] = turns(steps, 128)
    column = lane()

    def moved(main, edge, b):
        if b == 0:
            return main
        mixed = jnp.where((column < b) if b > 0 else (column >= 128 + b), edge, main)
        return pltpu.roll(mixed, (-b) % 128, axis=1)

    wait(coming[:1])
    full = jnp.dot(
        feat[...].reshape(near * channels, 256), turner[...], preferred_element_type=jnp.float32
    )
    for place in range(len(steps)):
        feat_turned[place] = full[:, 128 * place : 128 * place + 128].reshape(near, channels, 128)

    wait(coming[1:])

    def prepare(row):
        for place, field in enumerate((prob0, prob1, grad1, grad0)):
            main, edge = field[row, :, 0:128], field[row, :, 128:256]
            for b in steps:
                all_turned[b + REACH, row, pl.ds(place * PAD, PAD), :] = moved(main, edge, b)
        for group in range(REACH):
            rows = pl.ds(8 * group, 8)
            main, edge = kern[row, rows, 0:128], kern[row, rows, 128:256]
            kern_back[row, rows, :] = jnp.where(
                sublane() == 7, main, moved(main, edge, -(group + 1))
            )

    each_row(0, near, near, prepare)

    def pass_centre(y):
        total = jnp.zeros((PAD, 128), jnp.float32)
        last = pl.ds(3 * PAD, PAD)
        for group in range(REACH):
            step = group + 1
            back = [jnp.zeros((PAD, 128), jnp.float32)] * 2
            for a in range(-REACH, REACH + 1):
                one = pl.ds(8 * group + a + REACH, 1)
                total = total + kern[y, one, 0:128] * all_turned[step + REACH, y + a, last, :]
                for tile in range(2):
                    cols = slice(128 * tile, 128 * tile + 128)
                    back[tile] = back[tile] + kern[y - a, one, cols] * grad0[y - a, :, cols]
            one = pl.ds(8 * group + 7, 1)
            total = total + kern[y, one, 0:128] * grad0[y + step, :, 0:128]
            total = total + kern[y - step, one, 0:128] * grad0[y - step, :, 0:128]
            total = total + moved(back[0], back[1], -step)
        return total

    def unary_row(y):
        cot = pass_centre(y + REACH)
        prob = prob0[y + REACH, :, 0:128]
        value = partial[y] + prob * (cot - jnp.sum(cot * prob, axis=0, keepdims=True))
        for start in range(0, classes, 8):
            size = min(8, classes - start)
            unary_rows[pl.ds(start * height + y, size, stride=height), :] = value[
                start : start + size
            ]

    each_row(0, height, 4, unary_row)
    leaving = pltpu.make_async_copy(unary_rows, unary_out, out_sem)
    leaving.start()
    sub = sublane()

    def feature_row(y):
        row = y + REACH
        own = all_turned[REACH, row]
        mate = jnp.concatenate(
            [own[3 * PAD :], own[2 * PAD : 3 * PAD], own[PAD : 2 * PAD], own[0:PAD]], axis=0
        )
        total = None
        whole = None
        for sign in (1, -1):
            for group in range(REACH):
                parts = []
                places = []
                for s in range(8):
                    a, b = (s - REACH, group + 1) if s < 7 else (group + 1, 0)
                    a, b = sign * a, sign * b
                    places.append((a, b))
                    parts.append(fold(mate * all_turned[b + REACH, row + a]))
                if sign > 0:
                    weight = kern[row, pl.ds(8 * group, 8), 0:128]
                else:
                    weight = kern_back[row - (group + 1), pl.ds(8 * group, 8), :]
                    for s in range(7):
                        weight = jnp.where(
                            sub == s, kern_back[row - (s - REACH), pl.ds(8 * group, 8), :], weight
                        )
                weight = weight * merge(parts)
                whole = weight if whole is None else whole + weight
                at = 8 * (group + (0 if sign > 0 else REACH))
                weights[y, pl.ds(at, 8), :] = weight
                for s, (a, b) in enumerate(places):
                    term = weights[y, pl.ds(at + s, 1), :] * feat_turned[b + REACH, row + a]
                    total = term if total is None else total + term
        whole = jnp.sum(whole, axis=0, keepdims=True)
        total = total - whole * feat_turned[REACH, row]
        feat_out[pl.ds(y, channels, stride=height), :] = total * (1.0 / math.sqrt(channels))

    each_row(0, height, 1, feature_row)
    leaving.wait()


def finish(feat, kern, prob0, prob1, grad1, grad0, partial, classes):
    near, channels, _ = feat.shape
    height = partial.shape[0]

    def room(*dims):
        return pltpu.VMEM(dims, jnp.float32)

    return pl.pallas_call(
        finish_kernel,
        out_shape=(
            jax.ShapeDtypeStruct((classes * height, 128), jnp.float32),
            jax.ShapeDtypeStruct((channels * height, 128), jnp.float32),
        ),
        in_specs=[ANY] * 7,
        out_specs=(ANY, VMEM),
        scratch_shapes=[
            *map(like, (feat, kern, prob0, prob1, grad1, grad0, partial)),
            room(2 * REACH + 1, near, channels, 128),
            room(2 * REACH + 1, near, 4 * PAD, 128),
            room(near, PAD, 128),
            room(height, 6 * 8, 128),
            pltpu.VMEM((256, (2 * REACH + 1) * 128), jnp.bfloat16),
            room(classes * height, 128),
            pltpu.SemaphoreType.DMA((7,)),
            pltpu.SemaphoreType.DMA,
        ],
        compiler_params=params(56),
        cost_estimate=pl.CostEstimate(flops=200_000_000, bytes_accessed=8_000_000, transcendentals=0),
        name="finish",
    )(feat, kern, prob0, prob1, grad1, grad0, partial)


def on_device(unary, features, compat, grad_output):
    classes, height, width = unary.shape
    n_rows, n_cols = lax.axis_size("rows"), lax.axis_size("cols")

    below = [pair for i in range(0, n_rows, 2) for pair in ((i, i + 1), (i + 1, i))]
    above = [
        pair
        for i in range(1, n_rows, 2)
        for pair in ((i, (i + 1) % n_rows), ((i + 1) % n_rows, i))
    ]
    forward = [(i, i + 1) for i in range(n_cols - 1)]
    backward = [(i + 1, i) for i in range(n_cols - 1)]
    centre, left, right, inner_feat, inner_rest, outer_feat, outer_rest = pack(
        features, unary, grad_output
    )
    inner_feat = lax.ppermute(inner_feat, "rows", below)
    inner_rest = lax.ppermute(inner_rest, "rows", below)
    outer_feat = lax.ppermute(outer_feat, "rows", above)
    outer_rest = lax.ppermute(outer_rest, "rows", above)
    from_left = lax.ppermute(right, "cols", forward)
    from_right = lax.ppermute(left, "cols", backward)
    inner_corner, outer_corner = corners(from_left, from_right, outer_feat)
    outer_corner = lax.ppermute(outer_corner, "rows", above)
    inner_corner = lax.ppermute(inner_corner, "rows", below)
    main = main_affinities(centre, from_left, from_right, inner_feat, outer_feat)
    received = (
        from_left, from_right, inner_feat, inner_rest, outer_feat, outer_rest, inner_corner,
        outer_corner,
    )

    devices = n_rows * n_cols
    *fields, partial, share = iterate(
        compat, centre, received, main, devices
    )
    shares = lax.all_to_all(share, ("rows", "cols"), 0, 0)
    unary_grad, feature_grad = finish(*fields, partial, classes)
    summed = jnp.sum(shares, axis=0) / math.sqrt(n_rows * height * n_cols * width)
    compat_grad = jnp.concatenate(
        [summed[:, 0:PAD], summed[:, 32 : 32 + PAD], summed[:, 64 : 64 + PAD]], axis=0
    )[:classes, :classes]
    return (
        unary_grad.reshape(unary.shape),
        feature_grad.reshape(features.shape),
        compat_grad,
    )


def solution(mesh):
    placed = (P(None, "rows", "cols"), P(None, "rows", "cols"), P(), P(None, "rows", "cols"))
    return jax.shard_map(
        on_device,
        mesh=mesh,
        in_specs=placed,
        out_specs=(P(None, "rows", "cols"), P(None, "rows", "cols"), P()),
        check_vma=False,
    )
```

```python
import functools
import math

import jax
import jax.numpy as jnp
from jax import lax
from jax.experimental import pallas as pl
from jax.experimental.pallas import tpu as pltpu
from jax.sharding import PartitionSpec as P

ITERS = 2
REACH = 3
HALO = 2 * ITERS * REACH
GROUPS = 4
STRIP = 16
PAD = 24
DEEP = 32
LOW = -1e30
VMEM = pl.BlockSpec(memory_space=pltpu.VMEM)
ANY = pl.BlockSpec(memory_space=pl.ANY)


def params(mebibytes):
    return pltpu.CompilerParams(vmem_limit_bytes=mebibytes * 1024 * 1024)


def fetch(pairs, sems):
    copies = [
        pltpu.make_async_copy(source, target, sems.at[i])
        for i, (source, target) in enumerate(pairs)
    ]
    for copy in copies:
        copy.start()
    return copies


def wait(copies):
    for copy in copies:
        copy.wait()


def like(array):
    return pltpu.VMEM(array.shape, array.dtype)


def position(height):
    row, col = lax.axis_index("rows"), lax.axis_index("cols")
    return (
        row % 2 == 0,
        col > 0,
        col < lax.axis_size("cols") - 1,
        row * height - HALO,
        lax.axis_size("rows") * height,
    )


def sublane(width=128):
    return lax.broadcasted_iota(jnp.int32, (8, width), 0)


def lane(width=128):
    return lax.broadcasted_iota(jnp.int32, (1, width), 1)


def shifted(value, step):
    low, high = value[:, 0:128], value[:, 128:256]
    column = lane() + step
    here = (column >= 0) & (column < 128)
    low = pltpu.roll(low, (-step) % 128, axis=1)
    high = pltpu.roll(high, (-step) % 128, axis=1)
    return jnp.concatenate([jnp.where(here, low, high), jnp.where(here, high, low)], axis=1)


def turns(steps, width):
    source = lax.broadcasted_iota(jnp.int32, (256, width), 0)
    target = lax.broadcasted_iota(jnp.int32, (256, width), 1)
    return jnp.concatenate(
        [(source == (target + step) % 256).astype(jnp.bfloat16) for step in steps], axis=1
    )


def each_row(low, high, step, body):
    def some(turn, carry):
        for at in range(step):
            body(low + turn * step + at)
        return carry

    turns = (high - low) // step
    if turns > 1:
        lax.fori_loop(0, turns, some, 0)
    else:
        turns = 0
    for y in range(low + turns * step, high):
        body(y)


def split(value):
    parts = []
    for _ in range(2):
        part = value.astype(jnp.bfloat16)
        parts.append(part)
        value = value - part.astype(jnp.float32)
    return parts + [value.astype(jnp.bfloat16)]


def deep(value):
    return jnp.concatenate([value, jnp.zeros((DEEP - PAD, value.shape[1]), value.dtype)], axis=0)


def apply(square, value):
    high, middle, low = [part.astype(jnp.float32) for part in split(value)]
    stack = jnp.concatenate([high, middle, high, low, middle, high], axis=0)
    return jnp.dot(square, stack.astype(jnp.bfloat16), preferred_element_type=jnp.float32)[0:PAD]


def spread(square):
    high, middle, low = [part.astype(jnp.float32) for part in split(square[0:DEEP])]
    wide = [jnp.zeros((DEEP, 128), jnp.float32)] * 2
    for i, part in enumerate((high, high, middle, high, middle, low)):
        start = PAD * i
        moved = pltpu.roll(part, start % 128, axis=1)
        for tile in range(2):
            low_lane = start - 128 * tile
            if low_lane < 128 and low_lane + PAD > 0:
                here = (lane() >= low_lane) & (lane() < low_lane + PAD)
                wide[tile] = jnp.where(here, moved, wide[tile])
    return jnp.concatenate(wide, axis=1)[:, 0 : 6 * PAD].astype(jnp.bfloat16)


def outer(left, right):
    left = jnp.concatenate(split(deep(left)), axis=0)
    right = jnp.concatenate(split(deep(right)), axis=0)
    full = lax.dot_general(
        left, right, (((1,), (1,)), ((), ())), preferred_element_type=jnp.float32
    )
    total = None
    for i in range(3):
        for j in range(3 - i):
            term = full[i * DEEP : i * DEEP + PAD, j * DEEP : j * DEEP + PAD]
            total = term if total is None else total + term
    return total


def merge(parts):
    row = sublane(parts[0].shape[-1])
    bit = 1
    while len(parts) > 1:
        low = (row & bit) == 0
        parts = [
            jnp.where(low, first, second)
            + pltpu.roll(jnp.where(low, second, first), 8 - bit, axis=0)
            for first, second in zip(parts[::2], parts[1::2])
        ]
        bit *= 2
    return parts[0]


def fold(value):
    total = value[0:8]
    for start in range(8, value.shape[0], 8):
        total = total + value[start : start + 8]
    return total


def pack_kernel(
    feat, unary, grad, centre, left, right, inner_feat, inner_rest, outer_feat, outer_rest, wide,
    wide_unary, wide_grad,
):
    channels, height, _ = feat.shape
    classes = unary.shape[0] // height
    wide[...] = feat[...].astype(jnp.float32).reshape(channels * height, 128) * (
        1.0 / math.sqrt(channels)
    )
    for source, target, fill in ((unary, wide_unary, LOW), (grad, wide_grad, 0.0)):
        size = classes * height
        target[pl.ds(0, size)] = source[...]
        target[pl.ds(size, PAD * height - size)] = jnp.full(
            (PAD * height - size, 128), fill, jnp.float32
        )
    side = lane()
    for slot in range(height // 8):
        ends = [None, None]
        for i in range(8):
            y = 8 * slot + i
            rows = jnp.concatenate(
                [
                    wide[pl.ds(y, channels, stride=height), :],
                    wide_unary[pl.ds(y, PAD, stride=height), :],
                    wide_grad[pl.ds(y, PAD, stride=height), :],
                ],
                axis=0,
            )
            centre[y] = rows
            at = i * STRIP
            here = (side >= at) & (side < at + STRIP)
            for end, shift in ((0, at), (1, (at + STRIP) % 128)):
                moved = pltpu.roll(rows, shift, axis=1)
                ends[end] = moved if i == 0 else jnp.where(here, moved, ends[end])
        left[slot], right[slot] = ends
    even = position(height)[0]
    low = height - HALO
    for feat_out, rest_out, top in (
        (inner_feat, inner_rest, jnp.logical_not(even)),
        (outer_feat, outer_rest, even),
    ):
        base = jnp.where(top, 0, low)
        grad_base = jnp.where(top, 0, height - HALO // 2)
        for i in range(HALO):
            feat_out[i] = centre[base + i, 0:channels].astype(jnp.bfloat16)
            rest_out[i] = centre[base + i, channels : channels + PAD]
        for i in range(HALO // 2):
            rest_out[HALO + i] = centre[grad_base + i, channels + PAD :]


def pack(feat, unary, grad):
    channels, height, _ = feat.shape
    depth = channels + 2 * PAD

    def shape(*dims, dtype=jnp.float32):
        return jax.ShapeDtypeStruct(dims, dtype)

    return pl.pallas_call(
        pack_kernel,
        out_shape=(
            shape(height, depth, 128),
            shape(height // 8, depth, 128),
            shape(height // 8, depth, 128),
            shape(HALO, channels, 128, dtype=jnp.bfloat16),
            shape(HALO + HALO // 2, PAD, 128),
            shape(HALO, channels, 128, dtype=jnp.bfloat16),
            shape(HALO + HALO // 2, PAD, 128),
        ),
        in_specs=[VMEM] * 3,
        out_specs=(VMEM,) * 7,
        scratch_shapes=[
            pltpu.VMEM((count * height, 128), jnp.float32) for count in (channels, PAD, PAD)
        ],
        compiler_params=params(56),
        name="pack",
    )(feat, unary.reshape(-1, 128), grad.reshape(-1, 128))


def corner_kernel(left_in, right_in, _, inner, outer, left, right, sems):
    wait(fetch([(left_in, left), (right_in, right)], sems))
    depth = left.shape[1]
    short = depth - PAD
    even = position(8 * left.shape[0])[0]
    side = lane()
    for out, top in ((inner, jnp.logical_not(even)), (outer, even)):
        whole = jnp.where(top, 0, 1)
        out[pl.ds(0, depth)] = left[whole]
        out[pl.ds(depth, depth)] = right[whole]
        mine = (side < 64) == top
        out[pl.ds(2 * depth, short)] = jnp.where(
            mine,
            left[1 - whole, 0:short],
            pltpu.roll(right[1 - whole, 0:short], 64, axis=1),
        )


def corners(left, right, earlier):
    depth = left.shape[1]
    out = jax.ShapeDtypeStruct((3 * depth - PAD, 128), jnp.float32)
    return pl.pallas_call(
        corner_kernel,
        out_shape=(out, out),
        in_specs=[ANY] * 3,
        out_specs=(VMEM,) * 2,
        scratch_shapes=[like(left), like(right), pltpu.SemaphoreType.DMA((2,))],
        compiler_params=params(4),
        name="corners",
    )(left, right, earlier)


def sizes(here, there, size, size_there):
    rows = here.shape[0]

    def body(row):
        value = here[row]
        size[row] = fold(value * value) * 0.5
        for group in range(REACH):
            value = there[group, row]
            size_there[group, row] = fold(value * value) * 0.5

    each_row(0, rows, rows // 2, body)


def affinities(here, there, size, size_there, out):
    sub = sublane()

    def two(turn):
        y = 2 * turn
        mine = [here[y + i + REACH] for i in range(2)]
        mine_size = [size[y + i + REACH] for i in range(2)]
        for group in range(REACH):
            parts = [[], []]
            for row in range(-REACH, REACH + 2):
                other = there[group, y + row + REACH]
                other_size = size_there[group, y + row + REACH]
                for i in range(2):
                    if -REACH <= row - i <= REACH:
                        parts[i].append(fold(mine[i] * other) - (mine_size[i] + other_size))
            step_a = jnp.where(sub == 7, group + 1, sub - REACH)
            step_b = jnp.where(sub == 7, 0, group + 1)
            far = (step_a * step_a + step_b * step_b).astype(jnp.float32)
            for i in range(2):
                below = y + i + group + 1 + REACH
                parts[i].append(fold(mine[i] * here[below]) - (mine_size[i] + size[below]))
                out[y + i, pl.ds(8 * group, 8), :] = jnp.exp(
                    merge(parts[i]) - far * (1.0 / (2.0 * REACH * REACH))
                )

    each_row(0, out.shape[0] // 2, 1, two)


def strip_edge(left, left_at, right, right_at):
    right = pltpu.roll(right, (128 - right_at) % 128, axis=1)
    left = pltpu.roll(left, (128 - STRIP - left_at) % 128, axis=1)
    return jnp.where(lane() < 64, right, left)


def main_kernel(
    centre_in, inner_in, outer_in, kern_out,
    centre, inner, outer, feat, short, turned, size, size_turned, turner, sems,
):
    coming = fetch([(inner_in, inner), (outer_in, outer), (centre_in, centre)], sems)
    height, channels = centre.shape[0], feat.shape[1]
    tall = feat.shape[0]
    turner[...] = turns(range(1, REACH + 1), 128)[0:128]
    for at in (0, tall - REACH):
        feat[pl.ds(at, REACH)] = jnp.zeros((REACH, channels, 128), jnp.float32)
        short[pl.ds(at, REACH)] = jnp.zeros((REACH, channels, 128), jnp.bfloat16)
    even = position(height)[0]
    wait(coming)
    above = jnp.where(even, REACH + HALO + height, REACH)
    for source, base in ((inner, above), (outer, tall - HALO - above)):
        for i in range(HALO):
            feat[base + i] = source[i].astype(jnp.float32)
            short[base + i] = source[i]
    for y in range(height):
        row = y + HALO + REACH
        value = centre[y, 0:channels]
        feat[row] = value
        short[row] = value.astype(jnp.bfloat16)
    moved = jnp.dot(
        short[...].reshape(tall * channels, 128), turner[...], preferred_element_type=jnp.float32
    )
    for group in range(REACH):
        turned[group] = moved[:, 128 * group : 128 * group + 128].reshape(tall, channels, 128)
    sizes(feat, turned, size, size_turned)
    affinities(feat, turned, size, size_turned, kern_out)


def main_affinities(centre, inner, outer):
    height, depth, _ = centre.shape
    channels = depth - 2 * PAD
    rows = height + 2 * HALO
    tall = rows + 2 * REACH
    inputs = (centre, inner, outer)

    def room(*dims, dtype=jnp.float32):
        return pltpu.VMEM(dims, dtype)

    return pl.pallas_call(
        main_kernel,
        out_shape=jax.ShapeDtypeStruct((rows, PAD, 128), jnp.float32),
        in_specs=[ANY] * 3,
        out_specs=VMEM,
        scratch_shapes=[
            *map(like, inputs),
            room(tall, channels, 128),
            room(tall, channels, 128, dtype=jnp.bfloat16),
            room(REACH, tall, channels, 128),
            room(tall, 8, 128),
            room(REACH, tall, 8, 128),
            room(128, REACH * 128, dtype=jnp.bfloat16),
            pltpu.SemaphoreType.DMA((3,)),
        ],
        compiler_params=params(16),
        cost_estimate=pl.CostEstimate(
            flops=200_000_000, bytes_accessed=8_000_000, transcendentals=0
        ),
        name="main_affinities",
    )(*inputs)


def side_turns():
    target = lax.broadcasted_iota(jnp.int32, (256, 128), 1)
    source = lax.broadcasted_iota(jnp.int32, (256, 128), 0)
    place = target % 32
    column = jnp.where(place < 12, place - 12, jnp.where(place < 24, 116 + place, 101 + place))
    blocks = []
    for b in range(REACH + 1):
        hit = source == (column + b + 256) % 256
        blocks.append(
            jnp.concatenate(
                [(hit & (target // 32 == j)).astype(jnp.bfloat16) for j in range(GROUPS)], axis=0
            )
        )
    return jnp.concatenate(blocks, axis=1)


def pass_row(y, kern, field, turned):
    def weight(row, at):
        return kern[row, pl.ds(at, 1), :]

    total = None

    def plus(total, term):
        return term if total is None else total + term

    for group in range(REACH):
        step = group + 1
        back = None
        for a in range(-REACH, REACH + 1):
            at = 8 * group + a + REACH
            total = plus(total, weight(y, at) * turned[group, y + a])
            back = plus(back, weight(y - a, at) * field[y - a])
        total = total + weight(y, 8 * group + 7) * field[y + step]
        total = total + weight(y - step, 8 * group + 7) * field[y - step]
        total = total + shifted(back, -step)
    return total


def softmax(value):
    top = jnp.max(value, axis=0, keepdims=True)
    power = jnp.exp(value - top)
    return power * (1.0 / jnp.sum(power, axis=0, keepdims=True))


def field_kernel(
    square_in, centre_in, from_left_in, from_right_in, inner_feat_in, inner_rest_in,
    outer_feat_in, outer_rest_in, inner_corner_in, outer_corner_in, main_in,
    feat_out, kern_out, prob0_out, prob1_out, grad1_out, grad0_out, share,
    centre, from_left, from_right, inner_feat, inner_rest, outer_feat, outer_rest, inner_corner,
    outer_corner, main, short, side_feat, side_turned, side_size, side_size_turned, side_kern,
    kern, unary, grad, prob0,
    prob1, grad1, grad0, turned, message0, message1, logit1, logit0, side_turner, square, compat, compat_t,
    in_sems, out_sems,
):
    coming = fetch(
        [
            (centre_in, centre), (from_left_in, from_left), (from_right_in, from_right),
            (inner_feat_in, inner_feat), (inner_rest_in, inner_rest),
            (outer_feat_in, outer_feat), (outer_rest_in, outer_rest),
            (inner_corner_in, inner_corner), (outer_corner_in, outer_corner), (main_in, main),
        ],
        in_sems,
    )
    height = centre.shape[0]
    going = []

    def send(source, target, low):
        copy = pltpu.make_async_copy(
            source.at[pl.ds(low, target.shape[0])], target, out_sems.at[len(going)]
        )
        copy.start()
        going.append(copy)

    rows = height + 2 * HALO
    channels = short.shape[1]
    side = lane()
    side_turner[...] = side_turns()
    square[...] = jnp.zeros_like(square)
    square[0 : square_in.shape[0], 0 : square_in.shape[1]] = square_in[...]
    compat[...] = spread(square[...])
    compat_t[...] = spread(square[...].T)

    for at in (0, rows + REACH):
        short[pl.ds(at, REACH)] = jnp.zeros((REACH, channels, 256), jnp.bfloat16)

    def put(row, own, left, left_at, right, right_at):
        edge = strip_edge(left, left_at, right, right_at)
        for value, cols in ((own, slice(0, 128)), (edge, slice(128, 256))):
            short[row + REACH, :, cols] = value[0:channels].astype(jnp.bfloat16)
            unary[row, :, cols] = value[channels : channels + PAD]
            if value.shape[0] > channels + PAD:
                grad[row, :, cols] = value[channels + PAD :]

    wait(coming[:3])
    for y in range(height):
        at = (y % 8) * STRIP
        put(HALO + y, centre[y], from_left[y // 8], at, from_right[y // 8], at)

    wait(coming[3:])
    depth = channels + 2 * PAD
    slim = channels + PAD
    near = HALO // 2

    def edge_row(feat_in, rest_in, i, top):
        parts = [feat_in[i].astype(jnp.float32), rest_in[i]]
        row = i if top else i - near
        if 0 <= row < near:
            parts.append(rest_in[HALO + row])
        return jnp.concatenate(parts, axis=0)

    def put_rows(edge_rows, corner, top):
        base = HALO + height if top else 0
        half = HALO - 8
        for i in range(HALO):
            at = (i if top else i - half) * STRIP
            if 0 <= at < 128:
                left, right = corner[pl.ds(0, depth)], corner[pl.ds(depth, depth)]
                left_at = right_at = at
            else:
                left = right = corner[pl.ds(2 * depth, slim)]
                left_at = (i - 8) * STRIP if top else 64 + i * STRIP
                right_at = (left_at + 64) % 128
            own = edge_rows(i, top)
            size = min(own.shape[0], left.shape[0])
            put(base + i, own[0:size], left[0:size], left_at, right[0:size], right_at)

    even, has_left, has_right, first_row, all_rows = position(height)
    for edge_rows, corner, below in (
        (functools.partial(edge_row, inner_feat, inner_rest), inner_corner, even),
        (functools.partial(edge_row, outer_feat, outer_rest), outer_corner, jnp.logical_not(even)),
    ):
        pl.when(below)(functools.partial(put_rows, edge_rows, corner, True))
        pl.when(jnp.logical_not(below))(functools.partial(put_rows, edge_rows, corner, False))

    wide_lane = lane(256)
    inside_lane = (
        (wide_lane < 128)
        | ((wide_lane < 192) & has_right)
        | ((wide_lane >= 192) & has_left)
    )

    def inside(y):
        row = first_row + y
        return inside_lane & (row >= 0) & (row < all_rows)

    send(short, feat_out, HALO)
    slots = rows // GROUPS
    tall = slots + 2 * REACH
    stacked = jnp.concatenate(
        [
            jnp.concatenate([short[slots * j + k] for j in range(GROUPS)], axis=1)
            for k in range(tall)
        ],
        axis=0,
    )
    moved = jnp.dot(stacked, side_turner[...], preferred_element_type=jnp.float32)
    side_feat[...] = moved[:, 0:128].reshape(tall, channels, 128)
    for group in range(REACH):
        start = 128 * group + 128
        side_turned[group] = moved[:, start : start + 128].reshape(tall, channels, 128)
    sizes(side_feat, side_turned, side_size, side_size_turned)
    affinities(side_feat, side_turned, side_size, side_size_turned, side_kern)
    for j in range(GROUPS):
        for k in range(slots):
            y, value = slots * j + k, side_kern[k]
            kern[y, :, 128:256] = pltpu.roll(value, (116 - 32 * j) % 128, axis=1)
            last = pltpu.roll(value, (101 - 32 * j) % 128, axis=1)
            kern[y, :, 0:128] = jnp.where(side < 128 - REACH, main[y], last)
    send(kern, kern_out, HALO - REACH)

    def put_field(field, y, value):
        field[y] = value
        for group in range(REACH):
            turned[group, y] = shifted(value, group + 1)

    def start(y):
        put_field(prob0, y, jnp.where(inside(y), softmax(unary[y]), 0.0))

    each_row(0, rows, rows // 2, start)
    send(prob0, prob0_out, HALO - REACH)

    def run_pass(field, out, low, high):
        def body(y):
            out[y] = pass_row(y, kern, field, turned)

        each_row(low, high, 2, body)

    run_pass(prob0, message0, REACH, rows - REACH)

    def mix(y):
        value = softmax(unary[y] - apply(compat[...], message0[y]))
        put_field(prob1, y, jnp.where(inside(y), value, 0.0))

    each_row(REACH, rows - REACH, rows, mix)
    send(prob1, prob1_out, HALO - REACH)
    run_pass(prob1, message1, 2 * REACH, rows - 2 * REACH)

    def back1(y):
        prob = softmax(unary[y] - apply(compat[...], message1[y]))
        cot = grad[y]
        change = prob * (cot - jnp.sum(cot * prob, axis=0, keepdims=True))
        logit1[y] = change
        put_field(grad1, y, jnp.where(inside(y), -apply(compat_t[...], change), 0.0))

    each_row(2 * REACH, rows - 2 * REACH, rows, back1)
    def share_of(change, message):
        block = range(HALO, HALO + height)
        left = jnp.concatenate([change[y, :, 0:128] for y in block], axis=1)
        right = jnp.concatenate([message[y, :, 0:128] for y in block], axis=1)
        return outer(left, right)

    total = -share_of(logit1, message1)
    run_pass(grad1, message1, 3 * REACH, rows - 3 * REACH)

    def back0(y):
        prob = prob1[y]
        cot = message1[y]
        change = prob * (cot - jnp.sum(cot * prob, axis=0, keepdims=True))
        logit0[y] = change
        grad0[y] = jnp.where(inside(y), -apply(compat_t[...], change), 0.0)

    each_row(3 * REACH, rows - 3 * REACH, rows, back0)
    total = total - share_of(logit0, message0)

    total = jnp.concatenate([total, jnp.zeros((PAD, 128 - PAD), jnp.float32)], axis=1)
    packed = (
        total[0:8]
        + pltpu.roll(total[8:16], 32, axis=1)
        + pltpu.roll(total[16:24], 64, axis=1)
    )
    for slot in range(share.shape[0]):
        share[slot] = packed

    middle = (side >= 32) & (side < 96)

    def add_logit(y):
        at = y + HALO
        value = logit0[at, :, 0:128] + logit1[at, :, 0:128]
        for field, shift in ((grad1, 32), (grad0, 96)):
            field[at, :, 128:256] = jnp.where(
                middle, pltpu.roll(value, shift, axis=1), field[at, :, 128:256]
            )

    each_row(0, height, height, add_logit)
    send(grad1, grad1_out, HALO - REACH)
    send(grad0, grad0_out, HALO - REACH)
    wait(going)


def iterate(compat, centre, received, main, devices):
    height, depth, _ = centre.shape
    channels = depth - 2 * PAD
    rows = height + 2 * HALO
    tall = rows + 2 * REACH
    near = height + 2 * REACH
    slots = rows // GROUPS

    def shape(*dims):
        return jax.ShapeDtypeStruct(dims, jnp.float32)

    def room(*dims):
        return pltpu.VMEM(dims, jnp.float32)

    return pl.pallas_call(
        field_kernel,
        out_shape=(
            jax.ShapeDtypeStruct((near, channels, 256), jnp.bfloat16),
            shape(near, PAD, 256),
            shape(near, PAD, 256),
            shape(near, PAD, 256),
            shape(near, PAD, 256),
            shape(near, PAD, 256),
            shape(devices, 8, 128),
        ),
        in_specs=[VMEM] + [ANY] * (2 + len(received)),
        out_specs=(ANY,) * 6 + (VMEM,),
        scratch_shapes=[
            like(centre),
            *map(like, received),
            like(main),
            pltpu.VMEM((tall, channels, 256), jnp.bfloat16),
            room(slots + 2 * REACH, channels, 128),
            room(REACH, slots + 2 * REACH, channels, 128),
            room(slots + 2 * REACH, 8, 128),
            room(REACH, slots + 2 * REACH, 8, 128),
            room(slots, PAD, 128),
            *[room(rows, PAD, 256)] * 7,
            room(REACH, rows, PAD, 256),
            *[room(rows, PAD, 256)] * 4,
            pltpu.VMEM((GROUPS * 256, (REACH + 1) * 128), jnp.bfloat16),
            room(128, 128),
            pltpu.VMEM((DEEP, 6 * PAD), jnp.bfloat16),
            pltpu.VMEM((DEEP, 6 * PAD), jnp.bfloat16),
            pltpu.SemaphoreType.DMA((2 + len(received),)),
            pltpu.SemaphoreType.DMA((6,)),
        ],
        compiler_params=params(28),
        name="iterate",
    )(compat, centre, *received, main)


def finish_kernel(
    feat_in, kern_in, prob0_in, prob1_in, grad1_in, grad0_in, unary_out, feat_out,
    feat, kern, prob0, prob1, grad1, grad0, feat_turned, all_turned, kern_back, weights,
    turner, unary_rows, in_sems, out_sem,
):
    coming = fetch(
        [
            (feat_in, feat), (kern_in, kern), (prob0_in, prob0), (prob1_in, prob1),
            (grad1_in, grad1), (grad0_in, grad0),
        ],
        in_sems,
    )
    near = feat.shape[0]
    height = near - 2 * REACH
    channels = feat.shape[1]
    classes = unary_out.shape[0] // height
    steps = range(-REACH, REACH + 1)

    turner[...] = turns(steps, 128)
    column = lane()

    def moved(main, edge, b):
        if b == 0:
            return main
        mixed = jnp.where((column < b) if b > 0 else (column >= 128 + b), edge, main)
        return pltpu.roll(mixed, (-b) % 128, axis=1)

    wait(coming[:1])
    full = jnp.dot(
        feat[...].reshape(near * channels, 256), turner[...], preferred_element_type=jnp.float32
    )
    for place in range(len(steps)):
        feat_turned[place] = full[:, 128 * place : 128 * place + 128].reshape(near, channels, 128)

    wait(coming[1:])

    def prepare(row):
        for place, field in enumerate((prob0, prob1, grad1, grad0)):
            main, edge = field[row, :, 0:128], field[row, :, 128:256]
            for b in steps:
                all_turned[b + REACH, row, pl.ds(place * PAD, PAD), :] = moved(main, edge, b)
        for group in range(REACH):
            rows = pl.ds(8 * group, 8)
            main, edge = kern[row, rows, 0:128], kern[row, rows, 128:256]
            kern_back[row, rows, :] = jnp.where(
                sublane() == 7, main, moved(main, edge, -(group + 1))
            )

    each_row(0, near, near, prepare)

    def pass_centre(y):
        total = jnp.zeros((PAD, 128), jnp.float32)
        last = pl.ds(3 * PAD, PAD)
        for group in range(REACH):
            step = group + 1
            back = [jnp.zeros((PAD, 128), jnp.float32)] * 2
            for a in range(-REACH, REACH + 1):
                one = pl.ds(8 * group + a + REACH, 1)
                total = total + kern[y, one, 0:128] * all_turned[step + REACH, y + a, last, :]
                for tile in range(2):
                    cols = slice(128 * tile, 128 * tile + 128)
                    back[tile] = back[tile] + kern[y - a, one, cols] * grad0[y - a, :, cols]
            one = pl.ds(8 * group + 7, 1)
            total = total + kern[y, one, 0:128] * grad0[y + step, :, 0:128]
            total = total + kern[y - step, one, 0:128] * grad0[y - step, :, 0:128]
            total = total + moved(back[0], back[1], -step)
        return total

    def unary_row(y):
        cot = pass_centre(y + REACH)
        prob = prob0[y + REACH, :, 0:128]
        row = y + REACH
        partial = jnp.where(
            column < 64,
            pltpu.roll(grad1[row, :, 128:256], 96, axis=1),
            pltpu.roll(grad0[row, :, 128:256], 32, axis=1),
        )
        value = partial + prob * (cot - jnp.sum(cot * prob, axis=0, keepdims=True))
        unary_rows[pl.ds(y, PAD, stride=height), :] = value

    each_row(0, height, 4, unary_row)
    leaving = pltpu.make_async_copy(
        unary_rows.at[pl.ds(0, classes * height)], unary_out, out_sem
    )
    leaving.start()
    sub = sublane()

    def feature_row(y):
        row = y + REACH
        own = all_turned[REACH, row]
        mate = jnp.concatenate(
            [own[3 * PAD :], own[2 * PAD : 3 * PAD], own[PAD : 2 * PAD], own[0:PAD]], axis=0
        )
        total = None
        whole = None
        for sign in (1, -1):
            for group in range(REACH):
                parts = []
                places = []
                for s in range(8):
                    a, b = (s - REACH, group + 1) if s < 7 else (group + 1, 0)
                    a, b = sign * a, sign * b
                    places.append((a, b))
                    parts.append(fold(mate * all_turned[b + REACH, row + a]))
                if sign > 0:
                    weight = kern[row, pl.ds(8 * group, 8), 0:128]
                else:
                    weight = kern_back[row - (group + 1), pl.ds(8 * group, 8), :]
                    for s in range(7):
                        weight = jnp.where(
                            sub == s, kern_back[row - (s - REACH), pl.ds(8 * group, 8), :], weight
                        )
                weight = weight * merge(parts)
                whole = weight if whole is None else whole + weight
                at = 8 * (group + (0 if sign > 0 else REACH))
                weights[y, pl.ds(at, 8), :] = weight
                for s, (a, b) in enumerate(places):
                    term = weights[y, pl.ds(at + s, 1), :] * feat_turned[b + REACH, row + a]
                    total = term if total is None else total + term
        whole = jnp.sum(whole, axis=0, keepdims=True)
        total = total - whole * feat_turned[REACH, row]
        feat_out[pl.ds(y, channels, stride=height), :] = total * (1.0 / math.sqrt(channels))

    each_row(0, height, 1, feature_row)
    leaving.wait()


def finish(feat, kern, prob0, prob1, grad1, grad0, classes):
    near, channels, _ = feat.shape
    height = near - 2 * REACH

    def room(*dims):
        return pltpu.VMEM(dims, jnp.float32)

    return pl.pallas_call(
        finish_kernel,
        out_shape=(
            jax.ShapeDtypeStruct((classes * height, 128), jnp.float32),
            jax.ShapeDtypeStruct((channels * height, 128), jnp.float32),
        ),
        in_specs=[ANY] * 6,
        out_specs=(ANY, VMEM),
        scratch_shapes=[
            *map(like, (feat, kern, prob0, prob1, grad1, grad0)),
            room(2 * REACH + 1, near, channels, 128),
            room(2 * REACH + 1, near, 4 * PAD, 128),
            room(near, PAD, 128),
            room(height, 6 * 8, 128),
            pltpu.VMEM((256, (2 * REACH + 1) * 128), jnp.bfloat16),
            room(PAD * height, 128),
            pltpu.SemaphoreType.DMA((6,)),
            pltpu.SemaphoreType.DMA,
        ],
        compiler_params=params(24),
        cost_estimate=pl.CostEstimate(flops=200_000_000, bytes_accessed=8_000_000, transcendentals=0),
        name="finish",
    )(feat, kern, prob0, prob1, grad1, grad0)


def on_device(unary, features, compat, grad_output):
    classes, height, width = unary.shape
    n_rows, n_cols = lax.axis_size("rows"), lax.axis_size("cols")

    below = [pair for i in range(0, n_rows, 2) for pair in ((i, i + 1), (i + 1, i))]
    above = [
        pair
        for i in range(1, n_rows, 2)
        for pair in ((i, (i + 1) % n_rows), ((i + 1) % n_rows, i))
    ]
    forward = [(i, i + 1) for i in range(n_cols - 1)]
    backward = [(i + 1, i) for i in range(n_cols - 1)]
    centre, left, right, inner_feat, inner_rest, outer_feat, outer_rest = pack(
        features, unary, grad_output
    )
    inner_feat = lax.ppermute(inner_feat, "rows", below)
    inner_rest = lax.ppermute(inner_rest, "rows", below)
    outer_feat = lax.ppermute(outer_feat, "rows", above)
    outer_rest = lax.ppermute(outer_rest, "rows", above)
    from_left = lax.ppermute(right, "cols", forward)
    from_right = lax.ppermute(left, "cols", backward)
    inner_corner, outer_corner = corners(from_left, from_right, outer_feat)
    outer_corner = lax.ppermute(outer_corner, "rows", above)
    inner_corner = lax.ppermute(inner_corner, "rows", below)
    main = main_affinities(centre, inner_feat, outer_feat)
    received = (
        from_left, from_right, inner_feat, inner_rest, outer_feat, outer_rest, inner_corner,
        outer_corner,
    )

    devices = n_rows * n_cols
    *fields, share = iterate(
        compat, centre, received, main, devices
    )
    shares = lax.all_to_all(share, ("rows", "cols"), 0, 0)
    unary_grad, feature_grad = finish(*fields, classes)
    summed = jnp.sum(shares, axis=0) / math.sqrt(n_rows * height * n_cols * width)
    compat_grad = jnp.concatenate(
        [summed[:, 0:PAD], summed[:, 32 : 32 + PAD], summed[:, 64 : 64 + PAD]], axis=0
    )[:classes, :classes]
    return (
        unary_grad.reshape(unary.shape),
        feature_grad.reshape(features.shape),
        compat_grad,
    )


def solution(mesh):
    placed = (P(None, "rows", "cols"), P(None, "rows", "cols"), P(), P(None, "rows", "cols"))
    return jax.shard_map(
        on_device,
        mesh=mesh,
        in_specs=placed,
        out_specs=(P(None, "rows", "cols"), P(None, "rows", "cols"), P()),
        check_vma=False,
    )
```

```python
import functools
import math

import jax
import jax.numpy as jnp
from jax import lax
from jax.experimental import pallas as pl
from jax.experimental.pallas import tpu as pltpu
from jax.sharding import PartitionSpec as P

ITERS = 2
REACH = 3
HALO = 2 * ITERS * REACH
GROUPS = 4
STRIP = 16
PAD = 24
DEEP = 32
LOW = -1e30
VMEM = pl.BlockSpec(memory_space=pltpu.VMEM)
ANY = pl.BlockSpec(memory_space=pl.ANY)


def params(mebibytes):
    return pltpu.CompilerParams(vmem_limit_bytes=mebibytes * 1024 * 1024)


def fetch(pairs, sems):
    copies = [
        pltpu.make_async_copy(source, target, sems.at[i])
        for i, (source, target) in enumerate(pairs)
    ]
    for copy in copies:
        copy.start()
    return copies


def wait(copies):
    for copy in copies:
        copy.wait()


def like(array):
    return pltpu.VMEM(array.shape, array.dtype)


def position(height):
    row, col = lax.axis_index("rows"), lax.axis_index("cols")
    return (
        row % 2 == 0,
        col > 0,
        col < lax.axis_size("cols") - 1,
        row * height - HALO,
        lax.axis_size("rows") * height,
    )


def sublane(width=128):
    return lax.broadcasted_iota(jnp.int32, (8, width), 0)


def lane(width=128):
    return lax.broadcasted_iota(jnp.int32, (1, width), 1)


def shifted(value, step):
    low, high = value[:, 0:128], value[:, 128:256]
    column = lane() + step
    here = (column >= 0) & (column < 128)
    low = pltpu.roll(low, (-step) % 128, axis=1)
    high = pltpu.roll(high, (-step) % 128, axis=1)
    return jnp.concatenate([jnp.where(here, low, high), jnp.where(here, high, low)], axis=1)


def turns(steps, width):
    source = lax.broadcasted_iota(jnp.int32, (256, width), 0)
    target = lax.broadcasted_iota(jnp.int32, (256, width), 1)
    return jnp.concatenate(
        [(source == (target + step) % 256).astype(jnp.bfloat16) for step in steps], axis=1
    )


def each_row(low, high, step, body):
    def some(turn, carry):
        for at in range(step):
            body(low + turn * step + at)
        return carry

    turns = (high - low) // step
    if turns > 1:
        lax.fori_loop(0, turns, some, 0)
    else:
        turns = 0
    for y in range(low + turns * step, high):
        body(y)


def split(value):
    parts = []
    for _ in range(2):
        part = value.astype(jnp.bfloat16)
        parts.append(part)
        value = value - part.astype(jnp.float32)
    return parts + [value.astype(jnp.bfloat16)]


def deep(value):
    return jnp.concatenate([value, jnp.zeros((DEEP - PAD, value.shape[1]), value.dtype)], axis=0)


def apply(square, value):
    high, middle, low = [part.astype(jnp.float32) for part in split(value)]
    stack = jnp.concatenate([high, middle, high, low, middle, high], axis=0)
    return jnp.dot(square, stack.astype(jnp.bfloat16), preferred_element_type=jnp.float32)[0:PAD]


def spread(square):
    high, middle, low = [part.astype(jnp.float32) for part in split(square[0:DEEP])]
    wide = [jnp.zeros((DEEP, 128), jnp.float32)] * 2
    for i, part in enumerate((high, high, middle, high, middle, low)):
        start = PAD * i
        moved = pltpu.roll(part, start % 128, axis=1)
        for tile in range(2):
            low_lane = start - 128 * tile
            if low_lane < 128 and low_lane + PAD > 0:
                here = (lane() >= low_lane) & (lane() < low_lane + PAD)
                wide[tile] = jnp.where(here, moved, wide[tile])
    return jnp.concatenate(wide, axis=1)[:, 0 : 6 * PAD].astype(jnp.bfloat16)


def outer(left, right):
    left = jnp.concatenate(split(deep(left)), axis=0)
    right = jnp.concatenate(split(deep(right)), axis=0)
    full = lax.dot_general(
        left, right, (((1,), (1,)), ((), ())), preferred_element_type=jnp.float32
    )
    total = None
    for i in range(3):
        for j in range(3 - i):
            term = full[i * DEEP : i * DEEP + PAD, j * DEEP : j * DEEP + PAD]
            total = term if total is None else total + term
    return total


def merge(parts):
    row = sublane(parts[0].shape[-1])
    bit = 1
    while len(parts) > 1:
        low = (row & bit) == 0
        parts = [
            jnp.where(low, first, second)
            + pltpu.roll(jnp.where(low, second, first), 8 - bit, axis=0)
            for first, second in zip(parts[::2], parts[1::2])
        ]
        bit *= 2
    return parts[0]


def fold(value):
    total = value[0:8]
    for start in range(8, value.shape[0], 8):
        total = total + value[start : start + 8]
    return total


def pack_kernel(
    feat, unary, grad, centre, left, right, inner_feat, inner_rest, outer_feat, outer_rest, wide,
    wide_unary, wide_grad,
):
    channels, height, _ = feat.shape
    classes = unary.shape[0] // height
    wide[...] = feat[...].astype(jnp.float32).reshape(channels * height, 128) * (
        1.0 / math.sqrt(channels)
    )
    for source, target, fill in ((unary, wide_unary, LOW), (grad, wide_grad, 0.0)):
        size = classes * height
        target[pl.ds(0, size)] = source[...]
        target[pl.ds(size, PAD * height - size)] = jnp.full(
            (PAD * height - size, 128), fill, jnp.float32
        )
    side = lane()
    for slot in range(height // 8):
        ends = [None, None]
        for i in range(8):
            y = 8 * slot + i
            rows = jnp.concatenate(
                [
                    wide[pl.ds(y, channels, stride=height), :],
                    wide_unary[pl.ds(y, PAD, stride=height), :],
                    wide_grad[pl.ds(y, PAD, stride=height), :],
                ],
                axis=0,
            )
            centre[y] = rows
            at = i * STRIP
            here = (side >= at) & (side < at + STRIP)
            for end, shift in ((0, at), (1, (at + STRIP) % 128)):
                moved = pltpu.roll(rows, shift, axis=1)
                ends[end] = moved if i == 0 else jnp.where(here, moved, ends[end])
        left[slot], right[slot] = ends
    even = position(height)[0]
    low = height - HALO
    for feat_out, rest_out, top in (
        (inner_feat, inner_rest, jnp.logical_not(even)),
        (outer_feat, outer_rest, even),
    ):
        base = jnp.where(top, 0, low)
        grad_base = jnp.where(top, 0, height - HALO // 2)
        for i in range(HALO):
            feat_out[i] = centre[base + i, 0:channels].astype(jnp.bfloat16)
            rest_out[i] = centre[base + i, channels : channels + PAD]
        for i in range(HALO // 2):
            rest_out[HALO + i] = centre[grad_base + i, channels + PAD :]


def pack(feat, unary, grad):
    channels, height, _ = feat.shape
    depth = channels + 2 * PAD

    def shape(*dims, dtype=jnp.float32):
        return jax.ShapeDtypeStruct(dims, dtype)

    return pl.pallas_call(
        pack_kernel,
        out_shape=(
            shape(height, depth, 128),
            shape(height // 8, depth, 128),
            shape(height // 8, depth, 128),
            shape(HALO, channels, 128, dtype=jnp.bfloat16),
            shape(HALO + HALO // 2, PAD, 128),
            shape(HALO, channels, 128, dtype=jnp.bfloat16),
            shape(HALO + HALO // 2, PAD, 128),
        ),
        in_specs=[VMEM] * 3,
        out_specs=(VMEM,) * 7,
        scratch_shapes=[
            pltpu.VMEM((count * height, 128), jnp.float32) for count in (channels, PAD, PAD)
        ],
        compiler_params=params(56),
        name="pack",
    )(feat, unary.reshape(-1, 128), grad.reshape(-1, 128))


def corner_kernel(left_in, right_in, _, inner, outer, left, right, sems):
    wait(fetch([(left_in, left), (right_in, right)], sems))
    depth = left.shape[1]
    short = depth - PAD
    even = position(8 * left.shape[0])[0]
    side = lane()
    for out, top in ((inner, jnp.logical_not(even)), (outer, even)):
        whole = jnp.where(top, 0, 1)
        out[pl.ds(0, depth)] = left[whole]
        out[pl.ds(depth, depth)] = right[whole]
        mine = (side < 64) == top
        out[pl.ds(2 * depth, short)] = jnp.where(
            mine,
            left[1 - whole, 0:short],
            pltpu.roll(right[1 - whole, 0:short], 64, axis=1),
        )


def corners(left, right, earlier):
    depth = left.shape[1]
    out = jax.ShapeDtypeStruct((3 * depth - PAD, 128), jnp.float32)
    return pl.pallas_call(
        corner_kernel,
        out_shape=(out, out),
        in_specs=[ANY] * 3,
        out_specs=(VMEM,) * 2,
        scratch_shapes=[like(left), like(right), pltpu.SemaphoreType.DMA((2,))],
        compiler_params=params(4),
        name="corners",
    )(left, right, earlier)


def sizes(here, there, size, size_there):
    rows = here.shape[0]

    def body(row):
        value = here[row]
        size[row] = fold(value * value) * 0.5
        for group in range(REACH):
            value = there[group, row]
            size_there[group, row] = fold(value * value) * 0.5

    each_row(0, rows, rows // 2, body)


def affinities(here, there, size, size_there, out):
    sub = sublane()

    def two(turn):
        y = 2 * turn
        mine = [here[y + i + REACH] for i in range(2)]
        mine_size = [size[y + i + REACH] for i in range(2)]
        for group in range(REACH):
            parts = [[], []]
            for row in range(-REACH, REACH + 2):
                other = there[group, y + row + REACH]
                other_size = size_there[group, y + row + REACH]
                for i in range(2):
                    if -REACH <= row - i <= REACH:
                        parts[i].append(fold(mine[i] * other) - (mine_size[i] + other_size))
            step_a = jnp.where(sub == 7, group + 1, sub - REACH)
            step_b = jnp.where(sub == 7, 0, group + 1)
            far = (step_a * step_a + step_b * step_b).astype(jnp.float32)
            for i in range(2):
                below = y + i + group + 1 + REACH
                parts[i].append(fold(mine[i] * here[below]) - (mine_size[i] + size[below]))
                out[y + i, pl.ds(8 * group, 8), :] = jnp.exp(
                    merge(parts[i]) - far * (1.0 / (2.0 * REACH * REACH))
                )

    each_row(0, out.shape[0] // 2, 1, two)


def strip_edge(left, left_at, right, right_at):
    right = pltpu.roll(right, (128 - right_at) % 128, axis=1)
    left = pltpu.roll(left, (128 - STRIP - left_at) % 128, axis=1)
    return jnp.where(lane() < 64, right, left)


def main_kernel(
    centre, inner, outer, kern_out, feat, short, turned, size, size_turned, turner,
):
    height, channels = centre.shape[0], feat.shape[1]
    tall = feat.shape[0]
    turner[...] = turns(range(1, REACH + 1), 128)[0:128]
    for at in (0, tall - REACH):
        feat[pl.ds(at, REACH)] = jnp.zeros((REACH, channels, 128), jnp.float32)
        short[pl.ds(at, REACH)] = jnp.zeros((REACH, channels, 128), jnp.bfloat16)
    even = position(height)[0]
    above = jnp.where(even, REACH + HALO + height, REACH)
    for source, base in ((inner, above), (outer, tall - HALO - above)):
        for i in range(HALO):
            feat[base + i] = source[i].astype(jnp.float32)
            short[base + i] = source[i]
    for y in range(height):
        row = y + HALO + REACH
        value = centre[y, 0:channels]
        feat[row] = value
        short[row] = value.astype(jnp.bfloat16)
    moved = jnp.dot(
        short[...].reshape(tall * channels, 128), turner[...], preferred_element_type=jnp.float32
    )
    for group in range(REACH):
        turned[group] = moved[:, 128 * group : 128 * group + 128].reshape(tall, channels, 128)
    sizes(feat, turned, size, size_turned)
    affinities(feat, turned, size, size_turned, kern_out)


def main_affinities(centre, inner, outer):
    height, depth, _ = centre.shape
    channels = depth - 2 * PAD
    rows = height + 2 * HALO
    tall = rows + 2 * REACH
    inputs = (centre, inner, outer)

    def room(*dims, dtype=jnp.float32):
        return pltpu.VMEM(dims, dtype)

    return pl.pallas_call(
        main_kernel,
        out_shape=jax.ShapeDtypeStruct((rows, PAD, 128), jnp.float32),
        in_specs=[VMEM] * 3,
        out_specs=VMEM,
        scratch_shapes=[
            room(tall, channels, 128),
            room(tall, channels, 128, dtype=jnp.bfloat16),
            room(REACH, tall, channels, 128),
            room(tall, 8, 128),
            room(REACH, tall, 8, 128),
            room(128, REACH * 128, dtype=jnp.bfloat16),
        ],
        compiler_params=params(16),
        cost_estimate=pl.CostEstimate(
            flops=200_000_000, bytes_accessed=8_000_000, transcendentals=0
        ),
        name="main_affinities",
    )(*inputs)


def side_turns():
    target = lax.broadcasted_iota(jnp.int32, (256, 128), 1)
    source = lax.broadcasted_iota(jnp.int32, (256, 128), 0)
    place = target % 32
    column = jnp.where(place < 12, place - 12, jnp.where(place < 24, 116 + place, 101 + place))
    blocks = []
    for b in range(REACH + 1):
        hit = source == (column + b + 256) % 256
        blocks.append(
            jnp.concatenate(
                [(hit & (target // 32 == j)).astype(jnp.bfloat16) for j in range(GROUPS)], axis=0
            )
        )
    return jnp.concatenate(blocks, axis=1)


def pass_row(y, kern, field, turned):
    def weight(row, at):
        return kern[row, pl.ds(at, 1), :]

    total = None

    def plus(total, term):
        return term if total is None else total + term

    for group in range(REACH):
        step = group + 1
        back = None
        for a in range(-REACH, REACH + 1):
            at = 8 * group + a + REACH
            total = plus(total, weight(y, at) * turned[group, y + a])
            back = plus(back, weight(y - a, at) * field[y - a])
        total = total + weight(y, 8 * group + 7) * field[y + step]
        total = total + weight(y - step, 8 * group + 7) * field[y - step]
        total = total + shifted(back, -step)
    return total


def softmax(value):
    top = jnp.max(value, axis=0, keepdims=True)
    power = jnp.exp(value - top)
    return power * (1.0 / jnp.sum(power, axis=0, keepdims=True))


def field_kernel(
    square_in, centre, from_left, from_right, inner_feat, inner_rest, outer_feat, outer_rest,
    inner_corner, outer_corner, main,
    feat_out, kern_out, prob0_out, prob1_out, grad1_out, grad0_out, share,
    short, side_feat, side_turned, side_size, side_size_turned, side_kern,
    kern, unary, grad, prob0, prob1, grad1, grad0, turned, message0, message1, logit1, logit0,
    side_turner, square, compat, compat_t, out_sems,
):
    height = centre.shape[0]
    going = []

    def send(source, target, low):
        copy = pltpu.make_async_copy(
            source.at[pl.ds(low, target.shape[0])], target, out_sems.at[len(going)]
        )
        copy.start()
        going.append(copy)

    rows = height + 2 * HALO
    channels = short.shape[1]
    side = lane()
    side_turner[...] = side_turns()
    square[...] = jnp.zeros_like(square)
    square[0 : square_in.shape[0], 0 : square_in.shape[1]] = square_in[...]
    compat[...] = spread(square[...])
    compat_t[...] = spread(square[...].T)

    for at in (0, rows + REACH):
        short[pl.ds(at, REACH)] = jnp.zeros((REACH, channels, 256), jnp.bfloat16)

    def put(row, own, left, left_at, right, right_at):
        edge = strip_edge(left, left_at, right, right_at)
        for value, cols in ((own, slice(0, 128)), (edge, slice(128, 256))):
            short[row + REACH, :, cols] = value[0:channels].astype(jnp.bfloat16)
            unary[row, :, cols] = value[channels : channels + PAD]
            if value.shape[0] > channels + PAD:
                grad[row, :, cols] = value[channels + PAD :]

    for y in range(height):
        at = (y % 8) * STRIP
        put(HALO + y, centre[y], from_left[y // 8], at, from_right[y // 8], at)

    depth = channels + 2 * PAD
    slim = channels + PAD
    near = HALO // 2

    def edge_row(feat_in, rest_in, i, top):
        parts = [feat_in[i].astype(jnp.float32), rest_in[i]]
        row = i if top else i - near
        if 0 <= row < near:
            parts.append(rest_in[HALO + row])
        return jnp.concatenate(parts, axis=0)

    def put_rows(edge_rows, corner, top):
        base = HALO + height if top else 0
        half = HALO - 8
        for i in range(HALO):
            at = (i if top else i - half) * STRIP
            if 0 <= at < 128:
                left, right = corner[pl.ds(0, depth)], corner[pl.ds(depth, depth)]
                left_at = right_at = at
            else:
                left = right = corner[pl.ds(2 * depth, slim)]
                left_at = (i - 8) * STRIP if top else 64 + i * STRIP
                right_at = (left_at + 64) % 128
            own = edge_rows(i, top)
            size = min(own.shape[0], left.shape[0])
            put(base + i, own[0:size], left[0:size], left_at, right[0:size], right_at)

    even, has_left, has_right, first_row, all_rows = position(height)
    for edge_rows, corner, below in (
        (functools.partial(edge_row, inner_feat, inner_rest), inner_corner, even),
        (functools.partial(edge_row, outer_feat, outer_rest), outer_corner, jnp.logical_not(even)),
    ):
        pl.when(below)(functools.partial(put_rows, edge_rows, corner, True))
        pl.when(jnp.logical_not(below))(functools.partial(put_rows, edge_rows, corner, False))

    wide_lane = lane(256)
    inside_lane = (
        (wide_lane < 128)
        | ((wide_lane < 192) & has_right)
        | ((wide_lane >= 192) & has_left)
    )

    def inside(y):
        row = first_row + y
        return inside_lane & (row >= 0) & (row < all_rows)

    send(short, feat_out, HALO)
    slots = rows // GROUPS
    tall = slots + 2 * REACH
    stacked = jnp.concatenate(
        [
            jnp.concatenate([short[slots * j + k] for j in range(GROUPS)], axis=1)
            for k in range(tall)
        ],
        axis=0,
    )
    moved = jnp.dot(stacked, side_turner[...], preferred_element_type=jnp.float32)
    side_feat[...] = moved[:, 0:128].reshape(tall, channels, 128)
    for group in range(REACH):
        start = 128 * group + 128
        side_turned[group] = moved[:, start : start + 128].reshape(tall, channels, 128)
    sizes(side_feat, side_turned, side_size, side_size_turned)
    affinities(side_feat, side_turned, side_size, side_size_turned, side_kern)
    for j in range(GROUPS):
        for k in range(slots):
            y, value = slots * j + k, side_kern[k]
            kern[y, :, 128:256] = pltpu.roll(value, (116 - 32 * j) % 128, axis=1)
            last = pltpu.roll(value, (101 - 32 * j) % 128, axis=1)
            kern[y, :, 0:128] = jnp.where(side < 128 - REACH, main[y], last)
    send(kern, kern_out, HALO - REACH)

    def put_field(field, y, value):
        field[y] = value
        for group in range(REACH):
            turned[group, y] = shifted(value, group + 1)

    def start(y):
        put_field(prob0, y, jnp.where(inside(y), softmax(unary[y]), 0.0))

    each_row(0, rows, rows // 2, start)
    send(prob0, prob0_out, HALO - REACH)

    def run_pass(field, out, low, high):
        def body(y):
            out[y] = pass_row(y, kern, field, turned)

        each_row(low, high, 2, body)

    run_pass(prob0, message0, REACH, rows - REACH)

    def mix(y):
        value = softmax(unary[y] - apply(compat[...], message0[y]))
        put_field(prob1, y, jnp.where(inside(y), value, 0.0))

    each_row(REACH, rows - REACH, rows, mix)
    send(prob1, prob1_out, HALO - REACH)
    run_pass(prob1, message1, 2 * REACH, rows - 2 * REACH)

    def back1(y):
        prob = softmax(unary[y] - apply(compat[...], message1[y]))
        cot = grad[y]
        change = prob * (cot - jnp.sum(cot * prob, axis=0, keepdims=True))
        logit1[y] = change
        put_field(grad1, y, jnp.where(inside(y), -apply(compat_t[...], change), 0.0))

    each_row(2 * REACH, rows - 2 * REACH, rows, back1)
    def share_of(change, message):
        block = range(HALO, HALO + height)
        left = jnp.concatenate([change[y, :, 0:128] for y in block], axis=1)
        right = jnp.concatenate([message[y, :, 0:128] for y in block], axis=1)
        return outer(left, right)

    total = -share_of(logit1, message1)
    run_pass(grad1, message1, 3 * REACH, rows - 3 * REACH)

    def back0(y):
        prob = prob1[y]
        cot = message1[y]
        change = prob * (cot - jnp.sum(cot * prob, axis=0, keepdims=True))
        logit0[y] = change
        grad0[y] = jnp.where(inside(y), -apply(compat_t[...], change), 0.0)

    each_row(3 * REACH, rows - 3 * REACH, rows, back0)
    total = total - share_of(logit0, message0)

    total = jnp.concatenate([total, jnp.zeros((PAD, 128 - PAD), jnp.float32)], axis=1)
    packed = (
        total[0:8]
        + pltpu.roll(total[8:16], 32, axis=1)
        + pltpu.roll(total[16:24], 64, axis=1)
    )
    for slot in range(share.shape[0]):
        share[slot] = packed

    middle = (side >= 32) & (side < 96)

    def add_logit(y):
        at = y + HALO
        value = logit0[at, :, 0:128] + logit1[at, :, 0:128]
        for field, shift in ((grad1, 32), (grad0, 96)):
            field[at, :, 128:256] = jnp.where(
                middle, pltpu.roll(value, shift, axis=1), field[at, :, 128:256]
            )

    each_row(0, height, height, add_logit)
    send(grad1, grad1_out, HALO - REACH)
    send(grad0, grad0_out, HALO - REACH)
    wait(going)


def iterate(compat, centre, received, main, devices):
    height, depth, _ = centre.shape
    channels = depth - 2 * PAD
    rows = height + 2 * HALO
    tall = rows + 2 * REACH
    near = height + 2 * REACH
    slots = rows // GROUPS

    def shape(*dims):
        return jax.ShapeDtypeStruct(dims, jnp.float32)

    def room(*dims):
        return pltpu.VMEM(dims, jnp.float32)

    return pl.pallas_call(
        field_kernel,
        out_shape=(
            jax.ShapeDtypeStruct((near, channels, 256), jnp.bfloat16),
            shape(near, PAD, 256),
            shape(near, PAD, 256),
            shape(near, PAD, 256),
            shape(near, PAD, 256),
            shape(near, PAD, 256),
            shape(devices, 8, 128),
        ),
        in_specs=[VMEM] * (3 + len(received)),
        out_specs=(ANY,) * 6 + (VMEM,),
        scratch_shapes=[
            pltpu.VMEM((tall, channels, 256), jnp.bfloat16),
            room(slots + 2 * REACH, channels, 128),
            room(REACH, slots + 2 * REACH, channels, 128),
            room(slots + 2 * REACH, 8, 128),
            room(REACH, slots + 2 * REACH, 8, 128),
            room(slots, PAD, 128),
            *[room(rows, PAD, 256)] * 7,
            room(REACH, rows, PAD, 256),
            *[room(rows, PAD, 256)] * 4,
            pltpu.VMEM((GROUPS * 256, (REACH + 1) * 128), jnp.bfloat16),
            room(128, 128),
            pltpu.VMEM((DEEP, 6 * PAD), jnp.bfloat16),
            pltpu.VMEM((DEEP, 6 * PAD), jnp.bfloat16),
            pltpu.SemaphoreType.DMA((6,)),
        ],
        compiler_params=params(28),
        name="iterate",
    )(compat, centre, *received, main)


def finish_kernel(
    feat, kern, prob0, prob1, grad1, grad0, unary_out, feat_out, feat_turned, all_turned, kern_back, weights,
    turner, unary_rows, out_sem,
):
    near = feat.shape[0]
    height = near - 2 * REACH
    channels = feat.shape[1]
    classes = unary_out.shape[0] // height
    steps = range(-REACH, REACH + 1)

    turner[...] = turns(steps, 128)
    column = lane()

    def moved(main, edge, b):
        if b == 0:
            return main
        mixed = jnp.where((column < b) if b > 0 else (column >= 128 + b), edge, main)
        return pltpu.roll(mixed, (-b) % 128, axis=1)

    full = jnp.dot(
        feat[...].reshape(near * channels, 256), turner[...], preferred_element_type=jnp.float32
    )
    for place in range(len(steps)):
        feat_turned[place] = full[:, 128 * place : 128 * place + 128].reshape(near, channels, 128)

    def prepare(row):
        for place, field in enumerate((prob0, prob1, grad1, grad0)):
            main, edge = field[row, :, 0:128], field[row, :, 128:256]
            for b in steps:
                all_turned[b + REACH, row, pl.ds(place * PAD, PAD), :] = moved(main, edge, b)
        for group in range(REACH):
            rows = pl.ds(8 * group, 8)
            main, edge = kern[row, rows, 0:128], kern[row, rows, 128:256]
            kern_back[row, rows, :] = jnp.where(
                sublane() == 7, main, moved(main, edge, -(group + 1))
            )

    each_row(0, near, near, prepare)

    def pass_centre(y):
        total = jnp.zeros((PAD, 128), jnp.float32)
        last = pl.ds(3 * PAD, PAD)
        for group in range(REACH):
            step = group + 1
            back = [jnp.zeros((PAD, 128), jnp.float32)] * 2
            for a in range(-REACH, REACH + 1):
                one = pl.ds(8 * group + a + REACH, 1)
                total = total + kern[y, one, 0:128] * all_turned[step + REACH, y + a, last, :]
                for tile in range(2):
                    cols = slice(128 * tile, 128 * tile + 128)
                    back[tile] = back[tile] + kern[y - a, one, cols] * grad0[y - a, :, cols]
            one = pl.ds(8 * group + 7, 1)
            total = total + kern[y, one, 0:128] * grad0[y + step, :, 0:128]
            total = total + kern[y - step, one, 0:128] * grad0[y - step, :, 0:128]
            total = total + moved(back[0], back[1], -step)
        return total

    def unary_row(y):
        cot = pass_centre(y + REACH)
        prob = prob0[y + REACH, :, 0:128]
        row = y + REACH
        partial = jnp.where(
            column < 64,
            pltpu.roll(grad1[row, :, 128:256], 96, axis=1),
            pltpu.roll(grad0[row, :, 128:256], 32, axis=1),
        )
        value = partial + prob * (cot - jnp.sum(cot * prob, axis=0, keepdims=True))
        unary_rows[pl.ds(y, PAD, stride=height), :] = value

    each_row(0, height, 4, unary_row)
    leaving = pltpu.make_async_copy(
        unary_rows.at[pl.ds(0, classes * height)], unary_out, out_sem
    )
    leaving.start()
    sub = sublane()

    def feature_row(y):
        row = y + REACH
        own = all_turned[REACH, row]
        mate = jnp.concatenate(
            [own[3 * PAD :], own[2 * PAD : 3 * PAD], own[PAD : 2 * PAD], own[0:PAD]], axis=0
        )
        total = None
        whole = None
        for sign in (1, -1):
            for group in range(REACH):
                parts = []
                places = []
                for s in range(8):
                    a, b = (s - REACH, group + 1) if s < 7 else (group + 1, 0)
                    a, b = sign * a, sign * b
                    places.append((a, b))
                    parts.append(fold(mate * all_turned[b + REACH, row + a]))
                if sign > 0:
                    weight = kern[row, pl.ds(8 * group, 8), 0:128]
                else:
                    weight = kern_back[row - (group + 1), pl.ds(8 * group, 8), :]
                    for s in range(7):
                        weight = jnp.where(
                            sub == s, kern_back[row - (s - REACH), pl.ds(8 * group, 8), :], weight
                        )
                weight = weight * merge(parts)
                whole = weight if whole is None else whole + weight
                at = 8 * (group + (0 if sign > 0 else REACH))
                weights[y, pl.ds(at, 8), :] = weight
                for s, (a, b) in enumerate(places):
                    term = weights[y, pl.ds(at + s, 1), :] * feat_turned[b + REACH, row + a]
                    total = term if total is None else total + term
        whole = jnp.sum(whole, axis=0, keepdims=True)
        total = total - whole * feat_turned[REACH, row]
        feat_out[pl.ds(y, channels, stride=height), :] = total * (1.0 / math.sqrt(channels))

    each_row(0, height, 1, feature_row)
    leaving.wait()


def finish(feat, kern, prob0, prob1, grad1, grad0, classes):
    near, channels, _ = feat.shape
    height = near - 2 * REACH

    def room(*dims):
        return pltpu.VMEM(dims, jnp.float32)

    return pl.pallas_call(
        finish_kernel,
        out_shape=(
            jax.ShapeDtypeStruct((classes * height, 128), jnp.float32),
            jax.ShapeDtypeStruct((channels * height, 128), jnp.float32),
        ),
        in_specs=[VMEM] * 6,
        out_specs=(ANY, VMEM),
        scratch_shapes=[
            room(2 * REACH + 1, near, channels, 128),
            room(2 * REACH + 1, near, 4 * PAD, 128),
            room(near, PAD, 128),
            room(height, 6 * 8, 128),
            pltpu.VMEM((256, (2 * REACH + 1) * 128), jnp.bfloat16),
            room(PAD * height, 128),
            pltpu.SemaphoreType.DMA,
        ],
        compiler_params=params(24),
        cost_estimate=pl.CostEstimate(flops=200_000_000, bytes_accessed=8_000_000, transcendentals=0),
        name="finish",
    )(feat, kern, prob0, prob1, grad1, grad0)


def on_device(unary, features, compat, grad_output):
    classes, height, width = unary.shape
    n_rows, n_cols = lax.axis_size("rows"), lax.axis_size("cols")

    below = [pair for i in range(0, n_rows, 2) for pair in ((i, i + 1), (i + 1, i))]
    above = [
        pair
        for i in range(1, n_rows, 2)
        for pair in ((i, (i + 1) % n_rows), ((i + 1) % n_rows, i))
    ]
    forward = [(i, i + 1) for i in range(n_cols - 1)]
    backward = [(i + 1, i) for i in range(n_cols - 1)]
    centre, left, right, inner_feat, inner_rest, outer_feat, outer_rest = pack(
        features, unary, grad_output
    )
    inner_feat = lax.ppermute(inner_feat, "rows", below)
    inner_rest = lax.ppermute(inner_rest, "rows", below)
    outer_feat = lax.ppermute(outer_feat, "rows", above)
    outer_rest = lax.ppermute(outer_rest, "rows", above)
    from_left = lax.ppermute(right, "cols", forward)
    from_right = lax.ppermute(left, "cols", backward)
    inner_corner, outer_corner = corners(from_left, from_right, outer_feat)
    outer_corner = lax.ppermute(outer_corner, "rows", above)
    inner_corner = lax.ppermute(inner_corner, "rows", below)
    main = main_affinities(centre, inner_feat, outer_feat)
    received = (
        from_left, from_right, inner_feat, inner_rest, outer_feat, outer_rest, inner_corner,
        outer_corner,
    )

    devices = n_rows * n_cols
    *fields, share = iterate(
        compat, centre, received, main, devices
    )
    shares = lax.all_to_all(share, ("rows", "cols"), 0, 0)
    unary_grad, feature_grad = finish(*fields, classes)
    summed = jnp.sum(shares, axis=0) / math.sqrt(n_rows * height * n_cols * width)
    compat_grad = jnp.concatenate(
        [summed[:, 0:PAD], summed[:, 32 : 32 + PAD], summed[:, 64 : 64 + PAD]], axis=0
    )[:classes, :classes]
    return (
        unary_grad.reshape(unary.shape),
        feature_grad.reshape(features.shape),
        compat_grad,
    )


def solution(mesh):
    placed = (P(None, "rows", "cols"), P(None, "rows", "cols"), P(), P(None, "rows", "cols"))
    return jax.shard_map(
        on_device,
        mesh=mesh,
        in_specs=placed,
        out_specs=(P(None, "rows", "cols"), P(None, "rows", "cols"), P()),
        check_vma=False,
    )
```

```python
import functools
import math

import jax
import jax.numpy as jnp
from jax import lax
from jax.experimental import pallas as pl
from jax.experimental.pallas import tpu as pltpu
from jax.sharding import PartitionSpec as P

ITERS = 2
REACH = 3
HALO = 2 * ITERS * REACH
GROUPS = 4
STRIP = 16
PAD = 24
DEEP = 32
LOW = -1e30
VMEM = pl.BlockSpec(memory_space=pltpu.VMEM)
ANY = pl.BlockSpec(memory_space=pl.ANY)


def params(mebibytes):
    return pltpu.CompilerParams(vmem_limit_bytes=mebibytes * 1024 * 1024)


def fetch(pairs, sems):
    copies = [
        pltpu.make_async_copy(source, target, sems.at[i])
        for i, (source, target) in enumerate(pairs)
    ]
    for copy in copies:
        copy.start()
    return copies


def wait(copies):
    for copy in copies:
        copy.wait()


def like(array):
    return pltpu.VMEM(array.shape, array.dtype)


def position(height):
    row, col = lax.axis_index("rows"), lax.axis_index("cols")
    return (
        row % 2 == 0,
        col > 0,
        col < lax.axis_size("cols") - 1,
        row * height - HALO,
        lax.axis_size("rows") * height,
    )


def sublane(width=128):
    return lax.broadcasted_iota(jnp.int32, (8, width), 0)


def lane(width=128):
    return lax.broadcasted_iota(jnp.int32, (1, width), 1)


def shifted(value, step):
    low, high = value[:, 0:128], value[:, 128:256]
    column = lane() + step
    here = (column >= 0) & (column < 128)
    low = pltpu.roll(low, (-step) % 128, axis=1)
    high = pltpu.roll(high, (-step) % 128, axis=1)
    return jnp.concatenate([jnp.where(here, low, high), jnp.where(here, high, low)], axis=1)


def turns(steps, width):
    source = lax.broadcasted_iota(jnp.int32, (256, width), 0)
    target = lax.broadcasted_iota(jnp.int32, (256, width), 1)
    return jnp.concatenate(
        [(source == (target + step) % 256).astype(jnp.bfloat16) for step in steps], axis=1
    )


def each_row(low, high, step, body):
    def some(turn, carry):
        for at in range(step):
            body(low + turn * step + at)
        return carry

    turns = (high - low) // step
    if turns > 1:
        lax.fori_loop(0, turns, some, 0)
    else:
        turns = 0
    for y in range(low + turns * step, high):
        body(y)


def split(value):
    parts = []
    for _ in range(2):
        part = value.astype(jnp.bfloat16)
        parts.append(part)
        value = value - part.astype(jnp.float32)
    return parts + [value.astype(jnp.bfloat16)]


def deep(value):
    return jnp.concatenate([value, jnp.zeros((DEEP - PAD, value.shape[1]), value.dtype)], axis=0)


def apply(square, value):
    high, middle, low = [part.astype(jnp.float32) for part in split(value)]
    stack = jnp.concatenate([high, middle, high, low, middle, high], axis=0)
    return jnp.dot(square, stack.astype(jnp.bfloat16), preferred_element_type=jnp.float32)[0:PAD]


def spread(square):
    high, middle, low = [part.astype(jnp.float32) for part in split(square[0:DEEP])]
    wide = [jnp.zeros((DEEP, 128), jnp.float32)] * 2
    for i, part in enumerate((high, high, middle, high, middle, low)):
        start = PAD * i
        moved = pltpu.roll(part, start % 128, axis=1)
        for tile in range(2):
            low_lane = start - 128 * tile
            if low_lane < 128 and low_lane + PAD > 0:
                here = (lane() >= low_lane) & (lane() < low_lane + PAD)
                wide[tile] = jnp.where(here, moved, wide[tile])
    return jnp.concatenate(wide, axis=1)[:, 0 : 6 * PAD].astype(jnp.bfloat16)


def outer(left, right):
    left = jnp.concatenate(split(deep(left)), axis=0)
    right = jnp.concatenate(split(deep(right)), axis=0)
    full = lax.dot_general(
        left, right, (((1,), (1,)), ((), ())), preferred_element_type=jnp.float32
    )
    total = None
    for i in range(3):
        for j in range(3 - i):
            term = full[i * DEEP : i * DEEP + PAD, j * DEEP : j * DEEP + PAD]
            total = term if total is None else total + term
    return total


def merge(parts):
    row = sublane(parts[0].shape[-1])
    bit = 1
    while len(parts) > 1:
        low = (row & bit) == 0
        parts = [
            jnp.where(low, first, second)
            + pltpu.roll(jnp.where(low, second, first), 8 - bit, axis=0)
            for first, second in zip(parts[::2], parts[1::2])
        ]
        bit *= 2
    return parts[0]


def fold(value):
    total = value[0:8]
    for start in range(8, value.shape[0], 8):
        total = total + value[start : start + 8]
    return total


def pack_kernel(
    feat, unary, grad, centre, left, right, inner_feat, inner_rest, outer_feat, outer_rest, wide,
    wide_unary, wide_grad,
):
    channels, height, _ = feat.shape
    classes = unary.shape[0] // height
    wide[...] = feat[...].astype(jnp.float32).reshape(channels * height, 128) * (
        1.0 / math.sqrt(channels)
    )
    for source, target, fill in ((unary, wide_unary, LOW), (grad, wide_grad, 0.0)):
        size = classes * height
        target[pl.ds(0, size)] = source[...]
        target[pl.ds(size, PAD * height - size)] = jnp.full(
            (PAD * height - size, 128), fill, jnp.float32
        )
    side = lane()
    for slot in range(height // 8):
        ends = [None, None]
        for i in range(8):
            y = 8 * slot + i
            rows = jnp.concatenate(
                [
                    wide[pl.ds(y, channels, stride=height), :],
                    wide_unary[pl.ds(y, PAD, stride=height), :],
                    wide_grad[pl.ds(y, PAD, stride=height), :],
                ],
                axis=0,
            )
            centre[y] = rows
            at = i * STRIP
            here = (side >= at) & (side < at + STRIP)
            for end, shift in ((0, at), (1, (at + STRIP) % 128)):
                moved = pltpu.roll(rows, shift, axis=1)
                ends[end] = moved if i == 0 else jnp.where(here, moved, ends[end])
        left[slot], right[slot] = ends
    even = position(height)[0]
    low = height - HALO
    for feat_out, rest_out, top in (
        (inner_feat, inner_rest, jnp.logical_not(even)),
        (outer_feat, outer_rest, even),
    ):
        base = jnp.where(top, 0, low)
        grad_base = jnp.where(top, 0, height - HALO // 2)
        for i in range(HALO):
            feat_out[i] = centre[base + i, 0:channels].astype(jnp.bfloat16)
            rest_out[i] = centre[base + i, channels : channels + PAD]
        for i in range(HALO // 2):
            rest_out[HALO + i] = centre[grad_base + i, channels + PAD :]


def pack(feat, unary, grad):
    channels, height, _ = feat.shape
    depth = channels + 2 * PAD

    def shape(*dims, dtype=jnp.float32):
        return jax.ShapeDtypeStruct(dims, dtype)

    return pl.pallas_call(
        pack_kernel,
        out_shape=(
            shape(height, depth, 128),
            shape(height // 8, depth, 128),
            shape(height // 8, depth, 128),
            shape(HALO, channels, 128, dtype=jnp.bfloat16),
            shape(HALO + HALO // 2, PAD, 128),
            shape(HALO, channels, 128, dtype=jnp.bfloat16),
            shape(HALO + HALO // 2, PAD, 128),
        ),
        in_specs=[VMEM] * 3,
        out_specs=(VMEM,) * 7,
        scratch_shapes=[
            pltpu.VMEM((count * height, 128), jnp.float32) for count in (channels, PAD, PAD)
        ],
        compiler_params=params(56),
        name="pack",
    )(feat, unary.reshape(-1, 128), grad.reshape(-1, 128))


def corner_kernel(left_in, right_in, _, inner, outer, left, right, sems):
    wait(fetch([(left_in, left), (right_in, right)], sems))
    depth = left.shape[1]
    short = depth - PAD
    even = position(8 * left.shape[0])[0]
    side = lane()
    for out, top in ((inner, jnp.logical_not(even)), (outer, even)):
        whole = jnp.where(top, 0, 1)
        out[pl.ds(0, short)] = left[whole, 0:short]
        out[pl.ds(short, short)] = right[whole, 0:short]
        out[pl.ds(3 * short, PAD)] = jnp.where(
            side % STRIP < STRIP // 2, right[whole, short:], left[whole, short:]
        )
        mine = (side < 64) == top
        out[pl.ds(2 * short, short)] = jnp.where(
            mine,
            left[1 - whole, 0:short],
            pltpu.roll(right[1 - whole, 0:short], 64, axis=1),
        )


def corners(left, right, earlier):
    depth = left.shape[1]
    out = jax.ShapeDtypeStruct((3 * depth - 2 * PAD, 128), jnp.float32)
    return pl.pallas_call(
        corner_kernel,
        out_shape=(out, out),
        in_specs=[ANY] * 3,
        out_specs=(VMEM,) * 2,
        scratch_shapes=[like(left), like(right), pltpu.SemaphoreType.DMA((2,))],
        compiler_params=params(4),
        name="corners",
    )(left, right, earlier)


def sizes(here, there, size, size_there):
    rows = here.shape[0]

    def body(row):
        value = here[row]
        size[row] = fold(value * value) * 0.5
        for group in range(REACH):
            value = there[group, row]
            size_there[group, row] = fold(value * value) * 0.5

    each_row(0, rows, rows // 2, body)


def affinities(here, there, size, size_there, out):
    sub = sublane()

    def two(turn):
        y = 2 * turn
        mine = [here[y + i + REACH] for i in range(2)]
        mine_size = [size[y + i + REACH] for i in range(2)]
        for group in range(REACH):
            parts = [[], []]
            for row in range(-REACH, REACH + 2):
                other = there[group, y + row + REACH]
                other_size = size_there[group, y + row + REACH]
                for i in range(2):
                    if -REACH <= row - i <= REACH:
                        parts[i].append(fold(mine[i] * other) - (mine_size[i] + other_size))
            step_a = jnp.where(sub == 7, group + 1, sub - REACH)
            step_b = jnp.where(sub == 7, 0, group + 1)
            far = (step_a * step_a + step_b * step_b).astype(jnp.float32)
            for i in range(2):
                below = y + i + group + 1 + REACH
                parts[i].append(fold(mine[i] * here[below]) - (mine_size[i] + size[below]))
                out[y + i, pl.ds(8 * group, 8), :] = jnp.exp(
                    merge(parts[i]) - far * (1.0 / (2.0 * REACH * REACH))
                )

    each_row(0, out.shape[0] // 2, 1, two)


def strip_edge(left, left_at, right, right_at):
    right = pltpu.roll(right, (128 - right_at) % 128, axis=1)
    left = pltpu.roll(left, (128 - STRIP - left_at) % 128, axis=1)
    return jnp.where(lane() < 64, right, left)


def main_kernel(
    centre, inner, outer, kern_out, feat, short, turned, size, size_turned, turner,
):
    height, channels = centre.shape[0], feat.shape[1]
    tall = feat.shape[0]
    turner[...] = turns(range(1, REACH + 1), 128)[0:128]
    for at in (0, tall - REACH):
        feat[pl.ds(at, REACH)] = jnp.zeros((REACH, channels, 128), jnp.float32)
        short[pl.ds(at, REACH)] = jnp.zeros((REACH, channels, 128), jnp.bfloat16)
    even = position(height)[0]
    above = jnp.where(even, REACH + HALO + height, REACH)
    for source, base in ((inner, above), (outer, tall - HALO - above)):
        for i in range(HALO):
            feat[base + i] = source[i].astype(jnp.float32)
            short[base + i] = source[i]
    for y in range(height):
        row = y + HALO + REACH
        value = centre[y, 0:channels]
        feat[row] = value
        short[row] = value.astype(jnp.bfloat16)
    moved = jnp.dot(
        short[...].reshape(tall * channels, 128), turner[...], preferred_element_type=jnp.float32
    )
    for group in range(REACH):
        turned[group] = moved[:, 128 * group : 128 * group + 128].reshape(tall, channels, 128)
    sizes(feat, turned, size, size_turned)
    affinities(feat, turned, size, size_turned, kern_out)


def main_affinities(centre, inner, outer):
    height, depth, _ = centre.shape
    channels = depth - 2 * PAD
    rows = height + 2 * HALO
    tall = rows + 2 * REACH
    inputs = (centre, inner, outer)

    def room(*dims, dtype=jnp.float32):
        return pltpu.VMEM(dims, dtype)

    return pl.pallas_call(
        main_kernel,
        out_shape=jax.ShapeDtypeStruct((rows, PAD, 128), jnp.float32),
        in_specs=[VMEM] * 3,
        out_specs=VMEM,
        scratch_shapes=[
            room(tall, channels, 128),
            room(tall, channels, 128, dtype=jnp.bfloat16),
            room(REACH, tall, channels, 128),
            room(tall, 8, 128),
            room(REACH, tall, 8, 128),
            room(128, REACH * 128, dtype=jnp.bfloat16),
        ],
        compiler_params=params(16),
        cost_estimate=pl.CostEstimate(
            flops=200_000_000, bytes_accessed=8_000_000, transcendentals=0
        ),
        name="main_affinities",
    )(*inputs)


def side_turns():
    target = lax.broadcasted_iota(jnp.int32, (256, 128), 1)
    source = lax.broadcasted_iota(jnp.int32, (256, 128), 0)
    place = target % 32
    column = jnp.where(place < 12, place - 12, jnp.where(place < 24, 116 + place, 101 + place))
    blocks = []
    for b in range(REACH + 1):
        hit = source == (column + b + 256) % 256
        blocks.append(
            jnp.concatenate(
                [(hit & (target // 32 == j)).astype(jnp.bfloat16) for j in range(GROUPS)], axis=0
            )
        )
    return jnp.concatenate(blocks, axis=1)


def pass_row(y, kern, field, turned):
    def weight(row, at):
        return kern[row, pl.ds(at, 1), :]

    total = None

    def plus(total, term):
        return term if total is None else total + term

    for group in range(REACH):
        step = group + 1
        back = None
        for a in range(-REACH, REACH + 1):
            at = 8 * group + a + REACH
            total = plus(total, weight(y, at) * turned[group, y + a])
            back = plus(back, weight(y - a, at) * field[y - a])
        total = total + weight(y, 8 * group + 7) * field[y + step]
        total = total + weight(y - step, 8 * group + 7) * field[y - step]
        total = total + shifted(back, -step)
    return total


def softmax(value):
    top = jnp.max(value, axis=0, keepdims=True)
    power = jnp.exp(value - top)
    return power * (1.0 / jnp.sum(power, axis=0, keepdims=True))


def field_kernel(
    square_in, centre, from_left, from_right, inner_feat, inner_rest, outer_feat, outer_rest,
    inner_corner, outer_corner, main,
    feat_out, kern_out, prob0_out, prob1_out, grad1_out, grad0_out, share,
    short, side_feat, side_turned, side_size, side_size_turned, side_kern,
    kern, unary, grad, prob0, prob1, grad1, grad0, turned, message0, message1, logit1, logit0,
    side_turner, square, compat, compat_t,
):
    height = centre.shape[0]
    def send(source, target, low):
        def body(row):
            target[row] = source[row + low]

        each_row(0, target.shape[0], target.shape[0], body)

    rows = height + 2 * HALO
    channels = short.shape[1]
    side = lane()
    side_turner[...] = side_turns()
    square[...] = jnp.zeros_like(square)
    square[0 : square_in.shape[0], 0 : square_in.shape[1]] = square_in[...]
    compat[...] = spread(square[...])
    compat_t[...] = spread(square[...].T)

    for at in (0, rows + REACH):
        short[pl.ds(at, REACH)] = jnp.zeros((REACH, channels, 256), jnp.bfloat16)

    def put(row, own, left, left_at, right, right_at):
        edge = strip_edge(left, left_at, right, right_at)
        for value, cols in ((own, slice(0, 128)), (edge, slice(128, 256))):
            short[row + REACH, :, cols] = value[0:channels].astype(jnp.bfloat16)
            unary[row, :, cols] = value[channels : channels + PAD]
            if value.shape[0] > channels + PAD:
                grad[row, :, cols] = value[channels + PAD :]

    for y in range(height):
        at = (y % 8) * STRIP
        put(HALO + y, centre[y], from_left[y // 8], at, from_right[y // 8], at)

    slim = channels + PAD
    near = HALO // 2

    def edge_row(feat_in, rest_in, i, top):
        parts = [feat_in[i].astype(jnp.float32), rest_in[i]]
        row = i if top else i - near
        if 0 <= row < near:
            parts.append(rest_in[HALO + row])
        return jnp.concatenate(parts, axis=0)

    def put_rows(edge_rows, corner, top):
        base = HALO + height if top else 0
        half = HALO - 8
        for i in range(HALO):
            at = (i if top else i - half) * STRIP
            if 0 <= at < 128:
                shared = corner[pl.ds(3 * slim, PAD)]
                left = jnp.concatenate([corner[pl.ds(0, slim)], shared], axis=0)
                right = jnp.concatenate([corner[pl.ds(slim, slim)], shared], axis=0)
                left_at = right_at = at
            else:
                left = right = corner[pl.ds(2 * slim, slim)]
                left_at = (i - 8) * STRIP if top else 64 + i * STRIP
                right_at = (left_at + 64) % 128
            own = edge_rows(i, top)
            size = min(own.shape[0], left.shape[0])
            put(base + i, own[0:size], left[0:size], left_at, right[0:size], right_at)

    even, has_left, has_right, first_row, all_rows = position(height)
    for edge_rows, corner, below in (
        (functools.partial(edge_row, inner_feat, inner_rest), inner_corner, even),
        (functools.partial(edge_row, outer_feat, outer_rest), outer_corner, jnp.logical_not(even)),
    ):
        pl.when(below)(functools.partial(put_rows, edge_rows, corner, True))
        pl.when(jnp.logical_not(below))(functools.partial(put_rows, edge_rows, corner, False))

    wide_lane = lane(256)
    inside_lane = (
        (wide_lane < 128)
        | ((wide_lane < 192) & has_right)
        | ((wide_lane >= 192) & has_left)
    )

    def inside(y):
        row = first_row + y
        return inside_lane & (row >= 0) & (row < all_rows)

    send(short, feat_out, HALO)
    slots = rows // GROUPS
    tall = slots + 2 * REACH
    stacked = jnp.concatenate(
        [
            jnp.concatenate([short[slots * j + k] for j in range(GROUPS)], axis=1)
            for k in range(tall)
        ],
        axis=0,
    )
    moved = jnp.dot(stacked, side_turner[...], preferred_element_type=jnp.float32)
    side_feat[...] = moved[:, 0:128].reshape(tall, channels, 128)
    for group in range(REACH):
        start = 128 * group + 128
        side_turned[group] = moved[:, start : start + 128].reshape(tall, channels, 128)
    sizes(side_feat, side_turned, side_size, side_size_turned)
    affinities(side_feat, side_turned, side_size, side_size_turned, side_kern)
    for j in range(GROUPS):
        for k in range(slots):
            y, value = slots * j + k, side_kern[k]
            kern[y, :, 128:256] = pltpu.roll(value, (116 - 32 * j) % 128, axis=1)
            last = pltpu.roll(value, (101 - 32 * j) % 128, axis=1)
            kern[y, :, 0:128] = jnp.where(side < 128 - REACH, main[y], last)
    send(kern, kern_out, HALO - REACH)

    def put_field(field, y, value):
        field[y] = value
        for group in range(REACH):
            turned[group, y] = shifted(value, group + 1)

    def start(y):
        put_field(prob0, y, jnp.where(inside(y), softmax(unary[y]), 0.0))

    each_row(0, rows, rows // 2, start)
    send(prob0, prob0_out, HALO - REACH)

    def run_pass(field, out, low, high):
        def body(y):
            out[y] = pass_row(y, kern, field, turned)

        each_row(low, high, 2, body)

    run_pass(prob0, message0, REACH, rows - REACH)

    def mix(y):
        value = softmax(unary[y] - apply(compat[...], message0[y]))
        put_field(prob1, y, jnp.where(inside(y), value, 0.0))

    each_row(REACH, rows - REACH, rows, mix)
    send(prob1, prob1_out, HALO - REACH)
    run_pass(prob1, message1, 2 * REACH, rows - 2 * REACH)

    def back1(y):
        prob = softmax(unary[y] - apply(compat[...], message1[y]))
        cot = grad[y]
        change = prob * (cot - jnp.sum(cot * prob, axis=0, keepdims=True))
        logit1[y] = change
        put_field(grad1, y, jnp.where(inside(y), -apply(compat_t[...], change), 0.0))

    each_row(2 * REACH, rows - 2 * REACH, rows, back1)
    def share_of(change, message):
        block = range(HALO, HALO + height)
        left = jnp.concatenate([change[y, :, 0:128] for y in block], axis=1)
        right = jnp.concatenate([message[y, :, 0:128] for y in block], axis=1)
        return outer(left, right)

    total = -share_of(logit1, message1)
    run_pass(grad1, message1, 3 * REACH, rows - 3 * REACH)

    def back0(y):
        prob = prob1[y]
        cot = message1[y]
        change = prob * (cot - jnp.sum(cot * prob, axis=0, keepdims=True))
        logit0[y] = change
        grad0[y] = jnp.where(inside(y), -apply(compat_t[...], change), 0.0)

    each_row(3 * REACH, rows - 3 * REACH, rows, back0)
    total = total - share_of(logit0, message0)

    total = jnp.concatenate([total, jnp.zeros((PAD, 128 - PAD), jnp.float32)], axis=1)
    packed = (
        total[0:8]
        + pltpu.roll(total[8:16], 32, axis=1)
        + pltpu.roll(total[16:24], 64, axis=1)
    )
    for slot in range(share.shape[0]):
        share[slot] = packed

    middle = (side >= 32) & (side < 96)

    def add_logit(y):
        at = y + HALO
        value = logit0[at, :, 0:128] + logit1[at, :, 0:128]
        for field, shift in ((grad1, 32), (grad0, 96)):
            field[at, :, 128:256] = jnp.where(
                middle, pltpu.roll(value, shift, axis=1), field[at, :, 128:256]
            )

    each_row(0, height, height, add_logit)
    send(grad1, grad1_out, HALO - REACH)
    send(grad0, grad0_out, HALO - REACH)


def iterate(compat, centre, received, main, devices):
    height, depth, _ = centre.shape
    channels = depth - 2 * PAD
    rows = height + 2 * HALO
    tall = rows + 2 * REACH
    near = height + 2 * REACH
    slots = rows // GROUPS

    def shape(*dims):
        return jax.ShapeDtypeStruct(dims, jnp.float32)

    def room(*dims):
        return pltpu.VMEM(dims, jnp.float32)

    return pl.pallas_call(
        field_kernel,
        out_shape=(
            jax.ShapeDtypeStruct((near, channels, 256), jnp.bfloat16),
            shape(near, PAD, 256),
            shape(near, PAD, 256),
            shape(near, PAD, 256),
            shape(near, PAD, 256),
            shape(near, PAD, 256),
            shape(devices, 8, 128),
        ),
        in_specs=[VMEM] * (3 + len(received)),
        out_specs=(VMEM,) * 7,
        scratch_shapes=[
            pltpu.VMEM((tall, channels, 256), jnp.bfloat16),
            room(slots + 2 * REACH, channels, 128),
            room(REACH, slots + 2 * REACH, channels, 128),
            room(slots + 2 * REACH, 8, 128),
            room(REACH, slots + 2 * REACH, 8, 128),
            room(slots, PAD, 128),
            *[room(rows, PAD, 256)] * 7,
            room(REACH, rows, PAD, 256),
            *[room(rows, PAD, 256)] * 4,
            pltpu.VMEM((GROUPS * 256, (REACH + 1) * 128), jnp.bfloat16),
            room(128, 128),
            pltpu.VMEM((DEEP, 6 * PAD), jnp.bfloat16),
            pltpu.VMEM((DEEP, 6 * PAD), jnp.bfloat16),
        ],
        compiler_params=params(28),
        name="iterate",
    )(compat, centre, *received, main)


def finish_kernel(
    feat, kern, prob0, prob1, grad1, grad0, unary_out, feat_out, feat_turned, all_turned, kern_back, weights,
    turner, unary_rows, out_sem,
):
    near = feat.shape[0]
    height = near - 2 * REACH
    channels = feat.shape[1]
    classes = unary_out.shape[0] // height
    steps = range(-REACH, REACH + 1)

    turner[...] = turns(steps, 128)
    column = lane()

    def moved(main, edge, b):
        if b == 0:
            return main
        mixed = jnp.where((column < b) if b > 0 else (column >= 128 + b), edge, main)
        return pltpu.roll(mixed, (-b) % 128, axis=1)

    full = jnp.dot(
        feat[...].reshape(near * channels, 256), turner[...], preferred_element_type=jnp.float32
    )
    for place in range(len(steps)):
        feat_turned[place] = full[:, 128 * place : 128 * place + 128].reshape(near, channels, 128)

    def prepare(row):
        for place, field in enumerate((prob0, prob1, grad1, grad0)):
            main, edge = field[row, :, 0:128], field[row, :, 128:256]
            for b in steps:
                all_turned[b + REACH, row, pl.ds(place * PAD, PAD), :] = moved(main, edge, b)
        for group in range(REACH):
            rows = pl.ds(8 * group, 8)
            main, edge = kern[row, rows, 0:128], kern[row, rows, 128:256]
            kern_back[row, rows, :] = jnp.where(
                sublane() == 7, main, moved(main, edge, -(group + 1))
            )

    each_row(0, near, near, prepare)

    def pass_centre(y):
        total = jnp.zeros((PAD, 128), jnp.float32)
        last = pl.ds(3 * PAD, PAD)
        for group in range(REACH):
            step = group + 1
            back = [jnp.zeros((PAD, 128), jnp.float32)] * 2
            for a in range(-REACH, REACH + 1):
                one = pl.ds(8 * group + a + REACH, 1)
                total = total + kern[y, one, 0:128] * all_turned[step + REACH, y + a, last, :]
                for tile in range(2):
                    cols = slice(128 * tile, 128 * tile + 128)
                    back[tile] = back[tile] + kern[y - a, one, cols] * grad0[y - a, :, cols]
            one = pl.ds(8 * group + 7, 1)
            total = total + kern[y, one, 0:128] * grad0[y + step, :, 0:128]
            total = total + kern[y - step, one, 0:128] * grad0[y - step, :, 0:128]
            total = total + moved(back[0], back[1], -step)
        return total

    def unary_row(y):
        cot = pass_centre(y + REACH)
        prob = prob0[y + REACH, :, 0:128]
        row = y + REACH
        partial = jnp.where(
            column < 64,
            pltpu.roll(grad1[row, :, 128:256], 96, axis=1),
            pltpu.roll(grad0[row, :, 128:256], 32, axis=1),
        )
        value = partial + prob * (cot - jnp.sum(cot * prob, axis=0, keepdims=True))
        unary_rows[pl.ds(y, PAD, stride=height), :] = value

    each_row(0, height, 4, unary_row)
    leaving = pltpu.make_async_copy(
        unary_rows.at[pl.ds(0, classes * height)], unary_out, out_sem
    )
    leaving.start()
    sub = sublane()

    def feature_row(y):
        row = y + REACH
        own = all_turned[REACH, row]
        mate = jnp.concatenate(
            [own[3 * PAD :], own[2 * PAD : 3 * PAD], own[PAD : 2 * PAD], own[0:PAD]], axis=0
        )
        total = None
        whole = None
        for sign in (1, -1):
            for group in range(REACH):
                parts = []
                places = []
                for s in range(8):
                    a, b = (s - REACH, group + 1) if s < 7 else (group + 1, 0)
                    a, b = sign * a, sign * b
                    places.append((a, b))
                    parts.append(fold(mate * all_turned[b + REACH, row + a]))
                if sign > 0:
                    weight = kern[row, pl.ds(8 * group, 8), 0:128]
                else:
                    weight = kern_back[row - (group + 1), pl.ds(8 * group, 8), :]
                    for s in range(7):
                        weight = jnp.where(
                            sub == s, kern_back[row - (s - REACH), pl.ds(8 * group, 8), :], weight
                        )
                weight = weight * merge(parts)
                whole = weight if whole is None else whole + weight
                at = 8 * (group + (0 if sign > 0 else REACH))
                weights[y, pl.ds(at, 8), :] = weight
                for s, (a, b) in enumerate(places):
                    term = weights[y, pl.ds(at + s, 1), :] * feat_turned[b + REACH, row + a]
                    total = term if total is None else total + term
        whole = jnp.sum(whole, axis=0, keepdims=True)
        total = total - whole * feat_turned[REACH, row]
        feat_out[pl.ds(y, channels, stride=height), :] = total * (1.0 / math.sqrt(channels))

    each_row(0, height, 1, feature_row)
    leaving.wait()


def finish(feat, kern, prob0, prob1, grad1, grad0, classes):
    near, channels, _ = feat.shape
    height = near - 2 * REACH

    def room(*dims):
        return pltpu.VMEM(dims, jnp.float32)

    return pl.pallas_call(
        finish_kernel,
        out_shape=(
            jax.ShapeDtypeStruct((classes * height, 128), jnp.float32),
            jax.ShapeDtypeStruct((channels * height, 128), jnp.float32),
        ),
        in_specs=[VMEM] * 6,
        out_specs=(ANY, VMEM),
        scratch_shapes=[
            room(2 * REACH + 1, near, channels, 128),
            room(2 * REACH + 1, near, 4 * PAD, 128),
            room(near, PAD, 128),
            room(height, 6 * 8, 128),
            pltpu.VMEM((256, (2 * REACH + 1) * 128), jnp.bfloat16),
            room(PAD * height, 128),
            pltpu.SemaphoreType.DMA,
        ],
        compiler_params=params(24),
        cost_estimate=pl.CostEstimate(flops=200_000_000, bytes_accessed=8_000_000, transcendentals=0),
        name="finish",
    )(feat, kern, prob0, prob1, grad1, grad0)


def on_device(unary, features, compat, grad_output):
    classes, height, width = unary.shape
    n_rows, n_cols = lax.axis_size("rows"), lax.axis_size("cols")

    below = [pair for i in range(0, n_rows, 2) for pair in ((i, i + 1), (i + 1, i))]
    above = [
        pair
        for i in range(1, n_rows, 2)
        for pair in ((i, (i + 1) % n_rows), ((i + 1) % n_rows, i))
    ]
    forward = [(i, i + 1) for i in range(n_cols - 1)]
    backward = [(i + 1, i) for i in range(n_cols - 1)]
    centre, left, right, inner_feat, inner_rest, outer_feat, outer_rest = pack(
        features, unary, grad_output
    )
    inner_feat = lax.ppermute(inner_feat, "rows", below)
    inner_rest = lax.ppermute(inner_rest, "rows", below)
    outer_feat = lax.ppermute(outer_feat, "rows", above)
    outer_rest = lax.ppermute(outer_rest, "rows", above)
    from_left = lax.ppermute(right, "cols", forward)
    from_right = lax.ppermute(left, "cols", backward)
    inner_corner, outer_corner = corners(from_left, from_right, outer_feat)
    outer_corner = lax.ppermute(outer_corner, "rows", above)
    inner_corner = lax.ppermute(inner_corner, "rows", below)
    main = main_affinities(centre, inner_feat, outer_feat)
    received = (
        from_left, from_right, inner_feat, inner_rest, outer_feat, outer_rest, inner_corner,
        outer_corner,
    )

    devices = n_rows * n_cols
    *fields, share = iterate(
        compat, centre, received, main, devices
    )
    shares = lax.all_to_all(share, ("rows", "cols"), 0, 0)
    unary_grad, feature_grad = finish(*fields, classes)
    summed = jnp.sum(shares, axis=0) / math.sqrt(n_rows * height * n_cols * width)
    compat_grad = jnp.concatenate(
        [summed[:, 0:PAD], summed[:, 32 : 32 + PAD], summed[:, 64 : 64 + PAD]], axis=0
    )[:classes, :classes]
    return (
        unary_grad.reshape(unary.shape),
        feature_grad.reshape(features.shape),
        compat_grad,
    )


def solution(mesh):
    placed = (P(None, "rows", "cols"), P(None, "rows", "cols"), P(), P(None, "rows", "cols"))
    return jax.shard_map(
        on_device,
        mesh=mesh,
        in_specs=placed,
        out_specs=(P(None, "rows", "cols"), P(None, "rows", "cols"), P()),
        check_vma=False,
    )
```
